32 devices in a mesh: dp: 16 (over z, y, x), mp: 2 (over core).
Axes of the slice: x: 2, y: 2, z: 4, core: 2. Of those that a mesh axis runs over, the one named last changes fastest.
Arguments:
- tokens: bfloat16 [18464, 768], P('dp'), may hold values from -6 to 6
- row_ids: int32 [18464], P('dp'), may hold values from 0 to 31, as said below
- select: int32 [18464], P('dp'), may hold values 0 or 1
- priority: int32 [18464], P('dp'), may hold values from 0 to 1153, as said below
- first_gain: float32 [768], replicated, may hold values from 0.5 to 1.5
- first_shift: float32 [768], replicated, may hold values from -1 to 1
- router: float32 [768], replicated, may hold values from -0.21875 to 0.21875
- w_attend: bfloat16 [768, 3, 768], P(None, None, 'mp'), may hold values from -0.21875 to 0.21875
- w_output: bfloat16 [768, 768], P('mp'), may hold values from -3 to 3
- second_gain: float32 [768], replicated, may hold values from 0.5 to 1.5
- second_shift: float32 [768], replicated, may hold values from -1 to 1
- w_expand: bfloat16 [768, 3072], P(None, 'mp'), may hold values from -0.21875 to 0.21875
- w_reduce: bfloat16 [3072, 768], P('mp'), may hold values from -0.109375 to 0.109375
- cotangent: bfloat16 [18464, 768], P('dp'), may hold values from -6 to 6
Outputs:
- layer_out: bfloat16 [18464, 768], P('dp')
- tokens_grad: float32 [18464, 768], P('dp')
- first_gain_grad: float32 [768], P('dp')
- first_shift_grad: float32 [768], P('dp')
- router_grad: float32 [768], P('dp')
- attend_grad: float32 [768, 3, 768], P('dp', None, 'mp')
- output_grad: float32 [768, 768], P('mp', 'dp')
- second_gain_grad: float32 [768], P('dp')
- second_shift_grad: float32 [768], P('dp')
- expand_grad: float32 [768, 3072], P('dp', 'mp')
- reduce_grad: float32 [3072, 768], P('mp', 'dp')
The draws below stay inside these ranges and needn't reach their ends.
Inputs may be any that keep to these rules, and one draw needn't show every extreme that they name: `row_ids`: each of the 32 rows has 577 tokens, and every index of dp holds 36 or one more of every row's tokens. `priority`: on each index of dp the 1154 values are a permutation.
All inputs are finite; a program needn't handle non-finite values. No bound on the sum of `select` on one device may be relied on, other than what follows from the above.
Results may differ from the reference program's by a relative error of at most 0.015.
Values may be sent and summed in bfloat16 or wider, within the bound.
A program may use at most 192 MiB of HBM per device.

```python
import jax
import jax.numpy as jnp
from jax import lax

D = 768
H = 12
HD = 64
FF = 3072
ROW_LEN = 577
HH = 768
CAP = 22
SLOTS_ROW = 352
ROWS = 32
TOK_DEV = 1154
TOKENS = 18464
N_DP = 16


def draw_row_ids(key, part):
    key = jax.random.fold_in(key, 11)
    blocks = TOKENS // TOK_DEV
    relabel = jax.random.permutation(jax.random.fold_in(key, 1), ROWS).astype(jnp.int32)
    labels = jnp.arange(TOKENS, dtype=jnp.int32) // ROW_LEN
    spread = relabel[labels].reshape(TOK_DEV, blocks).T
    block_keys = jax.random.split(jax.random.fold_in(key, 2), blocks)
    shuffled = jax.vmap(jax.random.permutation)(block_keys, spread)
    return shuffled.reshape(TOKENS).astype(jnp.int32)


def draw_priority(key, part):
    key = jax.random.fold_in(key, 23)
    blocks = TOKENS // TOK_DEV
    block_keys = jax.random.split(key, blocks)
    ordered = jnp.broadcast_to(jnp.arange(TOK_DEV, dtype=jnp.int32), (blocks, TOK_DEV))
    return jax.vmap(jax.random.permutation)(block_keys, ordered).reshape(TOKENS).astype(jnp.int32)


def plant(entries, rng, smallest, largest):
    shape = entries.shape
    place = [jax.random.randint(jax.random.fold_in(rng, axis), (), 0, shape[axis]) for axis in range(len(shape))]
    entries = entries.at[tuple(place)].set(smallest)
    longest = shape.index(max(shape))
    place[longest] = (place[longest] + 1) % shape[longest]
    return entries.at[tuple(place)].set(largest)


def level_of(key, dims, pieces, least, top_value):
    loudness, own = 1.0, jax.random.fold_in(key, 6)
    for dim, blocks in pieces:
        steps = jnp.exp(jax.random.uniform(jax.random.fold_in(own, dim), (blocks,), jnp.float32, least / len(pieces), top_value / len(pieces)))
        loudness = loudness * jnp.repeat(steps, dims[dim] // blocks).reshape([-1 if axis == dim else 1 for axis in range(len(dims))])
    return loudness


def normal_values(stream_key, dims, deviation, reach, cuts=(), kind=jnp.bfloat16):
    entries = jax.random.normal(stream_key, dims, jnp.float32) * deviation
    if len(cuts) > 0:
        entries = level_of(stream_key, dims, cuts, -0.22, 0.18) * entries
    return jnp.clip(entries, min=-reach, max=reach).astype(kind)


def setup_inputs(seed: int = 0) -> dict:
    key_of = jax.random.split(jax.random.key(seed), 15)
    tokens = normal_values(key_of[0], (TOKENS, D), 1.0, 6.0, ((0, 16),))
    row_ids = draw_row_ids(jax.random.fold_in(key_of[14], 71), 0)
    select = plant((jax.random.randint(key_of[2], (TOKENS,), 0, 4) < 3).astype(jnp.int32), jax.random.fold_in(key_of[2], 1), 0, 1)
    priority = draw_priority(jax.random.fold_in(key_of[14], 71), 0)
    first_gain = jnp.clip(1.0 + 0.1 * jax.random.normal(key_of[4], (D,), jnp.float32), 0.5, 1.5)
    first_shift = normal_values(key_of[5], (D,), 0.2, 1.0, (), jnp.float32)
    router = normal_values(key_of[6], (D,), D ** -0.5, 0.21875, (), jnp.float32)
    w_attend = normal_values(key_of[7], (D, 3, HH), D ** -0.5, 0.21875, ((2, 2),))
    w_output = normal_values(key_of[8], (HH, D), 4 ** -0.5, 3.0, ((0, 2),))
    second_gain = jnp.clip(1.0 + 0.1 * jax.random.normal(key_of[9], (D,), jnp.float32), 0.5, 1.5)
    second_shift = normal_values(key_of[10], (D,), 0.2, 1.0, (), jnp.float32)
    w_expand = normal_values(key_of[11], (D, FF), D ** -0.5, 0.21875, ((1, 2),))
    w_reduce = normal_values(key_of[12], (FF, D), FF ** -0.5, 0.109375, ((0, 2),))
    cotangent = normal_values(key_of[13], (TOKENS, D), 1.0, 6.0, ((0, 16),))
    return {"tokens": tokens, "row_ids": row_ids, "select": select, "priority": priority, "first_gain": first_gain, "first_shift": first_shift, "router": router, "w_attend": w_attend, "w_output": w_output, "second_gain": second_gain, "second_shift": second_shift, "w_expand": w_expand, "w_reduce": w_reduce, "cotangent": cotangent}


EPSILON = 1e-06
MASKED_SCORE = -1000000000.0
HIGHEST_PRECISION = lax.Precision.HIGHEST

@jax.custom_vjp
def low(v):
    return lax.optimization_barrier(v.astype(jnp.bfloat16)).astype(jnp.float32)

@jax.custom_vjp
def low_back(v):
    return v

def low_keep(v):
    return (low(v), None)

def low_pass(kept, grad):
    return (grad,)

def back_keep(v):
    return (v, None)

def back_low(kept, grad):
    return (low(grad),)
low.defvjp(low_keep, low_pass)
low_back.defvjp(back_keep, back_low)

def layer_norm(value, gain, shift):
    center = value - lax.optimization_barrier(jnp.mean(value, axis=-1, keepdims=True))
    spread = lax.optimization_barrier(jnp.mean(center * center, axis=-1, keepdims=True))
    return center * lax.rsqrt(spread + EPSILON) * gain + shift

def slot_ranks(element):
    rows_here, chosen, ordering = element
    same_row = rows_here[:, None] == rows_here[None, :]
    earlier = ordering[None, :] < ordering[:, None]
    counted = same_row & earlier & (chosen[None, :] == 1)
    return lax.optimization_barrier(jnp.sum(counted.astype(jnp.int32), axis=1)).astype(jnp.int32)

def routing(row_ids, select, priority):
    rows_grid = row_ids.reshape(N_DP, TOK_DEV)
    chosen = select.reshape(N_DP, TOK_DEV)
    ranking = lax.map(slot_ranks, (rows_grid, chosen, priority.reshape(N_DP, TOK_DEV)))
    kept_mask = (chosen == 1) & (ranking < CAP)
    source = jnp.arange(N_DP, dtype=jnp.int32)[:, None]
    target = rows_grid * SLOTS_ROW + source * CAP + ranking
    target = jnp.where(kept_mask, target, ROWS * SLOTS_ROW)
    return target.reshape(TOKENS).astype(jnp.int32)

def attend_row(buffer, valid_keys, w_attend):
    proj_rows = jnp.einsum('sd,dch->csh', buffer, w_attend, precision=HIGHEST_PRECISION)
    proj_rows = low_back(low(proj_rows))
    query_part = proj_rows[0].reshape(SLOTS_ROW, H, HD)
    key_part = proj_rows[1].reshape(SLOTS_ROW, H, HD)
    value_part = proj_rows[2].reshape(SLOTS_ROW, H, HD)
    scores = jnp.einsum('qhd,khd->hqk', query_part, key_part, precision=HIGHEST_PRECISION) * HD ** (-0.5)
    scores = low_back(scores)
    scores = jnp.where(valid_keys[None, None, :], scores, MASKED_SCORE)
    row_peak = lax.optimization_barrier(jnp.max(scores, axis=-1, keepdims=True))
    weights = jnp.exp(scores - row_peak)
    probs = weights / lax.optimization_barrier(jnp.sum(weights, axis=-1, keepdims=True))
    context = jnp.einsum('hqk,khd->qhd', low(probs), value_part, precision=HIGHEST_PRECISION)
    return low_back(low(context.reshape(SLOTS_ROW, HH)))

def forward(tokens_wide, first_gain, first_shift, router, w_attend, w_output, second_gain, second_shift, w_expand, w_reduce, target, valid_slots):
    normed = low(layer_norm(tokens_wide, first_gain, first_shift))
    gate_value = jax.nn.sigmoid(jnp.dot(normed, router, precision=HIGHEST_PRECISION))
    buffer = jnp.zeros((ROWS * SLOTS_ROW + 1, D), jnp.float32).at[target].add(normed)
    buffer = buffer[:ROWS * SLOTS_ROW].reshape(ROWS, SLOTS_ROW, D)
    one_row = jax.checkpoint(lambda element: attend_row(element[0], element[1], w_attend))
    context = lax.map(one_row, (buffer, valid_slots))
    context = jnp.concatenate([context.reshape(ROWS * SLOTS_ROW, HH), jnp.zeros((1, HH), jnp.float32)], axis=0)
    attended = low_back(jnp.dot(context[target], w_output, precision=HIGHEST_PRECISION))
    mixed_rows = tokens_wide + gate_value[:, None] * attended

    def mlp_block(block_rows):
        hidden_two = low(layer_norm(block_rows, second_gain, second_shift))
        pre_act = low_back(jnp.dot(hidden_two, w_expand, precision=HIGHEST_PRECISION))
        activated = low(jax.nn.gelu(pre_act, approximate=False))
        return block_rows + jnp.dot(activated, w_reduce, precision=HIGHEST_PRECISION)
    layer_out = lax.map(jax.checkpoint(mlp_block), mixed_rows.reshape(N_DP, TOK_DEV, D))
    return layer_out.reshape(TOKENS, D)

def reference(tokens, row_ids, select, priority, first_gain, first_shift, router, w_attend, w_output, second_gain, second_shift, w_expand, w_reduce, cotangent):
    target = routing(row_ids, select, priority)
    occupied = jnp.zeros((ROWS * SLOTS_ROW + 1,), jnp.float32).at[target].add(1.0)
    valid_slots = occupied[:ROWS * SLOTS_ROW].reshape(ROWS, SLOTS_ROW) > 0.5
    params = (tokens.astype(jnp.float32), first_gain, first_shift, router, w_attend.astype(jnp.float32), w_output.astype(jnp.float32), second_gain, second_shift, w_expand.astype(jnp.float32), w_reduce.astype(jnp.float32))

    def run_layer(*inputs):
        return forward(*inputs, target, valid_slots)
    layer_out, pullback = jax.vjp(run_layer, *params)
    gradients = pullback(cotangent.astype(jnp.float32))
    return (layer_out.astype(jnp.bfloat16), gradients[0], gradients[1], gradients[2], gradients[3], gradients[4], gradients[5], gradients[6], gradients[7], gradients[8], gradients[9])
```

```python
import jax
import jax.numpy as jnp
from jax import lax
from jax.sharding import PartitionSpec as P

HD = 64
ROW_LEN = 577
EPSILON = 1e-06
MASKED_SCORE = -1000000000.0
EMPTY = 1e30
BF = jnp.bfloat16
F32 = jnp.float32


def mm(a, b, dims):
    return lax.dot_general(a, b, (dims, ((), ())), preferred_element_type=F32)


def norm_stats(value):
    center = value - jnp.mean(value, axis=-1, keepdims=True)
    inv = lax.rsqrt(jnp.mean(center * center, axis=-1, keepdims=True) + EPSILON)
    return center * inv, inv


def norm_pull(e, nhat, inv):
    return (e - jnp.mean(e, axis=-1, keepdims=True) - nhat * jnp.mean(e * nhat, axis=-1, keepdims=True)) * inv


def swap(value):
    return lax.ppermute(value, "mp", [(0, 1), (1, 0)])


def scatter_sum(grad, order):
    count = lax.axis_size("dp")
    me = lax.axis_index("dp")
    bits = count.bit_length() - 1
    width = grad.shape[0] // count
    dims = [2] * bits
    value = grad.reshape(dims + [width, grad.shape[1]])
    out = None
    for step in order:
        axis = bits - 1 - step
        mine = (me >> step) & 1
        give = lax.dynamic_slice_in_dim(value, 1 - mine, 1, axis)
        keep = lax.dynamic_slice_in_dim(value, mine, 1, axis)
        got = lax.ppermute(give, "dp", [(i, i ^ (1 << step)) for i in range(count)])
        out = keep.astype(F32) + got.astype(F32)
        value = out.astype(grad.dtype)
    return out.reshape(width, grad.shape[1])


def shards(
    tokens,
    row_ids,
    select,
    priority,
    first_gain,
    first_shift,
    router,
    w_attend,
    w_output,
    second_gain,
    second_shift,
    w_expand,
    w_reduce,
    cotangent,
):
    dp_count = lax.axis_size("dp")
    mp_count = lax.axis_size("mp")
    core = lax.axis_index("mp")
    bits = dp_count.bit_length() - 1
    order_a = list(range(bits))
    order_b = [1, 0] + list(range(2, bits))
    rows = dp_count * mp_count
    capacity = 5 * ROW_LEN // (8 * dp_count)
    half = capacity // mp_count
    count, width = tokens.shape
    own = count // mp_count
    slots = rows * half
    heads_cols = w_attend.shape[2]
    heads = heads_cols // HD

    w_attend_2 = (w_attend, swap(w_attend))
    w_output_2 = (w_output, swap(w_output))
    w_expand_2 = (w_expand, swap(w_expand))
    w_reduce_2 = (w_reduce, swap(w_reduce))

    chosen = select == 1
    same_row = row_ids[:, None] == row_ids[None, :]
    earlier = priority[None, :] < priority[:, None]
    rank = jnp.sum((same_row & earlier & chosen[None, :]).astype(jnp.int32), axis=1)
    kept = chosen & (rank < capacity)
    taken = jnp.sum(
        ((row_ids[None, :] == jnp.arange(rows)[:, None]) & kept[None, :]).astype(jnp.int32), axis=1
    )
    slot_of = (jnp.arange(mp_count) * half)[:, None, None] + jnp.arange(half)[None, None, :]
    filled = (slot_of < taken[None, :, None]).reshape(mp_count, slots)
    filled_all = jnp.pad(filled, ((0, 0), (0, own - slots))).reshape(count)
    place = jnp.where(
        kept,
        (rank // half) * own + row_ids * half + rank % half,
        count + jnp.cumsum(jnp.where(kept, 0, 1)),
    )
    want = jnp.where(filled_all, jnp.arange(count), count + jnp.cumsum(jnp.where(filled_all, 0, 1)))
    want = want.reshape(mp_count, own)
    want_own = jnp.where(core == 0, want[0], want[1])
    want_other = jnp.where(core == 0, want[1], want[0])
    mask = jnp.where(core == 0, filled[0], filled[1])[:, None]
    pick_own = (want_own[:, None] == place[None, :]).astype(BF)
    pick_other = (want_other[:, None] == place[None, :]).astype(BF)

    x = mm(pick_own, tokens, ((1,), (0,)))
    ct = mm(pick_own, cotangent, ((1,), (0,))).astype(BF)

    nhat_1, inv_1 = norm_stats(x)
    normed = (nhat_1 * first_gain + first_shift).astype(BF)
    normed_wide = normed.astype(F32)
    gate = jax.nn.sigmoid(jnp.sum(normed_wide * router, axis=-1, keepdims=True))

    def exchange(value):
        return lax.all_to_all(
            value.reshape(rows, half, width), ("dp", "mp"), split_axis=0, concat_axis=0, tiled=True
        ).reshape(slots, width)

    received = exchange(jnp.where(mask, normed[:slots], jnp.asarray(EMPTY, BF)))
    valid = received[:, :1].astype(F32) < 0.5 * EMPTY
    buffer = jnp.where(valid, received, jnp.zeros((), BF))
    valid_keys = valid[:, 0]

    def canonical(pair):
        return jnp.where(
            core == 0, jnp.concatenate(pair, axis=1), jnp.concatenate(pair[::-1], axis=1)
        )

    def uncanonical(value):
        first, second = jnp.split(value, 2, axis=1)
        return jnp.where(core == 0, first, second), jnp.where(core == 0, second, first)

    saved = []
    contexts = []
    for w in w_attend_2:
        proj = mm(buffer, w.reshape(width, 3 * heads_cols), ((1,), (0,))).astype(BF)
        q, k, v = (proj.reshape(slots, 3, heads, HD)[:, i] for i in range(3))
        scores = jnp.einsum("qhd,khd->hqk", q, k, preferred_element_type=F32) * HD ** (-0.5)
        scores = jnp.where(valid_keys[None, None, :], scores, MASKED_SCORE)
        peak = jnp.max(scores, axis=-1, keepdims=True)
        weights = jnp.exp(scores - peak)
        probs = (weights / jnp.sum(weights, axis=-1, keepdims=True)).astype(BF)
        context = jnp.einsum("hqk,khd->qhd", probs, v, preferred_element_type=F32)
        contexts.append(context.reshape(slots, heads_cols).astype(BF))
        saved.append((q, k, v, probs))
    gathered = exchange(canonical(contexts))
    gathered = uncanonical(jnp.where(mask, gathered, jnp.zeros((), BF)))
    attended_slots = sum(mm(g, w, ((1,), (0,))) for g, w in zip(gathered, w_output_2))
    attended = jnp.pad(attended_slots, ((0, own - slots), (0, 0)))
    mixed = x + gate * attended
    nhat_2, inv_2 = norm_stats(mixed)
    hidden_two = (nhat_2 * second_gain + second_shift).astype(BF)
    mlp_out = 0.0
    hidden_grad = 0.0
    expand_parts = []
    reduce_parts = []
    for w_e, w_r in zip(w_expand_2, w_reduce_2):
        pre = mm(hidden_two, w_e, ((1,), (0,)))
        act_grad = mm(ct, w_r, ((1,), (1,)))
        gelu, pull = jax.vjp(lambda v: jax.nn.gelu(v, approximate=False), pre)
        act = gelu.astype(BF)
        pre_grad = pull(act_grad)[0].astype(BF)
        mlp_out = mlp_out + mm(act, w_r, ((1,), (0,)))
        hidden_grad = hidden_grad + mm(pre_grad, w_e, ((1,), (1,)))
        expand_parts.append(mm(hidden_two, pre_grad, ((0,), (0,))).astype(BF))
        reduce_parts.append(mm(ct, act, ((0,), (0,))).astype(BF))
    layer_own = (mixed + mlp_out).astype(BF)

    def both(parts):
        return (parts[0].astype(F32) + swap(parts[1]).astype(F32)).astype(BF)

    expand_sum = scatter_sum(both(expand_parts), order_a)
    reduce_sum = scatter_sum(both(reduce_parts), order_b)

    second_gain_grad = jnp.sum(hidden_grad * nhat_2, axis=0)
    second_shift_grad = jnp.sum(hidden_grad, axis=0)
    mixed_grad = ct.astype(F32) + norm_pull(hidden_grad * second_gain, nhat_2, inv_2)
    attended_grad = (gate * mixed_grad)[:slots].astype(BF)
    logit_grad = jnp.sum(mixed_grad * attended, axis=-1, keepdims=True) * gate * (1.0 - gate)
    router_grad = jnp.sum(logit_grad * normed_wide, axis=0)
    context_grad = canonical([mm(attended_grad, w, ((1,), (1,))).astype(BF) for w in w_output_2])
    context_grad = exchange(jnp.where(mask, context_grad, jnp.zeros((), BF)))
    output_parts = [mm(attended_grad, g, ((0,), (0,))).astype(BF) for g in gathered]
    buffer_grad = 0.0
    attend_parts = []
    for upstream, w, (q, k, v, probs) in zip(uncanonical(context_grad), w_attend_2, saved):
        upstream = upstream.reshape(slots, heads, HD)
        probs_grad = jnp.einsum("qhd,khd->hqk", upstream, v, preferred_element_type=F32)
        probs_wide = probs.astype(F32)
        delta = jnp.sum(probs_wide * probs_grad, axis=-1, keepdims=True)
        scores_grad = (probs_wide * (probs_grad - delta)).astype(BF)
        v_grad = jnp.einsum("hqk,qhd->khd", probs, upstream, preferred_element_type=F32)
        q_grad = jnp.einsum("hqk,khd->qhd", scores_grad, k, preferred_element_type=F32) * HD ** (-0.5)
        k_grad = jnp.einsum("hqk,qhd->khd", scores_grad, q, preferred_element_type=F32) * HD ** (-0.5)
        proj_grad = jnp.stack([q_grad, k_grad, v_grad], axis=1).astype(BF).reshape(slots, 3 * heads_cols)
        w = w.reshape(width, 3 * heads_cols)
        buffer_grad = buffer_grad + mm(proj_grad, w, ((1,), (1,)))
        attend_parts.append(mm(buffer, proj_grad, ((0,), (0,))).astype(BF))
    late = both([jnp.concatenate(pair, axis=1) for pair in zip(attend_parts, output_parts)])
    split = late.shape[1] // 2
    late_sum = jnp.concatenate(
        [scatter_sum(late[:, :split], order_a), scatter_sum(late[:, split:], order_b)], axis=1
    )
    returned = exchange(buffer_grad.astype(BF))
    returned = jnp.where(mask, returned, jnp.zeros((), BF)).astype(F32)
    normed_grad = jnp.pad(returned, ((0, own - slots), (0, 0))) + logit_grad * router
    first_gain_grad = jnp.sum(normed_grad * nhat_1, axis=0)
    first_shift_grad = jnp.sum(normed_grad, axis=0)
    tokens_own = (mixed_grad + norm_pull(normed_grad * first_gain, nhat_1, inv_1)).astype(BF)

    vectors = jnp.stack(
        [first_gain_grad, first_shift_grad, router_grad, second_gain_grad, second_shift_grad]
    )
    vectors = vectors + swap(vectors)
    vectors = scatter_sum(vectors.T, order_a)

    def unpick(value):
        other = swap(value)
        return mm(pick_own, value, ((0,), (0,))) + mm(pick_other, other, ((0,), (0,)))

    layer_out = unpick(layer_own).astype(BF)
    tokens_grad = unpick(tokens_own)
    attend_cols = 3 * heads_cols
    return (
        layer_out,
        tokens_grad,
        vectors[:, 0],
        vectors[:, 1],
        vectors[:, 2],
        late_sum[:, :attend_cols].reshape(-1, 3, heads_cols),
        late_sum[:, attend_cols:].T,
        vectors[:, 3],
        vectors[:, 4],
        expand_sum,
        reduce_sum.T,
    )


def solution(mesh):
    in_specs = (
        P("dp", None),
        P("dp"),
        P("dp"),
        P("dp"),
        P(),
        P(),
        P(),
        P(None, None, "mp"),
        P("mp", None),
        P(),
        P(),
        P(None, "mp"),
        P("mp", None),
        P("dp", None),
    )
    out_specs = (
        P("dp", None),
        P("dp", None),
        P("dp"),
        P("dp"),
        P("dp"),
        P("dp", None, "mp"),
        P("mp", "dp"),
        P("dp"),
        P("dp"),
        P("dp", "mp"),
        P("mp", "dp"),
    )
    return jax.shard_map(shards, mesh=mesh, in_specs=in_specs, out_specs=out_specs, check_vma=False)
```

```python
import functools

import jax
import jax.numpy as jnp
from jax import lax
from jax.experimental import pallas as pl
from jax.experimental.pallas import tpu as pltpu
from jax.sharding import PartitionSpec as P

HD = 64
ROW_LEN = 577
EPSILON = 1e-06
MASKED_SCORE = -1000000000.0
EMPTY = 1e30
BF = jnp.bfloat16
F32 = jnp.float32
MESH = pl.DeviceIdType.MESH


def mm(a, b, dims):
    return lax.dot_general(a, b, (dims, ((), ())), preferred_element_type=F32)


def norm_stats(value):
    center = value - jnp.mean(value, axis=-1, keepdims=True)
    inv = lax.rsqrt(jnp.mean(center * center, axis=-1, keepdims=True) + EPSILON)
    return center * inv, inv


def norm_pull(e, nhat, inv):
    return (e - jnp.mean(e, axis=-1, keepdims=True) - nhat * jnp.mean(e * nhat, axis=-1, keepdims=True)) * inv


def swap(value):
    return lax.ppermute(value, "mp", [(0, 1), (1, 0)])


def scatter_sum(grad, order):
    count = lax.axis_size("dp")
    me = lax.axis_index("dp")
    bits = count.bit_length() - 1
    width = grad.shape[0] // count
    dims = [2] * bits
    value = grad.reshape(dims + [width, grad.shape[1]])
    out = None
    for step in order:
        axis = bits - 1 - step
        mine = (me >> step) & 1
        give = lax.dynamic_slice_in_dim(value, 1 - mine, 1, axis)
        keep = lax.dynamic_slice_in_dim(value, mine, 1, axis)
        got = lax.ppermute(give, "dp", [(i, i ^ (1 << step)) for i in range(count)])
        out = keep.astype(F32) + got.astype(F32)
        value = out.astype(grad.dtype)
    return out.reshape(width, grad.shape[1])


def block_plan(capacity, width):
    whole = capacity // 16 * 16
    left = capacity - whole
    parts = max(s for s in (1, 2, 3, 6) if left * s <= 16 and width % (128 * s) == 0)
    return whole, left, parts


def rest_map(peers, left, parts):
    at = jnp.arange(peers * 16)[None, :, None]
    row = jnp.arange(peers * left)[None, None, :]
    part = jnp.arange(parts)[:, None, None]
    return ((at // 16 == row // left) & (at % 16 == part * left + row % left)).astype(BF)


def greet(peers):
    me, core = lax.axis_index("dp"), lax.axis_index("mp")
    barrier = pltpu.get_barrier_semaphore()

    def hello(d, carry):
        pl.semaphore_signal(
            barrier, inc=1, device_id=(lax.rem(me + d, peers), core), device_id_type=MESH
        )
        return carry

    lax.fori_loop(1, peers, hello, 0)
    pl.semaphore_wait(barrier, peers - 1)


def pack(value, blocks, maps, whole):
    rest = blocks[-1]
    peers, lanes = rest.shape[0], rest.shape[2]
    if whole:
        blocks[0][...] = value[: peers * whole].reshape(peers, whole, value.shape[1])
    tail = value[peers * whole :]
    total = sum(
        mm(maps[i], tail[:, i * lanes : (i + 1) * lanes], ((1,), (0,)))
        for i in range(maps.shape[0])
    )
    rest[...] = total.astype(BF).reshape(peers, 16, lanes)


def unpack(blocks, maps, whole, out):
    rest = blocks[-1]
    peers, lanes = rest.shape[0], rest.shape[2]
    if whole:
        out[: peers * whole, :] = blocks[0][...].reshape(peers * whole, out.shape[1])
    left = rest[...].reshape(peers * 16, lanes)
    for i in range(maps.shape[0]):
        out[peers * whole :, i * lanes : (i + 1) * lanes] = mm(
            maps[i], left, ((0,), (0,))
        ).astype(BF)


def copies(d, pairs, sends, recvs, back=False):
    me, core = lax.axis_index("dp"), lax.axis_index("mp")
    peers = pairs[0][0].shape[0]
    to, source = lax.rem(me + d, peers), lax.rem(me + peers - d, peers)
    return [
        pltpu.make_async_remote_copy(
            src_ref=here.at[to],
            dst_ref=there.at[source if back else me],
            send_sem=sends.at[i, d],
            recv_sem=recvs.at[i, d],
            device_id=(to, core),
            device_id_type=MESH,
        )
        for i, (here, there) in enumerate(pairs)
    ]


def send_all(pairs, sends, recvs):
    me = lax.axis_index("dp")

    def start(d, carry):
        for copy in copies(d, pairs, sends, recvs):
            copy.start()
        return carry

    lax.fori_loop(1, pairs[0][0].shape[0], start, 0)
    for here, there in pairs:
        there[pl.ds(me, 1)] = here[pl.ds(me, 1)]


def wait_all(pairs, sends, recvs):
    def finish(d, carry):
        for copy in copies(d, pairs, sends, recvs, back=True):
            copy.wait_recv()
        return carry

    def drain(d, carry):
        for copy in copies(d, pairs, sends, recvs):
            copy.wait_send()
        return carry

    lax.fori_loop(1, pairs[0][0].shape[0], finish, 0)
    lax.fori_loop(1, pairs[0][0].shape[0], drain, 0)


def lane_masks():
    low = lax.broadcasted_iota(jnp.int32, (1, 128), 1) < HD
    return low, jnp.logical_not(low)


def attend_kernel(
    whole, normed, maps, w_own, w_other, gathered, buffer, proj, probs,
    w_vmem, context, key_mask, w_sem, send_1, recv_1, send_2, recv_2, *blocks,
):
    core = lax.axis_index("mp")
    loads = [
        pltpu.make_async_copy(w, w_vmem.at[i], w_sem.at[i]) for i, w in enumerate((w_own, w_other))
    ]
    for load in loads:
        load.start()
    given_1, taken_1, given_2, taken_2 = split_blocks(blocks)
    pack(normed[...], given_1, maps, whole)
    greet(given_1[-1].shape[0])
    first = list(zip(given_1, taken_1))
    send_all(first, send_1, recv_1)
    wait_all(first, send_1, recv_1)
    unpack(taken_1, maps, whole, buffer)
    pick = (lax.broadcasted_iota(jnp.int32, (8, 128), 1) == 0).astype(BF)
    key_mask[...] = jnp.where(
        mm(pick, buffer[:, :128], ((1,), (1,))) < 0.5 * EMPTY, 1.0, 0.0
    )
    received = buffer[...].astype(F32)
    buffer[...] = jnp.where(received[:, :1] < 0.5 * EMPTY, received, 0.0).astype(BF)
    cols = w_own.shape[1] // 3
    pairs = cols // 128
    masks = lane_masks()
    zero = jnp.zeros((), BF)
    for i in range(2):
        loads[i].wait()
        proj[i] = mm(buffer[...], w_vmem[i], ((1,), (0,))).astype(BF)
        canonical = core if i == 0 else 1 - core

        def pair_step(p, carry, i=i, canonical=canonical):
            def part(which):
                return proj[i, :, pl.ds(pl.multiple_of(which * cols + p * 128, 128), 128)]

            q, k, v = part(0), part(1), part(2)
            total = 0.0
            for e, lanes in enumerate(masks):
                scores = mm(q, jnp.where(lanes, k, zero), ((1,), (1,))) * HD ** (-0.5)
                scores = jnp.where(key_mask[:1, :] > 0.5, scores, MASKED_SCORE)
                weights = jnp.exp(scores - jnp.max(scores, axis=-1, keepdims=True))
                low = (weights * (1.0 / jnp.sum(weights, axis=-1, keepdims=True))).astype(BF)
                probs[(i * pairs + p) * 2 + e] = low
                total = total + mm(low, jnp.where(lanes, v, zero), ((1,), (0,)))
            context[:, pl.ds(pl.multiple_of(canonical * cols + p * 128, 128), 128)] = total.astype(BF)
            return carry

        lax.fori_loop(0, pairs, pair_step, 0)
    pack(context[...], given_2, maps, whole)
    second = list(zip(given_2, taken_2))
    send_all(second, send_2, recv_2)
    wait_all(second, send_2, recv_2)
    unpack(taken_2, maps, whole, gathered)


def attend_back_kernel(
    whole, context_grad, maps, buffer, w_own, w_other, proj_in, probs_in, returned, parts,
    w_vmem, proj, probs, upstream, proj_grad, total_grad, w_sem, send_1, recv_1, send_2, recv_2, *blocks,
):
    core = lax.axis_index("mp")
    loads = [
        pltpu.make_async_copy(here, there, w_sem.at[i])
        for i, (here, there) in enumerate(
            (
                (proj_in, proj),
                (probs_in, probs),
                (w_own, w_vmem.at[0]),
                (w_other, w_vmem.at[1]),
            )
        )
    ]
    for load in loads:
        load.start()
    given_1, taken_1, given_2, taken_2 = split_blocks(blocks)
    pack(context_grad[...], given_1, maps, whole)
    greet(given_1[-1].shape[0])
    first = list(zip(given_1, taken_1))
    send_all(first, send_1, recv_1)
    wait_all(first, send_1, recv_1)
    unpack(taken_1, maps, whole, upstream)
    for load in loads:
        load.wait()
    cols = w_own.shape[1] // 3
    pairs = cols // 128
    masks = lane_masks()
    zero = jnp.zeros((), BF)
    for i in range(2):
        canonical = core if i == 0 else 1 - core

        def pair_step(p, carry, i=i, canonical=canonical):
            def place(which):
                return pl.ds(pl.multiple_of(which * cols + p * 128, 128), 128)

            q, k, v = (proj[i, :, place(which)] for which in range(3))
            up = upstream[:, place(canonical)]
            q_grad = k_grad = v_grad = 0.0
            for e, lanes in enumerate(masks):
                low = probs[(i * pairs + p) * 2 + e]
                wide = low.astype(F32)
                probs_grad = mm(up, jnp.where(lanes, v, zero), ((1,), (1,)))
                delta = jnp.sum(wide * probs_grad, axis=-1, keepdims=True)
                scores_grad = (wide * (probs_grad - delta)).astype(BF)
                v_grad = v_grad + mm(low, jnp.where(lanes, up, zero), ((0,), (0,)))
                q_grad = q_grad + mm(scores_grad, jnp.where(lanes, k, zero), ((1,), (0,)))
                k_grad = k_grad + mm(scores_grad, jnp.where(lanes, q, zero), ((0,), (0,)))
            proj_grad[i, :, place(0)] = (q_grad * HD ** (-0.5)).astype(BF)
            proj_grad[i, :, place(1)] = (k_grad * HD ** (-0.5)).astype(BF)
            proj_grad[i, :, place(2)] = v_grad.astype(BF)
            return carry

        lax.fori_loop(0, pairs, pair_step, 0)
    total_grad[...] = (
        mm(proj_grad[0], w_vmem[0], ((1,), (1,))) + mm(proj_grad[1], w_vmem[1], ((1,), (1,)))
    ).astype(BF)
    pack(total_grad[...], given_2, maps, whole)
    second = list(zip(given_2, taken_2))
    send_all(second, send_2, recv_2)
    for i in range(2):
        parts[i] = mm(buffer[...], proj_grad[i], ((0,), (0,))).astype(BF)
    wait_all(second, send_2, recv_2)
    unpack(taken_2, maps, whole, returned)


def split_blocks(blocks):
    step = len(blocks) // 4
    return [blocks[i * step : (i + 1) * step] for i in range(4)]


def block_scratch(peers, whole, left, parts, width):
    shapes = [(peers, whole, width)] if whole else []
    shapes.append((peers, 16, width // parts))
    return [pltpu.VMEM(shape, BF) for _ in range(4) for shape in shapes], len(shapes)


def exchange_call(kernel, name, collective_id, capacity, args, spaces, outs, scratch):
    width = args[0].shape[1]
    peers = lax.axis_size("dp")
    whole, left, parts = block_plan(capacity, width)
    blocks, kinds = block_scratch(peers, whole, left, parts, width)
    return pl.pallas_call(
        functools.partial(kernel, whole),
        out_shape=[jax.ShapeDtypeStruct(shape, BF) for shape in outs],
        in_specs=[pl.BlockSpec(memory_space=space) for space in spaces],
        out_specs=[pl.BlockSpec(memory_space=pltpu.VMEM)] * len(outs),
        scratch_shapes=[
            *scratch,
            *[pltpu.SemaphoreType.DMA((kinds, peers))] * 4,
            *blocks,
        ],
        compiler_params=pltpu.CompilerParams(
            collective_id=collective_id, has_side_effects=True, vmem_limit_bytes=48 * 2**20
        ),
        name=name,
    )(*args)


def attend(normed, maps, w_own, w_other, capacity):
    slots, width = normed.shape
    columns = w_own.shape[1]
    heads = 2 * columns // 3 // HD
    return exchange_call(
        attend_kernel, "attend", 0, capacity,
        (normed, maps, w_own, w_other),
        (pltpu.VMEM, pltpu.VMEM, pl.ANY, pl.ANY),
        ((slots, width), (slots, width), (2, slots, columns), (heads, slots, slots)),
        [
            pltpu.VMEM((2, width, columns), BF),
            pltpu.VMEM((slots, width), BF),
            pltpu.VMEM((8, slots), F32),
            pltpu.SemaphoreType.DMA((2,)),
        ],
    )


def attend_back(context_grad, maps, buffer, w_own, w_other, proj, probs, capacity):
    slots, width = buffer.shape
    columns = w_own.shape[1]
    return exchange_call(
        attend_back_kernel, "attend_back", 1, capacity,
        (context_grad, maps, buffer, w_own, w_other, proj, probs),
        (pltpu.VMEM, pltpu.VMEM, pltpu.VMEM, pl.ANY, pl.ANY, pl.ANY, pl.ANY),
        ((slots, width), (2, width, columns)),
        [
            pltpu.VMEM((2, width, columns), BF),
            pltpu.VMEM(proj.shape, BF),
            pltpu.VMEM(probs.shape, BF),
            pltpu.VMEM((slots, width), BF),
            pltpu.VMEM((2, slots, columns), BF),
            pltpu.VMEM((slots, width), BF),
            pltpu.SemaphoreType.DMA((4,)),
        ],
    )


def shards(
    tokens,
    row_ids,
    select,
    priority,
    first_gain,
    first_shift,
    router,
    w_attend,
    w_output,
    second_gain,
    second_shift,
    w_expand,
    w_reduce,
    cotangent,
):
    dp_count = lax.axis_size("dp")
    mp_count = lax.axis_size("mp")
    core = lax.axis_index("mp")
    bits = dp_count.bit_length() - 1
    order_a = list(range(bits))
    order_b = [1, 0] + list(range(2, bits))
    rows = dp_count * mp_count
    capacity = 5 * ROW_LEN // (8 * dp_count)
    count, width = tokens.shape
    own = count // mp_count
    slots = dp_count * capacity
    heads_cols = w_attend.shape[2]
    whole, left, parts = block_plan(capacity, width)
    maps = rest_map(dp_count, left, parts)

    w_attend = w_attend.reshape(width, 3 * heads_cols)
    w_attend_2 = (w_attend, swap(w_attend))
    w_output_2 = (w_output, swap(w_output))
    w_expand_2 = (w_expand, swap(w_expand))
    w_reduce_2 = (w_reduce, swap(w_reduce))

    chosen = select == 1
    same_row = row_ids[:, None] == row_ids[None, :]
    earlier = priority[None, :] < priority[:, None]
    rank = jnp.sum((same_row & earlier & chosen[None, :]).astype(jnp.int32), axis=1)
    kept = chosen & (rank < capacity)
    taken = jnp.sum(
        ((row_ids[None, :] == jnp.arange(rows)[:, None]) & kept[None, :]).astype(jnp.int32), axis=1
    )
    at = jnp.arange(slots)
    row_at = jnp.where(at < dp_count * whole, at // max(whole, 1), (at - dp_count * whole) // left)
    rank_at = jnp.where(
        at < dp_count * whole, at % max(whole, 1), whole + (at - dp_count * whole) % left
    )
    hits = (row_at[:, None] == jnp.arange(dp_count)[None, :]).astype(jnp.int32)
    taken_at = jnp.sum(hits[None] * taken.reshape(dp_count, mp_count).T[:, None, :], axis=2)
    filled = rank_at[None, :] < taken_at
    filled_all = jnp.pad(filled, ((0, 0), (0, own - slots))).reshape(count)
    peer = row_ids // mp_count
    place = jnp.where(
        kept,
        (row_ids % mp_count) * own
        + jnp.where(
            rank < whole, peer * whole + rank, dp_count * whole + peer * left + rank - whole
        ),
        count + jnp.cumsum(jnp.where(kept, 0, 1)),
    )
    want = jnp.where(filled_all, jnp.arange(count), count + jnp.cumsum(jnp.where(filled_all, 0, 1)))
    want = want.reshape(mp_count, own)
    want_own = jnp.where(core == 0, want[0], want[1])
    want_other = jnp.where(core == 0, want[1], want[0])
    mask = jnp.where(core == 0, filled[0], filled[1])[:, None]
    pick_own = (want_own[:, None] == place[None, :]).astype(BF)
    pick_other = (want_other[:, None] == place[None, :]).astype(BF)

    x = mm(pick_own, tokens, ((1,), (0,)))
    ct = mm(pick_own, cotangent, ((1,), (0,))).astype(BF)

    nhat_1, inv_1 = norm_stats(x)
    normed = (nhat_1 * first_gain + first_shift).astype(BF)
    normed_wide = normed.astype(F32)
    gate = jax.nn.sigmoid(jnp.sum(normed_wide * router, axis=-1, keepdims=True))

    def canonical(pair):
        return jnp.where(
            core == 0, jnp.concatenate(pair, axis=1), jnp.concatenate(pair[::-1], axis=1)
        )

    def uncanonical(value):
        first, second = jnp.split(value, 2, axis=1)
        return jnp.where(core == 0, first, second), jnp.where(core == 0, second, first)

    gathered, buffer, proj, probs = attend(
        jnp.where(mask, normed[:slots], jnp.asarray(EMPTY, BF)), maps, *w_attend_2, capacity
    )
    gathered = uncanonical(jnp.where(mask, gathered, jnp.zeros((), BF)))
    attended_slots = sum(mm(g, w, ((1,), (0,))) for g, w in zip(gathered, w_output_2))
    attended = jnp.pad(attended_slots, ((0, own - slots), (0, 0)))
    mixed = x + gate * attended
    nhat_2, inv_2 = norm_stats(mixed)
    hidden_two = (nhat_2 * second_gain + second_shift).astype(BF)
    mlp_out = 0.0
    hidden_grad = 0.0
    expand_parts = []
    reduce_parts = []
    for w_e, w_r in zip(w_expand_2, w_reduce_2):
        pre = mm(hidden_two, w_e, ((1,), (0,)))
        act_grad = mm(ct, w_r, ((1,), (1,)))
        gelu, pull = jax.vjp(lambda v: jax.nn.gelu(v, approximate=False), pre)
        act = gelu.astype(BF)
        pre_grad = pull(act_grad)[0].astype(BF)
        mlp_out = mlp_out + mm(act, w_r, ((1,), (0,)))
        hidden_grad = hidden_grad + mm(pre_grad, w_e, ((1,), (1,)))
        expand_parts.append(mm(hidden_two, pre_grad, ((0,), (0,))).astype(BF))
        reduce_parts.append(mm(ct, act, ((0,), (0,))).astype(BF))
    layer_own = (mixed + mlp_out).astype(BF)

    def both(parts):
        return (parts[0].astype(F32) + swap(parts[1]).astype(F32)).astype(BF)

    expand_sum = scatter_sum(both(expand_parts), order_a)
    reduce_sum = scatter_sum(both(reduce_parts), order_b)

    second_gain_grad = jnp.sum(hidden_grad * nhat_2, axis=0)
    second_shift_grad = jnp.sum(hidden_grad, axis=0)
    mixed_grad = ct.astype(F32) + norm_pull(hidden_grad * second_gain, nhat_2, inv_2)
    attended_grad = (gate * mixed_grad)[:slots].astype(BF)
    logit_grad = jnp.sum(mixed_grad * attended, axis=-1, keepdims=True) * gate * (1.0 - gate)
    router_grad = jnp.sum(logit_grad * normed_wide, axis=0)
    context_grad = canonical([mm(attended_grad, w, ((1,), (1,))).astype(BF) for w in w_output_2])
    context_grad = jnp.where(mask, context_grad, jnp.zeros((), BF))
    output_parts = [mm(attended_grad, g, ((0,), (0,))).astype(BF) for g in gathered]
    returned, attend_parts = attend_back(
        context_grad, maps, buffer, *w_attend_2, proj, probs, capacity
    )
    late = both([jnp.concatenate(pair, axis=1) for pair in zip(attend_parts, output_parts)])
    split = late.shape[1] // 2
    late_sum = jnp.concatenate(
        [scatter_sum(late[:, :split], order_a), scatter_sum(late[:, split:], order_b)], axis=1
    )
    returned = jnp.where(mask, returned, jnp.zeros((), BF)).astype(F32)
    normed_grad = jnp.pad(returned, ((0, own - slots), (0, 0))) + logit_grad * router
    first_gain_grad = jnp.sum(normed_grad * nhat_1, axis=0)
    first_shift_grad = jnp.sum(normed_grad, axis=0)
    tokens_own = (mixed_grad + norm_pull(normed_grad * first_gain, nhat_1, inv_1)).astype(BF)

    vectors = jnp.stack(
        [first_gain_grad, first_shift_grad, router_grad, second_gain_grad, second_shift_grad]
    )
    vectors = vectors + swap(vectors)
    vectors = scatter_sum(vectors.T, order_a)

    def unpick(value):
        other = swap(value)
        return mm(pick_own, value, ((0,), (0,))) + mm(pick_other, other, ((0,), (0,)))

    layer_out = unpick(layer_own).astype(BF)
    tokens_grad = unpick(tokens_own)
    attend_cols = 3 * heads_cols
    return (
        layer_out,
        tokens_grad,
        vectors[:, 0],
        vectors[:, 1],
        vectors[:, 2],
        late_sum[:, :attend_cols].reshape(-1, 3, heads_cols),
        late_sum[:, attend_cols:].T,
        vectors[:, 3],
        vectors[:, 4],
        expand_sum,
        reduce_sum.T,
    )


def solution(mesh):
    in_specs = (
        P("dp", None),
        P("dp"),
        P("dp"),
        P("dp"),
        P(),
        P(),
        P(),
        P(None, None, "mp"),
        P("mp", None),
        P(),
        P(),
        P(None, "mp"),
        P("mp", None),
        P("dp", None),
    )
    out_specs = (
        P("dp", None),
        P("dp", None),
        P("dp"),
        P("dp"),
        P("dp"),
        P("dp", None, "mp"),
        P("mp", "dp"),
        P("dp"),
        P("dp"),
        P("dp", "mp"),
        P("mp", "dp"),
    )
    return jax.shard_map(shards, mesh=mesh, in_specs=in_specs, out_specs=out_specs, check_vma=False)
```

```python
import functools

import jax
import jax.numpy as jnp
from jax import lax
from jax.experimental import pallas as pl
from jax.experimental.pallas import tpu as pltpu
from jax.sharding import PartitionSpec as P

HD = 64
ROW_LEN = 577
EPSILON = 1e-06
MASKED_SCORE = -1000000000.0
EMPTY = 1e30
BF = jnp.bfloat16
F32 = jnp.float32
MESH = pl.DeviceIdType.MESH


def mm(a, b, dims):
    return lax.dot_general(a, b, (dims, ((), ())), preferred_element_type=F32)


def norm_stats(value):
    center = value - jnp.mean(value, axis=-1, keepdims=True)
    inv = lax.rsqrt(jnp.mean(center * center, axis=-1, keepdims=True) + EPSILON)
    return center * inv, inv


def norm_pull(e, nhat, inv):
    return (e - jnp.mean(e, axis=-1, keepdims=True) - nhat * jnp.mean(e * nhat, axis=-1, keepdims=True)) * inv


def swap(value):
    return lax.ppermute(value, "mp", [(0, 1), (1, 0)])


def scatter_sum(grad, order):
    count = lax.axis_size("dp")
    me = lax.axis_index("dp")
    bits = count.bit_length() - 1
    width = grad.shape[0] // count
    dims = [2] * bits
    value = grad.reshape(dims + [width, grad.shape[1]])
    out = None
    for step in order:
        axis = bits - 1 - step
        mine = (me >> step) & 1
        give = lax.dynamic_slice_in_dim(value, 1 - mine, 1, axis)
        keep = lax.dynamic_slice_in_dim(value, mine, 1, axis)
        got = lax.ppermute(give, "dp", [(i, i ^ (1 << step)) for i in range(count)])
        out = keep.astype(F32) + got.astype(F32)
        value = out.astype(grad.dtype)
    return out.reshape(width, grad.shape[1])


def block_plan(capacity, width):
    whole = capacity // 16 * 16
    left = capacity - whole
    parts = max(s for s in (1, 2, 3, 6) if left * s <= 16 and width % (128 * s) == 0)
    return whole, left, parts


def rest_map(peers, left, parts):
    at = jnp.arange(peers * 16)[None, :, None]
    row = jnp.arange(peers * left)[None, None, :]
    part = jnp.arange(parts)[:, None, None]
    return ((at // 16 == row // left) & (at % 16 == part * left + row % left)).astype(BF)


def greet(peers, with_pair=False):
    me, core = lax.axis_index("dp"), lax.axis_index("mp")
    barrier = pltpu.get_barrier_semaphore()

    def hello(d, carry):
        pl.semaphore_signal(
            barrier, inc=1, device_id=(lax.rem(me + d, peers), core), device_id_type=MESH
        )
        return carry

    lax.fori_loop(1, peers, hello, 0)
    if with_pair:
        pl.semaphore_signal(barrier, inc=1, device_id=(me, 1 - core), device_id_type=MESH)
    pl.semaphore_wait(barrier, peers if with_pair else peers - 1)


def pack(value, blocks, maps, whole):
    rest = blocks[-1]
    peers, lanes = rest.shape[0], rest.shape[2]
    if whole:
        blocks[0][...] = value[: peers * whole].reshape(peers, whole, value.shape[1])
    tail = value[peers * whole :]
    total = sum(
        mm(maps[i], tail[:, i * lanes : (i + 1) * lanes], ((1,), (0,)))
        for i in range(maps.shape[0])
    )
    rest[...] = total.astype(BF).reshape(peers, 16, lanes)


def unpack(blocks, maps, whole, out):
    rest = blocks[-1]
    peers, lanes = rest.shape[0], rest.shape[2]
    if whole:
        out[: peers * whole, :] = blocks[0][...].reshape(peers * whole, out.shape[1])
    left = rest[...].reshape(peers * 16, lanes)
    for i in range(maps.shape[0]):
        out[peers * whole :, i * lanes : (i + 1) * lanes] = mm(
            maps[i], left, ((0,), (0,))
        ).astype(BF)


def copies(d, pairs, sends, recvs, back=False):
    me, core = lax.axis_index("dp"), lax.axis_index("mp")
    peers = pairs[0][0].shape[0]
    to, source = lax.rem(me + d, peers), lax.rem(me + peers - d, peers)
    return [
        pltpu.make_async_remote_copy(
            src_ref=here.at[to],
            dst_ref=there.at[source if back else me],
            send_sem=sends.at[i, d],
            recv_sem=recvs.at[i, d],
            device_id=(to, core),
            device_id_type=MESH,
        )
        for i, (here, there) in enumerate(pairs)
    ]


def send_all(pairs, sends, recvs):
    me = lax.axis_index("dp")

    def start(d, carry):
        for copy in copies(d, pairs, sends, recvs):
            copy.start()
        return carry

    lax.fori_loop(1, pairs[0][0].shape[0], start, 0)
    for here, there in pairs:
        there[pl.ds(me, 1)] = here[pl.ds(me, 1)]


def wait_all(pairs, sends, recvs):
    def finish(d, carry):
        for copy in copies(d, pairs, sends, recvs, back=True):
            copy.wait_recv()
        return carry

    def drain(d, carry):
        for copy in copies(d, pairs, sends, recvs):
            copy.wait_send()
        return carry

    lax.fori_loop(1, pairs[0][0].shape[0], finish, 0)
    lax.fori_loop(1, pairs[0][0].shape[0], drain, 0)


def lane_masks():
    low = lax.broadcasted_iota(jnp.int32, (1, 128), 1) < HD
    return low, jnp.logical_not(low)


def attend_kernel(
    whole, normed, maps, w_own, w_other, gathered, buffer, proj, probs,
    w_vmem, context, key_mask, w_sem, send_1, recv_1, send_2, recv_2, *blocks,
):
    core = lax.axis_index("mp")
    loads = [
        pltpu.make_async_copy(w, w_vmem.at[i], w_sem.at[i]) for i, w in enumerate((w_own, w_other))
    ]
    for load in loads:
        load.start()
    given_1, taken_1, given_2, taken_2 = split_blocks(blocks)
    pack(normed[...], given_1, maps, whole)
    greet(given_1[-1].shape[0])
    first = list(zip(given_1, taken_1))
    send_all(first, send_1, recv_1)
    wait_all(first, send_1, recv_1)
    unpack(taken_1, maps, whole, buffer)
    pick = (lax.broadcasted_iota(jnp.int32, (8, 128), 1) == 0).astype(BF)
    key_mask[...] = jnp.where(
        mm(pick, buffer[:, :128], ((1,), (1,))) < 0.5 * EMPTY, 1.0, 0.0
    )
    received = buffer[...].astype(F32)
    buffer[...] = jnp.where(received[:, :1] < 0.5 * EMPTY, received, 0.0).astype(BF)
    cols = w_own.shape[1] // 3
    pairs = cols // 128
    masks = lane_masks()
    zero = jnp.zeros((), BF)
    for i in range(2):
        loads[i].wait()
        proj[i] = mm(buffer[...], w_vmem[i], ((1,), (0,))).astype(BF)
        canonical = core if i == 0 else 1 - core

        def pair_step(p, carry, i=i, canonical=canonical):
            def part(which):
                return proj[i, :, pl.ds(pl.multiple_of(which * cols + p * 128, 128), 128)]

            q, k, v = part(0), part(1), part(2)
            total = 0.0
            for e, lanes in enumerate(masks):
                scores = mm(q, jnp.where(lanes, k, zero), ((1,), (1,))) * HD ** (-0.5)
                scores = jnp.where(key_mask[:1, :] > 0.5, scores, MASKED_SCORE)
                weights = jnp.exp(scores - jnp.max(scores, axis=-1, keepdims=True))
                low = (weights * (1.0 / jnp.sum(weights, axis=-1, keepdims=True))).astype(BF)
                probs[(i * pairs + p) * 2 + e] = low
                total = total + mm(low, jnp.where(lanes, v, zero), ((1,), (0,)))
            context[:, pl.ds(pl.multiple_of(canonical * cols + p * 128, 128), 128)] = total.astype(BF)
            return carry

        lax.fori_loop(0, pairs, pair_step, 0)
    pack(context[...], given_2, maps, whole)
    second = list(zip(given_2, taken_2))
    send_all(second, send_2, recv_2)
    wait_all(second, send_2, recv_2)
    unpack(taken_2, maps, whole, gathered)


class Halving:
    def __init__(self, source, bufs, sends, recvs, order, out):
        self.source, self.bufs, self.sends, self.recvs = source, bufs, sends, recvs
        self.order, self.out = order, out
        self.stages = len(order)
        self.rows = bufs[0].shape[1]
        self.counts = [buf.shape[0] for buf in bufs]

    def bit(self, stage):
        return lax.rem(lax.div(lax.axis_index("dp"), 1 << self.order[stage]), 2)

    def block(self, k, kept):
        index = 0
        for stage in range(self.stages):
            mine = self.bit(stage)
            if stage == 0:
                value = mine if kept else 1 - mine
            else:
                part = lax.rem(lax.div(k, self.counts[stage]), 2)
                value = (1 - mine) * (1 - part) + mine * part
            index = index + value * (1 << self.order[stage])
        return pl.ds(pl.multiple_of(index * self.rows, 16), self.rows)

    def copy(self, stage, k):
        me, core = lax.axis_index("dp"), lax.axis_index("mp")
        to = me + (1 - 2 * self.bit(stage)) * (1 << self.order[stage])
        at = sum(self.counts[:stage]) + k
        src = self.source.at[self.block(k, False), :] if stage == 0 else self.bufs[stage - 1].at[k]
        return pltpu.make_async_remote_copy(
            src_ref=src,
            dst_ref=self.bufs[stage].at[k],
            send_sem=self.sends.at[at],
            recv_sem=self.recvs.at[at],
            device_id=(to, core),
            device_id_type=MESH,
        )

    def begin(self):
        def start(k, carry):
            self.copy(0, k).start()
            return carry

        lax.fori_loop(0, self.counts[0], start, 0)

    def step(self, stage, k):
        self.copy(stage, k).wait_recv()
        buf = self.bufs[stage]
        if stage == 0:
            own = self.source[self.block(k, True), :]
        else:
            own = self.bufs[stage - 1][pl.ds(self.counts[stage] + k, 1)][0]
        total = own.astype(F32) + buf[pl.ds(k, 1)][0].astype(F32)
        if stage == self.stages - 1:
            self.out[...] = total
            return
        buf[pl.ds(k, 1)] = total.astype(BF)[None]

        @pl.when(k < self.counts[stage + 1])
        def _():
            self.copy(stage + 1, k).start()

    def drain(self):
        for stage, count in enumerate(self.counts):

            def finish(k, carry, stage=stage):
                self.copy(stage, k).wait_send()
                return carry

            lax.fori_loop(0, count, finish, 0)


def advance(chains, stage, first, last):
    def body(k, carry):
        for chain in chains:
            chain.step(stage, k)
        return carry

    lax.fori_loop(first, last, body, 0)


def back_kernel(
    whole, orders, context_grad, maps, buffer, attended_grad, gathered, hidden_t, ct_t,
    act_in, pre_in, w_own, w_other, proj_in, probs_in,
    returned, expand_out, reduce_out, late_out,
    act, pre_grad, w_vmem, proj, probs, upstream, proj_grad, total_grad,
    expand_give, reduce_give, late_give, expand_got, reduce_got, late_got, expand_acc, reduce_acc, late_acc,
    load_sem, pair_send, pair_recv, send_1, recv_1, send_2, recv_2, *rest,
):
    dp, core = lax.axis_index("dp"), lax.axis_index("mp")
    if orders is None:
        expand_acc, reduce_acc, late_acc = expand_out, reduce_out, late_out
    local = (
        (act_in, act), (pre_in, pre_grad), (proj_in, proj), (probs_in, probs),
        (w_own, w_vmem.at[0]), (w_other, w_vmem.at[1]),
    )
    loads = [
        pltpu.make_async_copy(here, there, load_sem.at[i]) for i, (here, there) in enumerate(local)
    ]
    for load in loads:
        load.start()
    kinds = 2 if whole else 1
    given_1, taken_1, given_2, taken_2 = split_blocks(rest[: 4 * kinds])
    rest = rest[4 * kinds :]
    chains = []
    if orders is not None:
        stages = len(orders[0])
        kinds_of = (
            (expand_acc, expand_out, orders[0]),
            (reduce_acc, reduce_out, orders[1]),
            (late_acc.at[0], late_out.at[0], orders[0]),
            (late_acc.at[1], late_out.at[1], orders[1]),
        )
        for i, (source, out, order) in enumerate(kinds_of):
            mine = rest[i * (stages + 2) : (i + 1) * (stages + 2)]
            chains.append(Halving(source, mine[2:], mine[0], mine[1], order, out))

    pack(context_grad[...], given_1, maps, whole)
    greet(given_1[-1].shape[0], with_pair=True)
    first = list(zip(given_1, taken_1))
    send_all(first, send_1, recv_1)

    def pair_copy(at, give, got):
        return pltpu.make_async_remote_copy(
            src_ref=give,
            dst_ref=got,
            send_sem=pair_send.at[at],
            recv_sem=pair_recv.at[at],
            device_id=(dp, 1 - core),
            device_id_type=MESH,
        )

    width, columns = expand_acc.shape
    chunk = 512 if columns % 512 == 0 else columns
    steps = columns // chunk

    def at(j):
        return pl.ds(pl.multiple_of(j * chunk, 128), chunk)

    weights = (
        (hidden_t, pre_grad, expand_give, expand_got, expand_acc),
        (ct_t, act, reduce_give, reduce_got, reduce_acc),
    )
    for i, (left, right, give, got, acc) in enumerate(weights):
        loads[1 - i].wait()

        def other_part(j, carry, i=i, left=left, right=right, give=give, got=got):
            give[:, at(j)] = mm(left[...], right[1, :, at(j)], ((1,), (0,))).astype(BF)
            pair_copy(i * steps + j, give.at[:, at(j)], got.at[:, at(j)]).start()
            return carry

        lax.fori_loop(0, steps, other_part, 0)
    for i, (left, right, give, got, acc) in enumerate(weights):

        def own_part(j, carry, i=i, left=left, right=right, give=give, got=got, acc=acc):
            value = mm(left[...], right[0, :, at(j)], ((1,), (0,)))
            pair_copy(i * steps + j, give.at[:, at(j)], got.at[:, at(j)]).wait_recv()
            acc[:, at(j)] = (value + got[:, at(j)].astype(F32)).astype(BF)
            return carry

        lax.fori_loop(0, steps, own_part, 0)
        if chains:
            chains[i].begin()

    half = late_acc.shape[2]
    cols = w_own.shape[1] // 3
    own_cols = pl.ds(pl.multiple_of(core * cols, 128), cols)
    other_cols = pl.ds(pl.multiple_of((1 - core) * cols, 128), cols)
    tail = half - cols
    late_give[1, :, tail:] = mm(attended_grad[...], gathered[:, other_cols], ((0,), (0,))).astype(BF)
    late_acc[1, :, tail:] = mm(attended_grad[...], gathered[:, own_cols], ((0,), (0,))).astype(BF)

    wait_all(first, send_1, recv_1)
    unpack(taken_1, maps, whole, upstream)
    for load in loads[2:]:
        load.wait()
    pairs = cols // 128
    masks = lane_masks()
    zero = jnp.zeros((), BF)
    for i in range(2):
        canonical = core if i == 0 else 1 - core

        def pair_step(p, carry, i=i, canonical=canonical):
            def place(which):
                return pl.ds(pl.multiple_of(which * cols + p * 128, 128), 128)

            q, k, v = (proj[i, :, place(which)] for which in range(3))
            up = upstream[:, place(canonical)]
            q_grad = k_grad = v_grad = 0.0
            for e, lanes in enumerate(masks):
                low = probs[(i * pairs + p) * 2 + e]
                wide = low.astype(F32)
                probs_grad = mm(up, jnp.where(lanes, v, zero), ((1,), (1,)))
                delta = jnp.sum(wide * probs_grad, axis=-1, keepdims=True)
                scores_grad = (wide * (probs_grad - delta)).astype(BF)
                v_grad = v_grad + mm(low, jnp.where(lanes, up, zero), ((0,), (0,)))
                q_grad = q_grad + mm(scores_grad, jnp.where(lanes, k, zero), ((1,), (0,)))
                k_grad = k_grad + mm(scores_grad, jnp.where(lanes, q, zero), ((0,), (0,)))
            proj_grad[i, :, place(0)] = (q_grad * HD ** (-0.5)).astype(BF)
            proj_grad[i, :, place(1)] = (k_grad * HD ** (-0.5)).astype(BF)
            proj_grad[i, :, place(2)] = v_grad.astype(BF)
            if chains:
                for chain in chains[:2]:
                    chain.step(0, i * pairs + p)
            return carry

        lax.fori_loop(0, pairs, pair_step, 0)
    total_grad[...] = (
        mm(proj_grad[0], w_vmem[0], ((1,), (1,))) + mm(proj_grad[1], w_vmem[1], ((1,), (1,)))
    ).astype(BF)
    pack(total_grad[...], given_2, maps, whole)
    second = list(zip(given_2, taken_2))
    send_all(second, send_2, recv_2)

    base = 2 * steps
    value = mm(buffer[...], proj_grad[1], ((0,), (0,))).astype(BF)
    late_give[0] = value[:, :half]
    late_give[1, :, :tail] = value[:, half:]
    for j in range(2):
        pair_copy(base + j, late_give.at[j], late_got.at[j]).start()
    value = mm(buffer[...], proj_grad[0], ((0,), (0,)))
    for j in range(2):
        pair_copy(base + j, late_give.at[j], late_got.at[j]).wait_recv()
    late_acc[0] = (value[:, :half] + late_got[0].astype(F32)).astype(BF)
    late_acc[1, :, :tail] = (value[:, half:] + late_got[1, :, :tail].astype(F32)).astype(BF)
    late_acc[1, :, tail:] = (
        late_acc[1, :, tail:].astype(F32) + late_got[1, :, tail:].astype(F32)
    ).astype(BF)
    if chains:
        chains[2].begin()
        chains[3].begin()
        advance(chains[:2], 0, 2 * pairs, chains[0].counts[0])
        advance(chains[:2], 1, 0, chains[0].counts[1])
    wait_all(second, send_2, recv_2)
    unpack(taken_2, maps, whole, returned)
    if chains:
        for stage in range(2, stages):
            advance(chains[:2], stage, 0, chains[0].counts[stage])
        for stage in range(stages):
            advance(chains[2:], stage, 0, chains[0].counts[stage])
        for chain in chains:
            chain.drain()
    for i, (left, right, give, got, acc) in enumerate(weights):

        def finish(j, carry, i=i, give=give, got=got):
            pair_copy(i * steps + j, give.at[:, at(j)], got.at[:, at(j)]).wait_send()
            return carry

        lax.fori_loop(0, steps, finish, 0)
    for j in range(2):
        pair_copy(base + j, late_give.at[j], late_got.at[j]).wait_send()


def split_blocks(blocks):
    step = len(blocks) // 4
    return [blocks[i * step : (i + 1) * step] for i in range(4)]


def block_scratch(peers, whole, left, parts, width):
    shapes = [(peers, whole, width)] if whole else []
    shapes.append((peers, 16, width // parts))
    return [pltpu.VMEM(shape, BF) for _ in range(4) for shape in shapes], len(shapes)


def exchange_call(kernel, name, collective_id, capacity, args, spaces, outs, scratch, after=()):
    width = args[0].shape[1]
    peers = lax.axis_size("dp")
    whole, left, parts = block_plan(capacity, width)
    blocks, kinds = block_scratch(peers, whole, left, parts, width)
    return pl.pallas_call(
        functools.partial(kernel, whole),
        out_shape=[jax.ShapeDtypeStruct(*out) for out in outs],
        in_specs=[pl.BlockSpec(memory_space=space) for space in spaces],
        out_specs=[pl.BlockSpec(memory_space=pltpu.VMEM)] * len(outs),
        scratch_shapes=[
            *scratch,
            *[pltpu.SemaphoreType.DMA((kinds, peers))] * 4,
            *blocks,
            *after,
        ],
        compiler_params=pltpu.CompilerParams(
            collective_id=collective_id, has_side_effects=True, vmem_limit_bytes=58 * 2**20
        ),
        name=name,
    )(*args)


def attend(normed, maps, w_own, w_other, capacity):
    slots, width = normed.shape
    columns = w_own.shape[1]
    heads = 2 * columns // 3 // HD
    return exchange_call(
        attend_kernel, "attend", 0, capacity,
        (normed, maps, w_own, w_other),
        (pltpu.VMEM, pltpu.VMEM, pl.ANY, pl.ANY),
        [
            (shape, BF)
            for shape in ((slots, width), (slots, width), (2, slots, columns), (heads, slots, slots))
        ],
        [
            pltpu.VMEM((2, width, columns), BF),
            pltpu.VMEM((slots, width), BF),
            pltpu.VMEM((8, slots), F32),
            pltpu.SemaphoreType.DMA((2,)),
        ],
    )


def back(
    context_grad, maps, buffer, attended_grad, gathered, hidden_t, ct_t, act, pre_grad,
    w_own, w_other, proj, probs, capacity, orders,
):
    slots, width = buffer.shape
    columns = w_own.shape[1]
    hidden = act.shape[2]
    late = columns + columns // 3
    peers = lax.axis_size("dp")
    vmem, hbm = pltpu.VMEM, pl.ANY
    rows = width // peers
    after = []
    if orders is None:
        outs = [((width, hidden), BF), ((width, hidden), BF), ((2, width, late // 2), BF)]
    else:
        outs = [((rows, hidden), F32), ((rows, hidden), F32), ((2, rows, late // 2), F32)]
        counts = [peers >> (stage + 1) for stage in range(len(orders[0]))]
        for size in (hidden, hidden, late // 2, late // 2):
            after += [pltpu.SemaphoreType.DMA((sum(counts),))] * 2
            after += [vmem((count, rows, size), BF) for count in counts]
    chunks = 2 * (hidden // (512 if hidden % 512 == 0 else hidden)) + 2
    wide, narrow = vmem((width, hidden), BF), vmem((2, width, late // 2), BF)
    return exchange_call(
        lambda whole, *refs: back_kernel(whole, orders, *refs), "back", 1, capacity,
        (context_grad, maps, buffer, attended_grad, gathered, hidden_t, ct_t, act, pre_grad,
         w_own, w_other, proj, probs),
        (vmem,) * 7 + (hbm,) * 6,
        [((slots, width), BF), *outs],
        [
            vmem(act.shape, BF), vmem(pre_grad.shape, BF),
            vmem((2, width, columns), BF), vmem(proj.shape, BF), vmem(probs.shape, BF),
            vmem((slots, width), BF), vmem((2, slots, columns), BF), vmem((slots, width), BF),
            wide, wide, narrow, wide, wide, narrow,
            *((wide, wide, narrow) if orders else [vmem((16, 128), BF)] * 3),
            pltpu.SemaphoreType.DMA((6,)),
            pltpu.SemaphoreType.DMA((chunks,)),
            pltpu.SemaphoreType.DMA((chunks,)),
        ],
        after,
    )


def shards(
    tokens,
    row_ids,
    select,
    priority,
    first_gain,
    first_shift,
    router,
    w_attend,
    w_output,
    second_gain,
    second_shift,
    w_expand,
    w_reduce,
    cotangent,
):
    dp_count = lax.axis_size("dp")
    mp_count = lax.axis_size("mp")
    core = lax.axis_index("mp")
    bits = dp_count.bit_length() - 1
    order_a = list(range(bits))
    order_b = [1, 0] + list(range(2, bits))
    rows = dp_count * mp_count
    capacity = 5 * ROW_LEN // (8 * dp_count)
    count, width = tokens.shape
    own = count // mp_count
    own_pad = -(-own // 128) * 128
    slots = dp_count * capacity
    heads_cols = w_attend.shape[2]
    whole, left, parts = block_plan(capacity, width)
    maps = rest_map(dp_count, left, parts)

    w_attend = w_attend.reshape(width, 3 * heads_cols)
    w_attend_2 = (w_attend, swap(w_attend))
    w_output_2 = (w_output, swap(w_output))
    w_expand_2 = (w_expand, swap(w_expand))
    w_reduce_2 = (w_reduce, swap(w_reduce))

    chosen = select == 1
    same_row = row_ids[:, None] == row_ids[None, :]
    earlier = priority[None, :] < priority[:, None]
    rank = jnp.sum((same_row & earlier & chosen[None, :]).astype(jnp.int32), axis=1)
    kept = chosen & (rank < capacity)
    taken = jnp.sum(
        ((row_ids[None, :] == jnp.arange(rows)[:, None]) & kept[None, :]).astype(jnp.int32), axis=1
    )
    at = jnp.arange(slots)
    row_at = jnp.where(at < dp_count * whole, at // max(whole, 1), (at - dp_count * whole) // left)
    rank_at = jnp.where(
        at < dp_count * whole, at % max(whole, 1), whole + (at - dp_count * whole) % left
    )
    hits = (row_at[:, None] == jnp.arange(dp_count)[None, :]).astype(jnp.int32)
    taken_at = jnp.sum(hits[None] * taken.reshape(dp_count, mp_count).T[:, None, :], axis=2)
    filled = rank_at[None, :] < taken_at
    filled_all = jnp.pad(filled, ((0, 0), (0, own - slots))).reshape(count)
    peer = row_ids // mp_count
    place = jnp.where(
        kept,
        (row_ids % mp_count) * own
        + jnp.where(
            rank < whole, peer * whole + rank, dp_count * whole + peer * left + rank - whole
        ),
        count + jnp.cumsum(jnp.where(kept, 0, 1)),
    )
    want = jnp.where(filled_all, jnp.arange(count), count + jnp.cumsum(jnp.where(filled_all, 0, 1)))
    want = jnp.pad(want.reshape(mp_count, own), ((0, 0), (0, own_pad - own)), constant_values=-1)
    want_own = jnp.where(core == 0, want[0], want[1])
    want_other = jnp.where(core == 0, want[1], want[0])
    mask = jnp.where(core == 0, filled[0], filled[1])[:, None]
    pick_own = (want_own[:, None] == place[None, :]).astype(BF)
    pick_other = (want_other[:, None] == place[None, :]).astype(BF)

    x = mm(pick_own, tokens, ((1,), (0,)))
    ct = mm(pick_own, cotangent, ((1,), (0,))).astype(BF)

    nhat_1, inv_1 = norm_stats(x)
    normed = (nhat_1 * first_gain + first_shift).astype(BF)
    normed_wide = normed.astype(F32)
    gate = jax.nn.sigmoid(jnp.sum(normed_wide * router, axis=-1, keepdims=True))

    def canonical(pair):
        return jnp.where(
            core == 0, jnp.concatenate(pair, axis=1), jnp.concatenate(pair[::-1], axis=1)
        )

    def uncanonical(value):
        first, second = jnp.split(value, 2, axis=1)
        return jnp.where(core == 0, first, second), jnp.where(core == 0, second, first)

    gathered, buffer, proj, probs = attend(
        jnp.where(mask, normed[:slots], jnp.asarray(EMPTY, BF)), maps, *w_attend_2, capacity
    )
    gathered = uncanonical(jnp.where(mask, gathered, jnp.zeros((), BF)))
    attended_slots = sum(mm(g, w, ((1,), (0,))) for g, w in zip(gathered, w_output_2))
    attended = jnp.pad(attended_slots, ((0, own_pad - slots), (0, 0)))
    mixed = x + gate * attended
    nhat_2, inv_2 = norm_stats(mixed)
    hidden_two = (nhat_2 * second_gain + second_shift).astype(BF)
    mlp_out = 0.0
    hidden_grad = 0.0
    acts = []
    pre_grads = []
    for w_e, w_r in zip(w_expand_2, w_reduce_2):
        pre = mm(hidden_two, w_e, ((1,), (0,)))
        act_grad = mm(ct, w_r, ((1,), (1,)))
        gelu, pull = jax.vjp(lambda v: jax.nn.gelu(v, approximate=False), pre)
        act = gelu.astype(BF)
        pre_grad = pull(act_grad)[0].astype(BF)
        mlp_out = mlp_out + mm(act, w_r, ((1,), (0,)))
        hidden_grad = hidden_grad + mm(pre_grad, w_e, ((1,), (1,)))
        acts.append(act)
        pre_grads.append(pre_grad)
    layer_own = (mixed + mlp_out).astype(BF)

    second_gain_grad = jnp.sum(hidden_grad * nhat_2, axis=0)
    second_shift_grad = jnp.sum(hidden_grad, axis=0)
    mixed_grad = ct.astype(F32) + norm_pull(hidden_grad * second_gain, nhat_2, inv_2)
    attended_grad = (gate * mixed_grad)[:slots].astype(BF)
    logit_grad = jnp.sum(mixed_grad * attended, axis=-1, keepdims=True) * gate * (1.0 - gate)
    router_grad = jnp.sum(logit_grad * normed_wide, axis=0)
    context_grad = canonical([mm(attended_grad, w, ((1,), (1,))).astype(BF) for w in w_output_2])
    context_grad = jnp.where(mask, context_grad, jnp.zeros((), BF))
    orders = (order_a, order_b) if width // dp_count % 16 == 0 else None
    returned, expand_sum, reduce_sum, late_sum = back(
        context_grad, maps, buffer, attended_grad, canonical(gathered), hidden_two.T, ct.T,
        jnp.stack(acts), jnp.stack(pre_grads), *w_attend_2, proj, probs, capacity, orders,
    )
    if orders is None:
        expand_sum = scatter_sum(expand_sum, order_a)
        reduce_sum = scatter_sum(reduce_sum, order_b)
        late_sum = [scatter_sum(late_sum[0], order_a), scatter_sum(late_sum[1], order_b)]
    late_sum = jnp.concatenate([late_sum[0], late_sum[1]], axis=1)
    returned = jnp.where(mask, returned, jnp.zeros((), BF)).astype(F32)
    normed_grad = jnp.pad(returned, ((0, own_pad - slots), (0, 0))) + logit_grad * router
    first_gain_grad = jnp.sum(normed_grad * nhat_1, axis=0)
    first_shift_grad = jnp.sum(normed_grad, axis=0)
    tokens_own = (mixed_grad + norm_pull(normed_grad * first_gain, nhat_1, inv_1)).astype(BF)

    vectors = jnp.stack(
        [first_gain_grad, first_shift_grad, router_grad, second_gain_grad, second_shift_grad]
    )
    vectors = vectors + swap(vectors)
    vectors = scatter_sum(vectors.T, order_a)

    def unpick(value):
        other = swap(value)
        return mm(pick_own, value, ((0,), (0,))) + mm(pick_other, other, ((0,), (0,)))

    layer_out = unpick(layer_own).astype(BF)
    tokens_grad = unpick(tokens_own)
    attend_cols = 3 * heads_cols
    return (
        layer_out,
        tokens_grad,
        vectors[:, 0],
        vectors[:, 1],
        vectors[:, 2],
        late_sum[:, :attend_cols].reshape(-1, 3, heads_cols),
        late_sum[:, attend_cols:].T,
        vectors[:, 3],
        vectors[:, 4],
        expand_sum,
        reduce_sum.T,
    )


def solution(mesh):
    in_specs = (
        P("dp", None),
        P("dp"),
        P("dp"),
        P("dp"),
        P(),
        P(),
        P(),
        P(None, None, "mp"),
        P("mp", None),
        P(),
        P(),
        P(None, "mp"),
        P("mp", None),
        P("dp", None),
    )
    out_specs = (
        P("dp", None),
        P("dp", None),
        P("dp"),
        P("dp"),
        P("dp"),
        P("dp", None, "mp"),
        P("mp", "dp"),
        P("dp"),
        P("dp"),
        P("dp", "mp"),
        P("mp", "dp"),
    )
    return jax.shard_map(shards, mesh=mesh, in_specs=in_specs, out_specs=out_specs, check_vma=False)
```

```python
import functools

import jax
import jax.numpy as jnp
from jax import lax
from jax.experimental import pallas as pl
from jax.experimental.pallas import tpu as pltpu
from jax.sharding import PartitionSpec as P

HD = 64
ROW_LEN = 577
EPSILON = 1e-06
MASKED_SCORE = -1000000000.0
EMPTY = 1e30
WINDOW = 3
BF = jnp.bfloat16
F32 = jnp.float32
MESH = pl.DeviceIdType.MESH


def mm(a, b, dims):
    return lax.dot_general(a, b, (dims, ((), ())), preferred_element_type=F32)


def norm_stats(value):
    center = value - jnp.mean(value, axis=-1, keepdims=True)
    inv = lax.rsqrt(jnp.mean(center * center, axis=-1, keepdims=True) + EPSILON)
    return center * inv, inv


def norm_pull(e, nhat, inv):
    return (e - jnp.mean(e, axis=-1, keepdims=True) - nhat * jnp.mean(e * nhat, axis=-1, keepdims=True)) * inv


def swap(value):
    return lax.ppermute(value, "mp", [(0, 1), (1, 0)])


def scatter_sum(grad, order):
    count = lax.axis_size("dp")
    me = lax.axis_index("dp")
    bits = count.bit_length() - 1
    width = grad.shape[0] // count
    dims = [2] * bits
    value = grad.reshape(dims + [width, grad.shape[1]])
    out = None
    for step in order:
        axis = bits - 1 - step
        mine = (me >> step) & 1
        give = lax.dynamic_slice_in_dim(value, 1 - mine, 1, axis)
        keep = lax.dynamic_slice_in_dim(value, mine, 1, axis)
        got = lax.ppermute(give, "dp", [(i, i ^ (1 << step)) for i in range(count)])
        out = keep.astype(F32) + got.astype(F32)
        value = out.astype(grad.dtype)
    return out.reshape(width, grad.shape[1])


def block_plan(capacity, width):
    whole = capacity // 16 * 16
    left = capacity - whole
    parts = max(s for s in (1, 2, 3, 6) if left * s <= 16 and width % (128 * s) == 0)
    return whole, left, parts


def rest_map(peers, left, parts):
    at = jnp.arange(peers * 16)[None, :, None]
    row = jnp.arange(peers * left)[None, None, :]
    part = jnp.arange(parts)[:, None, None]
    return ((at // 16 == row // left) & (at % 16 == part * left + row % left)).astype(BF)


def greet(peers, with_pair=False):
    me, core = lax.axis_index("dp"), lax.axis_index("mp")
    barrier = pltpu.get_barrier_semaphore()

    def hello(d, carry):
        pl.semaphore_signal(
            barrier, inc=1, device_id=(lax.rem(me + d, peers), core), device_id_type=MESH
        )
        return carry

    lax.fori_loop(1, peers, hello, 0)
    if with_pair:
        pl.semaphore_signal(barrier, inc=1, device_id=(me, 1 - core), device_id_type=MESH)
    pl.semaphore_wait(barrier, peers if with_pair else peers - 1)


def pack(value, blocks, maps, whole):
    rest = blocks[-1]
    peers, lanes = rest.shape[0], rest.shape[2]
    if whole:
        blocks[0][...] = value[: peers * whole].reshape(peers, whole, value.shape[1])
    tail = value[peers * whole :]
    total = sum(
        mm(maps[i], tail[:, i * lanes : (i + 1) * lanes], ((1,), (0,)))
        for i in range(maps.shape[0])
    )
    rest[...] = total.astype(BF).reshape(peers, 16, lanes)


def unpack(blocks, maps, whole, out):
    rest = blocks[-1]
    peers, lanes = rest.shape[0], rest.shape[2]
    if whole:
        out[: peers * whole, :] = blocks[0][...].reshape(peers * whole, out.shape[1])
    left = rest[...].reshape(peers * 16, lanes)
    for i in range(maps.shape[0]):
        out[peers * whole :, i * lanes : (i + 1) * lanes] = mm(
            maps[i], left, ((0,), (0,))
        ).astype(BF)


def copies(d, pairs, sends, recvs, back=False):
    me, core = lax.axis_index("dp"), lax.axis_index("mp")
    peers = pairs[0][0].shape[0]
    to, source = lax.rem(me + d, peers), lax.rem(me + peers - d, peers)
    return [
        pltpu.make_async_remote_copy(
            src_ref=here.at[to],
            dst_ref=there.at[source if back else me],
            send_sem=sends.at[i, d],
            recv_sem=recvs.at[i, d],
            device_id=(to, core),
            device_id_type=MESH,
        )
        for i, (here, there) in enumerate(pairs)
    ]


def send_all(pairs, sends, recvs):
    me = lax.axis_index("dp")

    def start(d, carry):
        for copy in copies(d, pairs, sends, recvs):
            copy.start()
        return carry

    lax.fori_loop(1, pairs[0][0].shape[0], start, 0)
    for here, there in pairs:
        there[pl.ds(me, 1)] = here[pl.ds(me, 1)]


def wait_all(pairs, sends, recvs):
    def finish(d, carry):
        for copy in copies(d, pairs, sends, recvs, back=True):
            copy.wait_recv()
        return carry

    def drain(d, carry):
        for copy in copies(d, pairs, sends, recvs):
            copy.wait_send()
        return carry

    lax.fori_loop(1, pairs[0][0].shape[0], finish, 0)
    lax.fori_loop(1, pairs[0][0].shape[0], drain, 0)


def lane_masks():
    low = lax.broadcasted_iota(jnp.int32, (1, 128), 1) < HD
    return low, jnp.logical_not(low)


def attend_kernel(
    whole, normed, maps, w_own, w_other, gathered, buffer, proj, probs,
    w_vmem, context, key_mask, w_sem, send_1, recv_1, send_2, recv_2, *blocks,
):
    core = lax.axis_index("mp")
    loads = [
        pltpu.make_async_copy(w, w_vmem.at[i], w_sem.at[i]) for i, w in enumerate((w_own, w_other))
    ]
    for load in loads:
        load.start()
    given_1, taken_1, given_2, taken_2 = split_blocks(blocks)
    pack(normed[...], given_1, maps, whole)
    greet(given_1[-1].shape[0])
    first = list(zip(given_1, taken_1))
    send_all(first, send_1, recv_1)
    wait_all(first, send_1, recv_1)
    unpack(taken_1, maps, whole, buffer)
    pick = (lax.broadcasted_iota(jnp.int32, (8, 128), 1) == 0).astype(BF)
    key_mask[...] = jnp.where(
        mm(pick, buffer[:, :128], ((1,), (1,))) < 0.5 * EMPTY, 1.0, 0.0
    )
    received = buffer[...].astype(F32)
    buffer[...] = jnp.where(received[:, :1] < 0.5 * EMPTY, received, 0.0).astype(BF)
    cols = w_own.shape[2]
    pairs = cols // 128
    masks = lane_masks()
    zero = jnp.zeros((), BF)
    for i in range(2):
        loads[i].wait()
        for which in range(3):
            proj[i, :, which * cols : (which + 1) * cols] = mm(
                buffer[...], w_vmem[i, which], ((1,), (0,))
            ).astype(BF)
        canonical = core if i == 0 else 1 - core

        def pair_step(p, carry, i=i, canonical=canonical):
            def part(which):
                return proj[i, :, pl.ds(pl.multiple_of(which * cols + p * 128, 128), 128)]

            q, k, v = part(0), part(1), part(2)
            total = 0.0
            for e, lanes in enumerate(masks):
                scores = mm(q, jnp.where(lanes, k, zero), ((1,), (1,))) * HD ** (-0.5)
                scores = jnp.where(key_mask[:1, :] > 0.5, scores, MASKED_SCORE)
                weights = jnp.exp(scores - jnp.max(scores, axis=-1, keepdims=True))
                low = (weights * (1.0 / jnp.sum(weights, axis=-1, keepdims=True))).astype(BF)
                probs[(i * pairs + p) * 2 + e] = low
                total = total + mm(low, jnp.where(lanes, v, zero), ((1,), (0,)))
            context[:, pl.ds(pl.multiple_of(canonical * cols + p * 128, 128), 128)] = total.astype(BF)
            return carry

        lax.fori_loop(0, pairs, pair_step, 0)
    pack(context[...], given_2, maps, whole)
    second = list(zip(given_2, taken_2))
    send_all(second, send_2, recv_2)
    wait_all(second, send_2, recv_2)
    unpack(taken_2, maps, whole, gathered)


class Halving:
    def __init__(self, source, bufs, sends, recvs, order, out):
        self.source, self.bufs, self.sends, self.recvs = source, bufs, sends, recvs
        self.order, self.out = order, out
        self.stages = len(order)
        self.rows = bufs[0].shape[1]
        self.counts = [buf.shape[0] for buf in bufs]
        self.first = [k for stage, k in halving_plan(self.stages) if stage == 0]

    def bit(self, stage):
        return lax.rem(lax.div(lax.axis_index("dp"), 1 << self.order[stage]), 2)

    def block(self, k, kept):
        index = 0
        for stage in range(self.stages):
            mine = self.bit(stage)
            if stage == 0:
                value = mine if kept else 1 - mine
            else:
                part = lax.rem(lax.div(k, self.counts[stage]), 2)
                value = (1 - mine) * (1 - part) + mine * part
            index = index + value * (1 << self.order[stage])
        return pl.ds(pl.multiple_of(index * self.rows, 16), self.rows)

    def copy(self, stage, k):
        me, core = lax.axis_index("dp"), lax.axis_index("mp")
        to = me + (1 - 2 * self.bit(stage)) * (1 << self.order[stage])
        at = sum(self.counts[:stage]) + k
        src = self.source.at[self.block(k, False), :] if stage == 0 else self.bufs[stage - 1].at[k]
        return pltpu.make_async_remote_copy(
            src_ref=src,
            dst_ref=self.bufs[stage].at[k],
            send_sem=self.sends.at[at],
            recv_sem=self.recvs.at[at],
            device_id=(to, core),
            device_id_type=MESH,
        )

    def begin(self):
        for k in self.first[:WINDOW]:
            self.copy(0, k).start()

    def step(self, stage, k):
        self.copy(stage, k).wait_recv()
        buf = self.bufs[stage]
        if stage == 0:
            own = self.source[self.block(k, True), :]
        else:
            own = self.bufs[stage - 1][pl.ds(self.counts[stage] + k, 1)][0]
        total = own.astype(F32) + buf[pl.ds(k, 1)][0].astype(F32)
        if stage == self.stages - 1:
            self.out[...] = total
            return
        buf[pl.ds(k, 1)] = total.astype(BF)[None]
        if k < self.counts[stage + 1]:
            self.copy(stage + 1, k).start()
        if stage == 0:
            ahead = self.first.index(k) + WINDOW
            if ahead < len(self.first):
                self.copy(0, self.first[ahead]).start()

    def drain(self):
        for stage, count in enumerate(self.counts):

            def finish(k, carry, stage=stage):
                self.copy(stage, k).wait_send()
                return carry

            lax.fori_loop(0, count, finish, 0)


def halving_plan(stages):
    counts = [1 << (stages - 1 - stage) for stage in range(stages)]
    times = {}
    for stage, count in enumerate(counts):
        for k in range(count):
            if stage == 0:
                bits = [(k >> i) & 1 for i in range(stages - 1)]
                times[stage, k] = 1 + sum(bit << (stages - 2 - i) for i, bit in enumerate(bits))
            else:
                times[stage, k] = 1.6 + max(times[stage - 1, k], times[stage - 1, count + k])
    return sorted(times, key=lambda key: (times[key], key))


def advance(chains, steps):
    for stage, k in steps:
        for chain in chains:
            chain.step(stage, k)


def back_kernel(
    whole, orders, context_grad, maps, mask, logit_grad, second_sums, gain, shift, router, place, want,
    act_in, pre_in, w_own, w_other, proj_in, probs_in,
    buffer_in, attended_in, gathered_in, hidden_in, ct_in, x_in, mixed_in, layer_in,
    expand_out, reduce_out, late_out, layer_out, tokens_out, sums_out,
    act, pre_grad, w_vmem, proj, probs, upstream, proj_grad, total_grad,
    expand_give, reduce_give, expand_got, reduce_got, expand_acc, reduce_acc, sums, sums_got, layer_stage, tokens_stage, out_sem,
    buffer, attended_grad, gathered, hidden_t, ct_t, x, mixed_grad, layer_own,
    load_sem, pair_send, pair_recv, sums_send, sums_recv, free_sem, send_1, recv_1, send_2, recv_2, *rest,
):
    dp, core = lax.axis_index("dp"), lax.axis_index("mp")
    peers = lax.axis_size("dp")
    width, columns = expand_give.shape
    slots = buffer.shape[0]
    count = x.shape[0]
    late_give, late_got = act.at[pl.ds(0, width), :], pre_grad.at[pl.ds(0, width), :]
    late_acc = expand_give
    if orders is None:
        expand_acc, reduce_acc, late_acc = expand_out, reduce_out, late_out
    own, other = pl.ds(0, count), pl.ds(count, count)
    local = [
        (hidden_in, hidden_t),
        (pre_in.at[1], pre_grad.at[other, :]),
        (pre_in.at[0], pre_grad.at[own, :]),
        (ct_in, ct_t),
        (act_in.at[1], act.at[other, :]),
        (act_in.at[0], act.at[own, :]),
        (attended_in, attended_grad),
        (gathered_in, gathered),
        (proj_in, proj),
        (probs_in, probs),
        (w_own, w_vmem.at[0]),
        (w_other, w_vmem.at[1]),
        (buffer_in, buffer),
        (layer_in, layer_own),
        (x_in, x),
        (mixed_in, mixed_grad),
    ]
    loads = [
        pltpu.make_async_copy(here, there, load_sem.at[i]) for i, (here, there) in enumerate(local)
    ]
    for load in loads:
        load.start()
    kinds = 2 if whole else 1
    given_1, taken_1, given_2, taken_2 = split_blocks(rest[: 4 * kinds])
    rest = rest[4 * kinds :]
    half = columns // 2
    left_half, right_half = pl.ds(0, half), pl.ds(half, half)
    chains = []
    stages = 0
    if orders is not None:
        stages = len(orders[0])
        kinds_of = (
            (expand_acc, expand_out, orders[0]),
            (reduce_acc, reduce_out, orders[1]),
            (late_acc.at[:, left_half], late_out.at[:, left_half], orders[0]),
            (late_acc.at[:, right_half], late_out.at[:, right_half], orders[1]),
        )
        for i, (source, out, order) in enumerate(kinds_of):
            mine = rest[i * (stages + 2) : (i + 1) * (stages + 2)]
            chains.append(Halving(source, mine[2:], mine[0], mine[1], order, out))

    pack(context_grad[...], given_1, maps, whole)
    greet(peers, with_pair=True)
    first = list(zip(given_1, taken_1))
    send_all(first, send_1, recv_1)

    def pair_copy(at, give, got):
        return pltpu.make_async_remote_copy(
            src_ref=give,
            dst_ref=got,
            send_sem=pair_send.at[at],
            recv_sem=pair_recv.at[at],
            device_id=(dp, 1 - core),
            device_id_type=MESH,
        )

    chunk = 512 if columns % 512 == 0 else columns
    steps = columns // chunk

    def at(j):
        return pl.ds(pl.multiple_of(j * chunk, 128), chunk)

    weights = (
        (hidden_t, pre_grad, expand_give, expand_got, expand_acc),
        (ct_t, act, reduce_give, reduce_got, reduce_acc),
    )

    def weight_copy(i, j):
        give, got = weights[i][2:4]
        return pair_copy(i * steps + j, give.at[:, at(j)], got.at[:, at(j)])

    for i, (left, right, give, got, acc) in enumerate(weights):
        loads[3 * i].wait()
        loads[3 * i + 1].wait()

        def other_part(j, carry, i=i, left=left, right=right, give=give):
            give[:, at(j)] = mm(left[...], right[other, at(j)], ((1,), (0,))).astype(BF)
            weight_copy(i, j).start()
            return carry

        def own_part(j, carry, i=i, left=left, right=right, got=got, acc=acc):
            value = mm(left[...], right[own, at(j)], ((1,), (0,)))
            weight_copy(i, j).wait_recv()
            acc[:, at(j)] = (value + got[:, at(j)].astype(F32)).astype(BF)
            return carry

        lax.fori_loop(0, steps, other_part, 0)
        loads[3 * i + 2].wait()
        lax.fori_loop(0, steps, own_part, 0)
        if chains:
            chains[i].begin()
    pl.semaphore_signal(free_sem, inc=1, device_id=(dp, 1 - core), device_id_type=MESH)
    for i in range(2):

        def sent(j, carry, i=i):
            weight_copy(i, j).wait_send()
            return carry

        lax.fori_loop(0, steps, sent, 0)
    cols = w_own.shape[2]
    attend_cols = 3 * cols
    own_cols = pl.ds(pl.multiple_of(core * cols, 128), cols)
    other_cols = pl.ds(pl.multiple_of((1 - core) * cols, 128), cols)
    loads[6].wait()
    loads[7].wait()
    late_give[:, attend_cols:] = mm(
        attended_grad[...], gathered[:, other_cols], ((0,), (0,))
    ).astype(BF)
    late_acc[:, attend_cols:] = mm(attended_grad[...], gathered[:, own_cols], ((0,), (0,))).astype(BF)
    pl.semaphore_wait(free_sem, 1)

    wait_all(first, send_1, recv_1)
    unpack(taken_1, maps, whole, upstream)
    for load in loads[8:]:
        load.wait()
    pairs = cols // 128
    masks = lane_masks()
    zero = jnp.zeros((), BF)
    for i in range(2):
        canonical = core if i == 0 else 1 - core

        def pair_step(p, carry, i=i, canonical=canonical):
            def place_of(which):
                return pl.ds(pl.multiple_of(which * cols + p * 128, 128), 128)

            q, k, v = (proj[i, :, place_of(which)] for which in range(3))
            up = upstream[:, place_of(canonical)]
            q_grad = k_grad = v_grad = 0.0
            for e, lanes in enumerate(masks):
                low = probs[(i * pairs + p) * 2 + e]
                wide = low.astype(F32)
                probs_grad = mm(up, jnp.where(lanes, v, zero), ((1,), (1,)))
                delta = jnp.sum(wide * probs_grad, axis=-1, keepdims=True)
                scores_grad = (wide * (probs_grad - delta)).astype(BF)
                v_grad = v_grad + mm(low, jnp.where(lanes, up, zero), ((0,), (0,)))
                q_grad = q_grad + mm(scores_grad, jnp.where(lanes, k, zero), ((1,), (0,)))
                k_grad = k_grad + mm(scores_grad, jnp.where(lanes, q, zero), ((0,), (0,)))
            proj_grad[i, :, place_of(0)] = (q_grad * HD ** (-0.5)).astype(BF)
            proj_grad[i, :, place_of(1)] = (k_grad * HD ** (-0.5)).astype(BF)
            proj_grad[i, :, place_of(2)] = v_grad.astype(BF)
            return carry

        lax.fori_loop(0, pairs, pair_step, 0)
    total_grad[...] = sum(
        mm(proj_grad[i, :, which * cols : (which + 1) * cols], w_vmem[i, which], ((1,), (1,)))
        for i in range(2)
        for which in range(3)
    ).astype(BF)
    pack(total_grad[...], given_2, maps, whole)
    second = list(zip(given_2, taken_2))
    send_all(second, send_2, recv_2)

    base = 2 * steps
    late_copy = [
        pair_copy(base + j, late_give.at[:, part], late_got.at[:, part])
        for j, part in enumerate((left_half, right_half))
    ]
    def attend_at(which):
        return pl.ds(pl.multiple_of(which * cols, 128), cols)

    def late_other(which, carry):
        value = mm(buffer[...], proj_grad[1, :, attend_at(which)], ((0,), (0,)))
        act[pl.ds(0, width), attend_at(which)] = value.astype(BF)
        return carry

    def late_own(which, carry):
        value = mm(buffer[...], proj_grad[0, :, attend_at(which)], ((0,), (0,)))
        got = pre_grad[pl.ds(0, width), attend_at(which)].astype(F32)
        late_acc[:, attend_at(which)] = (value + got).astype(BF)
        return carry

    lax.fori_loop(0, 3, late_other, 0)
    for copy in late_copy:
        copy.start()
    for copy in late_copy:
        copy.wait_recv()
    lax.fori_loop(0, 3, late_own, 0)
    late_acc[:, attend_cols:] = (
        late_acc[:, attend_cols:].astype(F32) + late_got[:, attend_cols:].astype(F32)
    ).astype(BF)
    for chain in chains[2:]:
        chain.begin()
    layer_copy = pair_copy(
        base + 2, layer_own, reduce_got.at[pl.ds(0, count), pl.ds(0, width)]
    )
    layer_copy.start()
    steps_left = halving_plan(stages) if chains else []
    cuts = [len(steps_left) * part // 15 for part in (5, 10, 13, 15)]
    advance(chains[:2], steps_left[: cuts[0]])

    wait_all(second, send_2, recv_2)
    unpack(taken_2, maps, whole, upstream)
    step_rows = 32
    tokens_own = reduce_give.at[pl.ds(0, count), pl.ds(0, width)]
    tokens_got = expand_got.at[pl.ds(0, count), pl.ds(0, width)]

    def norm_rows(r, carry, kept):
        rows = pl.ds(pl.multiple_of(r * step_rows, step_rows), step_rows)
        normal, scale = norm_stats(x[rows, :].astype(F32))
        normed = (normal * gain[...] + shift[...]).astype(BF).astype(F32)
        logit = logit_grad[rows, :]
        grad = logit * router[...]
        if kept:
            grad = grad + jnp.where(mask[rows, :] > 0.5, upstream[rows, :].astype(F32), 0.0)
        total = mixed_grad[rows, :] + norm_pull(grad * gain[...], normal, scale)
        reduce_give[rows, pl.ds(0, width)] = total.astype(BF)
        return (
            carry[0] + row_sums(grad * normal),
            carry[1] + row_sums(grad),
            carry[2] + row_sums(logit * normed),
        )

    zeros = jnp.zeros((8, width), F32)
    carry = (zeros, zeros, zeros)
    kept_steps = slots // step_rows
    carry = lax.fori_loop(0, kept_steps, functools.partial(norm_rows, kept=True), carry)
    carry = lax.fori_loop(
        kept_steps, count // step_rows, functools.partial(norm_rows, kept=False), carry
    )
    tokens_copy = pair_copy(base + 3, tokens_own, tokens_got)
    tokens_copy.start()
    for i in range(3):
        sums[0, i : i + 1, :] = jnp.sum(carry[i], axis=0, keepdims=True)
    sums[0, 3:5, :] = second_sums[...]
    sums[0, 5:8, :] = jnp.zeros((3, width), F32)

    def sums_copy(stage):
        if stage < sums_got.shape[0] - 1:
            bit = lax.rem(lax.div(dp, 1 << stage), 2)
            to = (dp + (1 - 2 * bit) * (1 << stage), core)
        else:
            to = (dp, 1 - core)
        return pltpu.make_async_remote_copy(
            src_ref=sums.at[stage],
            dst_ref=sums_got.at[stage],
            send_sem=sums_send.at[stage],
            recv_sem=sums_recv.at[stage],
            device_id=to,
            device_id_type=MESH,
        )

    sums_stages = sums_got.shape[0]
    sums_copy(0).start()

    def sums_step(stage):
        sums_copy(stage).wait_recv()
        total = sums[stage] + sums_got[stage]
        if stage + 1 < sums_stages:
            sums[stage + 1] = total
            sums_copy(stage + 1).start()
        else:
            sums_out[...] = total

    def unpick(own, other, out, stage, sems):
        total = out.shape[0]
        block = stage.shape[1]
        full = total // block
        tail = total - full * block

        def out_copy(r, size):
            slot = lax.rem(r, 2)
            rows = pl.ds(pl.multiple_of(r * block, block), size)
            return pltpu.make_async_copy(
                stage.at[slot, pl.ds(0, size), :], out.at[rows, :], sems.at[slot]
            )

        def emit(r, size):
            rows = pl.ds(pl.multiple_of(r * block, block), size)
            hit = (place[rows, :] == want[...]).astype(F32).astype(BF)
            value = mm(hit[:, :count], own[...], ((1,), (0,))) + mm(
                hit[:, count:], other[...], ((1,), (0,))
            )
            stage[lax.rem(r, 2), pl.ds(0, size), :] = value.astype(out.dtype)
            out_copy(r, size).start()

        def body(r, carry):
            @pl.when(r >= 2)
            def _():
                out_copy(r - 2, block).wait()

            emit(r, block)
            return carry

        lax.fori_loop(0, full, body, 0)
        if tail:
            out_copy(full - 2, block).wait()
            emit(full, tail)
            out_copy(full - 1, block).wait()
            out_copy(full, tail).wait()
        else:
            out_copy(full - 2, block).wait()
            out_copy(full - 1, block).wait()

    advance(chains[:2], steps_left[cuts[0] : cuts[1]])
    layer_copy.wait_recv()
    layer_got = reduce_got.at[pl.ds(0, count), pl.ds(0, width)]
    unpick(layer_own, layer_got, layer_out, layer_stage, out_sem.at[0])
    sums_step(0)
    advance(chains[:2], steps_left[cuts[1] : cuts[2]])
    sums_step(1)
    tokens_copy.wait_recv()
    unpick(tokens_own, tokens_got, tokens_out, tokens_stage, out_sem.at[1])
    sums_step(2)
    advance(chains[:2], steps_left[cuts[2] :])
    for stage in range(3, sums_stages):
        sums_step(stage)
    advance(chains[2:], steps_left)
    for chain in chains:
        chain.drain()
    for copy in (*late_copy, layer_copy, tokens_copy):
        copy.wait_send()
    for stage in range(sums_stages):
        sums_copy(stage).wait_send()


def split_blocks(blocks):
    step = len(blocks) // 4
    return [blocks[i * step : (i + 1) * step] for i in range(4)]


def block_scratch(peers, whole, left, parts, width):
    shapes = [(peers, whole, width)] if whole else []
    shapes.append((peers, 16, width // parts))
    return [pltpu.VMEM(shape, BF) for _ in range(4) for shape in shapes], len(shapes)


def exchange_call(
    kernel, name, collective_id, capacity, args, spaces, outs, scratch, after=(), out_spaces=None
):
    width = args[0].shape[1]
    peers = lax.axis_size("dp")
    whole, left, parts = block_plan(capacity, width)
    blocks, kinds = block_scratch(peers, whole, left, parts, width)
    return pl.pallas_call(
        functools.partial(kernel, whole),
        out_shape=[jax.ShapeDtypeStruct(*out) for out in outs],
        in_specs=[pl.BlockSpec(memory_space=space) for space in spaces],
        out_specs=[
            pl.BlockSpec(memory_space=space) for space in out_spaces or [pltpu.VMEM] * len(outs)
        ],
        scratch_shapes=[
            *scratch,
            *[pltpu.SemaphoreType.DMA((kinds, peers))] * 4,
            *blocks,
            *after,
        ],
        compiler_params=pltpu.CompilerParams(
            collective_id=collective_id, has_side_effects=True, vmem_limit_bytes=58 * 2**20
        ),
        name=name,
    )(*args)


def attend(normed, maps, w_own, w_other, capacity):
    slots, width = normed.shape
    columns = 3 * w_own.shape[2]
    heads = 2 * columns // 3 // HD
    return exchange_call(
        attend_kernel, "attend", 0, capacity,
        (normed, maps, w_own, w_other),
        (pltpu.VMEM, pltpu.VMEM, pl.ANY, pl.ANY),
        [
            (shape, BF)
            for shape in ((slots, width), (slots, width), (2, slots, columns), (heads, slots, slots))
        ],
        [
            pltpu.VMEM((2, *w_own.shape), BF),
            pltpu.VMEM((slots, width), BF),
            pltpu.VMEM((8, slots), F32),
            pltpu.SemaphoreType.DMA((2,)),
        ],
    )


def back(
    context_grad, maps, buffer, attended_grad, gathered, hidden_t, ct_t,
    mask, x, mixed_grad, logit_grad, layer_own, second_sums, gain, shift, router, place, want,
    act, pre_grad, w_own, w_other, proj, probs, capacity, orders,
):
    slots, width = buffer.shape
    columns = proj.shape[2]
    hidden = act.shape[2]
    loaded = (buffer, attended_grad, gathered, hidden_t, ct_t, x, mixed_grad, layer_own)
    count = x.shape[0]
    peers = lax.axis_size("dp")
    vmem, hbm = pltpu.VMEM, pl.ANY
    dma = pltpu.SemaphoreType.DMA
    rows = width // peers
    after = []
    if orders is None:
        outs = [((width, hidden), BF)] * 3
    else:
        outs = [((rows, hidden), F32)] * 3
        counts = [peers >> (stage + 1) for stage in range(len(orders[0]))]
        for size in (hidden, hidden, hidden // 2, hidden // 2):
            after += [dma((sum(counts),))] * 2
            after += [vmem((n, rows, size), BF) for n in counts]
    outs += [((place.shape[0], width), BF), ((place.shape[0], width), F32), ((8, width), F32)]
    chunks = 2 * (hidden // (512 if hidden % 512 == 0 else hidden)) + 4
    wide = vmem((width, hidden), BF)
    sums_stages = peers.bit_length()
    return exchange_call(
        lambda whole, *refs: back_kernel(whole, orders, *refs), "back", 1, capacity,
        (context_grad, maps, mask, logit_grad, second_sums, gain, shift, router, place, want,
         act, pre_grad, w_own, w_other, proj, probs, *loaded),
        (vmem,) * 10 + (hbm,) * (6 + len(loaded)),
        outs,
        [
            vmem((2 * count, hidden), BF), vmem((2 * count, hidden), BF),
            vmem((2, *w_own.shape), BF), vmem(proj.shape, BF), vmem(probs.shape, BF),
            vmem((slots, width), BF), vmem((2, slots, columns), BF), vmem((slots, width), BF),
            wide, wide, wide, wide,
            *((wide, wide) if orders else [vmem((16, 128), BF)] * 2),
            vmem((sums_stages, 8, width), F32), vmem((sums_stages, 8, width), F32),
            vmem((2, 128, width), BF), vmem((2, 128, width), F32), dma((2, 2)),
            *[vmem(value.shape, value.dtype) for value in loaded],
            dma((8 + len(loaded),)), dma((chunks,)), dma((chunks,)), dma((sums_stages,)), dma((sums_stages,)),
            pltpu.SemaphoreType.REGULAR,
        ],
        after,
        (vmem, vmem, vmem, hbm, hbm, vmem),
    )


def half_erfc(value, bell):
    t = 1.0 / (1.0 + (0.3275911 * 0.5**0.5) * jnp.abs(value))
    poly = 1.061405429 * t - 1.453152027
    poly = poly * t + 1.421413741
    poly = poly * t - 0.284496736
    poly = poly * t + 0.254829592
    return 0.5 * poly * t * bell


def row_sums(value):
    return jnp.sum(value.reshape(value.shape[0] // 8, 8, value.shape[1]), axis=0)


def feed_kernel(
    gathered, mask, x, ct, gate, gain, shift, wo_own, wo_other, we_own, we_other, wr_own, wr_other,
    layer, mixed_grad, attended_grad, context_grad, logit_grad, sums, hidden_t, ct_t, act_out, pre_out,
    we, wr, attended, mixed, nhat, inv, hidden, mlp, hidden_grad, pre, act_grad, act, pre_grad,
    we_sem, wr_sem, act_sem, pre_sem,
):
    core = lax.axis_index("mp")
    slots, width = gathered.shape
    count = x.shape[0]
    columns = we_own.shape[1]
    chunk = pre.shape[1]
    steps = columns // chunk
    cols = wo_own.shape[0]
    step_rows = 32

    def chunk_loads(i, j):
        at = pl.ds(pl.multiple_of(j * chunk, 128), chunk)
        here_e, here_r = (we_own, wr_own) if i == 0 else (we_other, wr_other)
        return (
            pltpu.make_async_copy(here_e.at[:, at], we.at[i * steps + j], we_sem.at[i * steps + j]),
            pltpu.make_async_copy(here_r.at[at, :], wr.at[i * steps + j], wr_sem.at[i * steps + j]),
        )

    for i in range(2):
        for j in range(steps):
            for load in chunk_loads(i, j):
                load.start()

    own_cols = pl.ds(pl.multiple_of(core * cols, 128), cols)
    other_cols = pl.ds(pl.multiple_of((1 - core) * cols, 128), cols)
    attended[...] = mm(gathered[:, own_cols], wo_own[...], ((1,), (0,))) + mm(
        gathered[:, other_cols], wo_other[...], ((1,), (0,))
    )

    def rows_of(r):
        return pl.ds(pl.multiple_of(r * step_rows, step_rows), step_rows)

    def norm_rows(r, carry, kept):
        at = rows_of(r)
        value = x[at, :].astype(F32)
        if kept:
            shown = jnp.where(mask[at, :] > 0.5, attended[at, :], 0.0)
            attended[at, :] = shown
            value = value + gate[at, :] * shown
        mixed[at, :] = value
        normal, scale = norm_stats(value)
        nhat[at, :] = normal
        inv[at, :] = scale
        hidden[at, :] = (normal * gain[...] + shift[...]).astype(BF)
        mlp[at, :] = jnp.zeros((step_rows, width), F32)
        hidden_grad[at, :] = jnp.zeros((step_rows, width), F32)
        return carry

    kept_steps = slots // step_rows
    lax.fori_loop(0, kept_steps, functools.partial(norm_rows, kept=True), 0)
    lax.fori_loop(kept_steps, count // step_rows, functools.partial(norm_rows, kept=False), 0)
    hidden_t[...] = hidden[...].T
    ct_t[...] = ct[...].T

    def outs(i, j):
        at = pl.ds(pl.multiple_of(j * chunk, 128), chunk)
        n = i * steps + j
        return (
            pltpu.make_async_copy(act.at[n % 2], act_out.at[i, :, at], act_sem.at[n]),
            pltpu.make_async_copy(pre_grad.at[n % 2], pre_out.at[i, :, at], pre_sem.at[n]),
        )

    for n, (i, j) in enumerate([(i, j) for i in range(2) for j in range(steps)]):
        for load in chunk_loads(i, j):
            load.wait()
        w_e, w_r = we[n], wr[n]
        pre[...] = mm(hidden[...], w_e, ((1,), (0,)))
        act_grad[...] = mm(ct[...], w_r, ((1,), (1,)))
        if n >= 2:
            m = n - 2
            for out in outs(m // steps, m % steps):
                out.wait()

        def gelu_rows(r, carry, n=n):
            at = pl.ds(pl.multiple_of(r * 16, 16), 16)
            value = pre[at, :]
            bell = jnp.exp(-0.5 * value * value)
            tail = half_erfc(value, bell)
            phi = jnp.where(value < 0.0, tail, 1.0 - tail)
            act[n % 2, at, :] = (value * phi).astype(BF)
            slope = phi + value * bell * 0.3989422804014327
            pre_grad[n % 2, at, :] = (act_grad[at, :] * slope).astype(BF)
            return carry

        lax.fori_loop(0, count // 16, gelu_rows, 0, unroll=2)
        for out in outs(i, j):
            out.start()
        mlp[...] += mm(act[n % 2], w_r, ((1,), (0,)))
        hidden_grad[...] += mm(pre_grad[n % 2], w_e, ((1,), (1,)))

    def back_rows(r, carry, kept):
        at = rows_of(r)
        layer[at, :] = (mixed[at, :] + mlp[at, :]).astype(BF)
        grad = hidden_grad[at, :]
        normal = nhat[at, :]
        total = ct[at, :].astype(F32) + norm_pull(grad * gain[...], normal, inv[at, :])
        mixed_grad[at, :] = total
        if kept:
            scale = gate[at, :]
            attended_grad[at, :] = jnp.where(mask[at, :] > 0.5, scale * total, 0.0).astype(BF)
            logit_grad[at, :] = (
                jnp.sum(total * attended[at, :], axis=-1, keepdims=True) * scale * (1.0 - scale)
            )
        else:
            logit_grad[at, :] = jnp.zeros((step_rows, 1), F32)
        return (carry[0] + row_sums(grad * normal), carry[1] + row_sums(grad))

    zeros = jnp.zeros((8, width), F32)
    carry = lax.fori_loop(0, kept_steps, functools.partial(back_rows, kept=True), (zeros, zeros))
    carry = lax.fori_loop(
        kept_steps, count // step_rows, functools.partial(back_rows, kept=False), carry
    )
    for i in range(2):
        sums[i : i + 1, :] = jnp.sum(carry[i], axis=0, keepdims=True)
    for w, at in ((wo_own, own_cols), (wo_other, other_cols)):
        part = mm(attended_grad[...], w[...], ((1,), (1,)))
        context_grad[:, at] = jnp.where(mask[...] > 0.5, part, 0.0).astype(BF)
    last = 2 * steps
    for n in range(max(0, last - 2), last):
        for out in outs(n // steps, n % steps):
            out.wait()


def feed(gathered, mask, x, ct, gate, gain, shift, w_output_2, w_expand_2, w_reduce_2):
    slots, width = gathered.shape
    count = x.shape[0]
    columns = w_expand_2[0].shape[1]
    chunk = 512 if columns % 512 == 0 else columns
    steps = columns // chunk
    vmem, hbm = pltpu.VMEM, pl.ANY
    dma = pltpu.SemaphoreType.DMA
    outs = [
        ((count, width), BF, vmem), ((count, width), F32, vmem), ((slots, width), BF, vmem),
        ((slots, width), BF, vmem), ((count, 1), F32, vmem), ((2, width), F32, vmem),
        ((width, count), BF, vmem), ((width, count), BF, vmem),
        ((2, count, columns), BF, hbm), ((2, count, columns), BF, hbm),
    ]
    return pl.pallas_call(
        feed_kernel,
        out_shape=[jax.ShapeDtypeStruct(shape, kind) for shape, kind, _ in outs],
        in_specs=[pl.BlockSpec(memory_space=space) for space in (vmem,) * 9 + (hbm,) * 4],
        out_specs=[pl.BlockSpec(memory_space=space) for _, _, space in outs],
        scratch_shapes=[
            vmem((2 * steps, width, chunk), BF), vmem((2 * steps, chunk, width), BF),
            vmem((slots, width), F32), vmem((count, width), F32), vmem((count, width), F32),
            vmem((count, 1), F32), vmem((count, width), BF), vmem((count, width), F32),
            vmem((count, width), F32), vmem((count, chunk), F32), vmem((count, chunk), F32),
            vmem((2, count, chunk), BF), vmem((2, count, chunk), BF),
            *[dma((2 * steps,))] * 4,
        ],
        compiler_params=pltpu.CompilerParams(vmem_limit_bytes=48 * 2**20),
        name="feed",
    )(gathered, mask, x, ct, gate, gain[None], shift[None], *w_output_2, *w_expand_2, *w_reduce_2)


def shards(
    tokens,
    row_ids,
    select,
    priority,
    first_gain,
    first_shift,
    router,
    w_attend,
    w_output,
    second_gain,
    second_shift,
    w_expand,
    w_reduce,
    cotangent,
):
    dp_count = lax.axis_size("dp")
    mp_count = lax.axis_size("mp")
    core = lax.axis_index("mp")
    bits = dp_count.bit_length() - 1
    order_a = list(range(bits))
    order_b = [1, 0] + list(range(bits - 1, 1, -1))
    rows = dp_count * mp_count
    capacity = 5 * ROW_LEN // (8 * dp_count)
    count, width = tokens.shape
    own = count // mp_count
    own_pad = -(-own // 128) * 128
    slots = dp_count * capacity
    heads_cols = w_attend.shape[2]
    whole, left, parts = block_plan(capacity, width)
    maps = rest_map(dp_count, left, parts)

    w_attend = w_attend.transpose(1, 0, 2)
    w_attend_2 = (w_attend, swap(w_attend))
    w_output_2 = (w_output, swap(w_output))
    w_expand_2 = (w_expand, swap(w_expand))
    w_reduce_2 = (w_reduce, swap(w_reduce))

    chosen = select == 1
    same_row = row_ids[:, None] == row_ids[None, :]
    earlier = priority[None, :] < priority[:, None]
    rank = jnp.sum((same_row & earlier & chosen[None, :]).astype(jnp.int32), axis=1)
    kept = chosen & (rank < capacity)
    taken = jnp.sum(
        ((row_ids[None, :] == jnp.arange(rows)[:, None]) & kept[None, :]).astype(jnp.int32), axis=1
    )
    at = jnp.arange(slots)
    row_at = jnp.where(at < dp_count * whole, at // max(whole, 1), (at - dp_count * whole) // left)
    rank_at = jnp.where(
        at < dp_count * whole, at % max(whole, 1), whole + (at - dp_count * whole) % left
    )
    hits = (row_at[:, None] == jnp.arange(dp_count)[None, :]).astype(jnp.int32)
    taken_at = jnp.sum(hits[None] * taken.reshape(dp_count, mp_count).T[:, None, :], axis=2)
    filled = rank_at[None, :] < taken_at
    filled_all = jnp.pad(filled, ((0, 0), (0, own - slots))).reshape(count)
    peer = row_ids // mp_count
    place = jnp.where(
        kept,
        (row_ids % mp_count) * own
        + jnp.where(
            rank < whole, peer * whole + rank, dp_count * whole + peer * left + rank - whole
        ),
        count + jnp.cumsum(jnp.where(kept, 0, 1)),
    )
    want = jnp.where(filled_all, jnp.arange(count), count + jnp.cumsum(jnp.where(filled_all, 0, 1)))
    want = jnp.pad(want.reshape(mp_count, own), ((0, 0), (0, own_pad - own)), constant_values=-1)
    want_own = jnp.where(core == 0, want[0], want[1])
    want_other = jnp.where(core == 0, want[1], want[0])
    mask = jnp.where(core == 0, filled[0], filled[1])[:, None]
    pick_own = (want_own[:, None] == place[None, :]).astype(BF)

    x = mm(pick_own, tokens, ((1,), (0,)))
    ct = mm(pick_own, cotangent, ((1,), (0,))).astype(BF)

    nhat_1, inv_1 = norm_stats(x)
    normed = (nhat_1 * first_gain + first_shift).astype(BF)
    normed_wide = normed.astype(F32)
    mask_wide, x_low = mask.astype(F32), x.astype(BF)
    gate = jax.nn.sigmoid(jnp.sum(normed_wide * router, axis=-1, keepdims=True))

    gathered, buffer, proj, probs = attend(
        jnp.where(mask, normed[:slots], jnp.asarray(EMPTY, BF)), maps, *w_attend_2, capacity
    )
    (layer_own, mixed_grad, attended_grad, context_grad, logit_grad, sums, hidden_t, ct_t, acts, pre_grads) = feed(
        gathered, mask_wide, x_low, ct, gate, second_gain, second_shift,
        w_output_2, w_expand_2, w_reduce_2,
    )
    place_pad = jnp.pad(place.astype(jnp.int32), (0, -count % 16), constant_values=-2)[:, None]
    orders = (order_a, order_b) if width // dp_count % 16 == 0 else None
    expand_sum, reduce_sum, late_sum, layer_out, tokens_grad, vectors = back(
        context_grad, maps, buffer, attended_grad, gathered, hidden_t, ct_t,
        mask_wide, x_low, mixed_grad, logit_grad, layer_own, sums, first_gain[None], first_shift[None],
        router[None], place_pad, jnp.concatenate([want_own, want_other])[None].astype(jnp.int32),
        acts, pre_grads, *w_attend_2, proj, probs, capacity, orders,
    )
    if orders is None:
        expand_sum = scatter_sum(expand_sum, order_a)
        reduce_sum = scatter_sum(reduce_sum, order_b)
        late_sum = scatter_sum(late_sum, order_a)
    rows_here = width // dp_count
    vectors = lax.dynamic_slice_in_dim(vectors, lax.axis_index("dp") * rows_here, rows_here, 1)

    attend_cols = 3 * heads_cols
    return (
        layer_out[:count],
        tokens_grad[:count],
        vectors[0],
        vectors[1],
        vectors[2],
        late_sum[:, :attend_cols].reshape(-1, 3, heads_cols),
        late_sum[:, attend_cols:].T,
        vectors[3],
        vectors[4],
        expand_sum,
        reduce_sum.T,
    )


def solution(mesh):
    in_specs = (
        P("dp", None),
        P("dp"),
        P("dp"),
        P("dp"),
        P(),
        P(),
        P(),
        P(None, None, "mp"),
        P("mp", None),
        P(),
        P(),
        P(None, "mp"),
        P("mp", None),
        P("dp", None),
    )
    out_specs = (
        P("dp", None),
        P("dp", None),
        P("dp"),
        P("dp"),
        P("dp"),
        P("dp", None, "mp"),
        P("mp", "dp"),
        P("dp"),
        P("dp"),
        P("dp", "mp"),
        P("mp", "dp"),
    )
    return jax.shard_map(shards, mesh=mesh, in_specs=in_specs, out_specs=out_specs, check_vma=False)
```

```python
import functools

import jax
import jax.numpy as jnp
import numpy as np
from jax import lax
from jax.experimental import pallas as pl
from jax.experimental.pallas import tpu as pltpu
from jax.sharding import PartitionSpec as P

HD = 64
ROW_LEN = 577
EPSILON = 1e-06
MASKED_SCORE = -1000000000.0
EMPTY = 1e30
BF = jnp.bfloat16
F32 = jnp.float32
MESH = pl.DeviceIdType.MESH


def mm(a, b, dims):
    return lax.dot_general(a, b, (dims, ((), ())), preferred_element_type=F32)


def norm_stats(value):
    center = value - jnp.mean(value, axis=-1, keepdims=True)
    inv = lax.rsqrt(jnp.mean(center * center, axis=-1, keepdims=True) + EPSILON)
    return center * inv, inv


def norm_pull(e, nhat, inv):
    return (e - jnp.mean(e, axis=-1, keepdims=True) - nhat * jnp.mean(e * nhat, axis=-1, keepdims=True)) * inv


def swap(value):
    return lax.ppermute(value, "mp", [(0, 1), (1, 0)])


def scatter_sum(grad, order):
    count = lax.axis_size("dp")
    me = lax.axis_index("dp")
    bits = count.bit_length() - 1
    width = grad.shape[0] // count
    dims = [2] * bits
    value = grad.reshape(dims + [width, grad.shape[1]])
    out = None
    for step in order:
        axis = bits - 1 - step
        mine = (me >> step) & 1
        give = lax.dynamic_slice_in_dim(value, 1 - mine, 1, axis)
        keep = lax.dynamic_slice_in_dim(value, mine, 1, axis)
        got = lax.ppermute(give, "dp", [(i, i ^ (1 << step)) for i in range(count)])
        out = keep.astype(F32) + got.astype(F32)
        value = out.astype(grad.dtype)
    return out.reshape(width, grad.shape[1])


def block_plan(capacity, width):
    whole = capacity // 16 * 16
    left = capacity - whole
    parts = max(s for s in (1, 2, 3, 6) if left * s <= 16 and width % (128 * s) == 0)
    return whole, left, parts


def rest_map(peers, left, parts):
    at = jnp.arange(peers * 16)[None, :, None]
    row = jnp.arange(peers * left)[None, None, :]
    part = jnp.arange(parts)[:, None, None]
    return ((at // 16 == row // left) & (at % 16 == part * left + row % left)).astype(BF)


def greet(peers, with_pair=False):
    me, core = lax.axis_index("dp"), lax.axis_index("mp")
    barrier = pltpu.get_barrier_semaphore()

    def hello(d, carry):
        pl.semaphore_signal(
            barrier, inc=1, device_id=(lax.rem(me + d, peers), core), device_id_type=MESH
        )
        return carry

    lax.fori_loop(1, peers, hello, 0)
    if with_pair:
        pl.semaphore_signal(barrier, inc=1, device_id=(me, 1 - core), device_id_type=MESH)
    return lambda: pl.semaphore_wait(barrier, peers if with_pair else peers - 1)


def pack(value, blocks, maps, whole):
    rest = blocks[-1]
    peers, lanes = rest.shape[0], rest.shape[2]
    if whole:
        blocks[0][...] = value[: peers * whole].reshape(peers, whole, value.shape[1])
    tail = value[peers * whole :]
    total = sum(
        mm(maps[i], tail[:, i * lanes : (i + 1) * lanes], ((1,), (0,)))
        for i in range(maps.shape[0])
    )
    rest[...] = total.astype(BF).reshape(peers, 16, lanes)


def unpack(blocks, maps, whole, out):
    rest = blocks[-1]
    peers, lanes = rest.shape[0], rest.shape[2]
    if whole:
        out[: peers * whole, :] = blocks[0][...].reshape(peers * whole, out.shape[1])
    left = rest[...].reshape(peers * 16, lanes)
    for i in range(maps.shape[0]):
        out[peers * whole :, i * lanes : (i + 1) * lanes] = mm(
            maps[i], left, ((0,), (0,))
        ).astype(BF)


def copies(d, pairs, sends, recvs, back=False):
    me, core = lax.axis_index("dp"), lax.axis_index("mp")
    peers = pairs[0][0].shape[0]
    to, source = lax.rem(me + d, peers), lax.rem(me + peers - d, peers)
    return [
        pltpu.make_async_remote_copy(
            src_ref=here.at[to],
            dst_ref=there.at[source if back else me],
            send_sem=sends.at[i, d],
            recv_sem=recvs.at[i, d],
            device_id=(to, core),
            device_id_type=MESH,
        )
        for i, (here, there) in enumerate(pairs)
    ]


def send_all(pairs, sends, recvs):
    me = lax.axis_index("dp")

    def start(d, carry):
        for copy in copies(d, pairs, sends, recvs):
            copy.start()
        return carry

    lax.fori_loop(1, pairs[0][0].shape[0], start, 0)
    for here, there in pairs:
        there[pl.ds(me, 1)] = here[pl.ds(me, 1)]


def wait_all(pairs, sends, recvs):
    def finish(d, carry):
        for copy in copies(d, pairs, sends, recvs, back=True):
            copy.wait_recv()
        return carry

    def drain(d, carry):
        for copy in copies(d, pairs, sends, recvs):
            copy.wait_send()
        return carry

    lax.fori_loop(1, pairs[0][0].shape[0], finish, 0)
    lax.fori_loop(1, pairs[0][0].shape[0], drain, 0)


def lane_masks():
    low = lax.broadcasted_iota(jnp.int32, (1, 128), 1) < HD
    return low, jnp.logical_not(low)


def routing(info, layout, capacity, count, wide_cols, hit_rows, routes, route_cols):
    core = lax.axis_index("mp").astype(F32)
    cores = lax.axis_size("mp")
    total = info.shape[1]
    blocks = total // 128
    row, chosen, priority = (info[i : i + 1, :].astype(F32) for i in range(3))
    device, slot, spot, side = (layout[i : i + 1, :].astype(F32) for i in range(4))
    core_of = core + side * (1.0 - 2.0 * core)
    row_of = device * cores + core_of
    spot_of = jnp.where(spot >= 0.0, core_of * total + spot, -1.0)
    low = row * 2048.0
    key = low + priority
    picked = chosen > 0.5
    hit_rows[...] = jnp.zeros(hit_rows.shape, F32)
    hit_rows[0:1, :] = jnp.where(picked, key, -1.0)
    hit_rows[1:2, :] = jnp.where(picked, row, -1.0)
    wide_cols[...] = hit_rows[...].T

    def fold(hit):
        return jnp.sum(jnp.where(hit, 1.0, 0.0).reshape(16, 8, total), axis=0)

    def count_rows(b, carry):
        at = pl.ds(pl.multiple_of(b * 128, 128), 128)
        keys, rows = wide_cols[at, 0:1], wide_cols[at, 1:2]
        return (
            carry[0] + fold((keys >= low) & (keys < key)),
            carry[1] + fold(rows == row_of),
        )

    zeros = jnp.zeros((8, total), F32)
    ranks, sizes = lax.fori_loop(0, blocks, count_rows, (zeros, zeros))
    rank = jnp.sum(ranks, axis=0, keepdims=True)
    size = jnp.sum(sizes, axis=0, keepdims=True)
    kept = picked & (rank < capacity)
    filled = slot < jnp.minimum(size, float(capacity))
    index = lax.broadcasted_iota(jnp.int32, (1, total), 1).astype(F32)
    rest = (index < count) & jnp.logical_not(kept)
    free = (spot_of >= 0.0) & jnp.logical_not(filled)
    hit_rows[0:1, :] = jnp.where(rest, index, 1e9)
    hit_rows[1:2, :] = jnp.where(free, spot_of, 1e9)
    wide_cols[...] = hit_rows[...].T

    def count_rest(b, carry):
        at = pl.ds(pl.multiple_of(b * 128, 128), 128)
        return (
            carry[0] + fold(wide_cols[at, 0:1] < index),
            carry[1] + fold(wide_cols[at, 1:2] < spot_of),
        )

    before, ahead = lax.fori_loop(0, blocks, count_rest, (zeros, zeros))
    base = float(lax.axis_size("dp") * cores * capacity)
    before = base + jnp.sum(before, axis=0, keepdims=True)
    ahead = base + jnp.sum(ahead, axis=0, keepdims=True)
    routes[...] = jnp.zeros(routes.shape, F32)
    routes[0:1, :] = jnp.where(
        filled, row_of * capacity + slot, jnp.where(spot_of >= 0.0, ahead, -1.0)
    )
    routes[1:2, :] = jnp.where(filled, 1.0, 0.0)
    routes[2:3, :] = jnp.where(kept, row * capacity + rank, jnp.where(rest, before, -2.0))
    route_cols[...] = routes[...].T


def attend_kernel(
    whole, capacity, info, layout, vectors, maps, tokens_in, cotangent_in, w_own, w_other,
    gathered, buffer, proj, probs, x, ct, gate, routes, route_cols,
    tokens, cotangent, wide_cols, hit_rows,
    w_vmem, context, key_mask, w_sem, send_1, recv_1, send_2, recv_2, *blocks,
):
    core = lax.axis_index("mp")
    loads = [
        pltpu.make_async_copy(here, there, w_sem.at[i])
        for i, (here, there) in enumerate(
            (
                (tokens_in, tokens),
                (cotangent_in, cotangent),
                (w_own, w_vmem.at[0]),
                (w_other, w_vmem.at[1]),
            )
        )
    ]
    for load in loads:
        load.start()
    given_1, taken_1, given_2, taken_2 = split_blocks(blocks)
    ready = greet(given_1[-1].shape[0])
    count, width = tokens.shape
    slots = buffer.shape[0]
    total_rows = x.shape[0]
    routing(info, layout, capacity, count, wide_cols, hit_rows, routes, route_cols)
    loads[0].wait()

    def pick(r, source, out):
        at = pl.ds(pl.multiple_of(r * 128, 128), 128)
        hit = (route_cols[at, 0:1] == routes[2:3, :count]).astype(F32).astype(BF)
        out[at, :] = mm(hit, source[...], ((1,), (0,))).astype(BF)

    def norm_rows(r, carry, sent):
        at = pl.ds(pl.multiple_of(r * 32, 32), 32)
        normal, _ = norm_stats(x[at, :].astype(F32))
        normed = (normal * vectors[0:1, :] + vectors[1:2, :]).astype(BF)
        wide = normed.astype(F32)
        gate[at, :] = jax.nn.sigmoid(jnp.sum(wide * vectors[2:3, :], axis=-1, keepdims=True))
        if sent:
            context[at, :] = jnp.where(route_cols[at, 1:2] > 0.5, wide, EMPTY).astype(BF)
        return carry

    def picks(first, last, source, out):
        def body(r, carry):
            pick(r, source, out)
            return carry

        lax.fori_loop(first, last, body, 0)

    kept_blocks = -(-slots // 128)
    picks(0, kept_blocks, tokens, x)
    lax.fori_loop(0, slots // 32, functools.partial(norm_rows, sent=True), 0)
    pack(context[...], given_1, maps, whole)
    ready()
    first = list(zip(given_1, taken_1))
    send_all(first, send_1, recv_1)
    picks(kept_blocks, total_rows // 128, tokens, x)
    lax.fori_loop(slots // 32, total_rows // 32, functools.partial(norm_rows, sent=False), 0)
    loads[1].wait()
    picks(0, total_rows // 128, cotangent, ct)
    wait_all(first, send_1, recv_1)
    unpack(taken_1, maps, whole, buffer)
    lane = (lax.broadcasted_iota(jnp.int32, (8, 128), 1) == 0).astype(F32).astype(BF)
    key_mask[...] = jnp.where(
        mm(lane, buffer[:, :128], ((1,), (1,))) < 0.5 * EMPTY, 1.0, 0.0
    )
    received = buffer[...].astype(F32)
    buffer[...] = jnp.where(received[:, :1] < 0.5 * EMPTY, received, 0.0).astype(BF)
    cols = w_own.shape[2]
    pairs = cols // 128
    masks = lane_masks()
    zero = jnp.zeros((), BF)
    for i in range(2):
        loads[2 + i].wait()
        for which in range(3):
            proj[i, :, which * cols : (which + 1) * cols] = mm(
                buffer[...], w_vmem[i, which], ((1,), (0,))
            ).astype(BF)
        canonical = core if i == 0 else 1 - core

        def pair_step(p, carry, i=i, canonical=canonical):
            def part(which):
                return proj[i, :, pl.ds(pl.multiple_of(which * cols + p * 128, 128), 128)]

            q, k, v = part(0), part(1), part(2)
            total = 0.0
            for e, lanes in enumerate(masks):
                scores = mm(q, jnp.where(lanes, k, zero), ((1,), (1,))) * HD ** (-0.5)
                scores = jnp.where(key_mask[:1, :] > 0.5, scores, MASKED_SCORE)
                weights = jnp.exp(scores - jnp.max(scores, axis=-1, keepdims=True))
                low = (weights * (1.0 / jnp.sum(weights, axis=-1, keepdims=True))).astype(BF)
                probs[(i * pairs + p) * 2 + e] = low
                total = total + mm(low, jnp.where(lanes, v, zero), ((1,), (0,)))
            context[:, pl.ds(pl.multiple_of(canonical * cols + p * 128, 128), 128)] = total.astype(BF)
            return carry

        lax.fori_loop(0, pairs, pair_step, 0)
    pack(context[...], given_2, maps, whole)
    second = list(zip(given_2, taken_2))
    send_all(second, send_2, recv_2)
    wait_all(second, send_2, recv_2)
    unpack(taken_2, maps, whole, gathered)


class Halving:
    def __init__(self, source, bufs, sends, recvs, order, out, window):
        self.source, self.bufs, self.sends, self.recvs = source, bufs, sends, recvs
        self.order, self.out, self.window = order, out, window
        self.stages = len(order)
        self.rows = bufs[0].shape[1]
        self.counts = [buf.shape[0] for buf in bufs]
        self.first = [k for stage, k in halving_plan(self.stages) if stage == 0]

    def bit(self, stage):
        return lax.rem(lax.div(lax.axis_index("dp"), 1 << self.order[stage]), 2)

    def block(self, k, kept):
        index = 0
        for stage in range(self.stages):
            mine = self.bit(stage)
            if stage == 0:
                value = mine if kept else 1 - mine
            else:
                part = lax.rem(lax.div(k, self.counts[stage]), 2)
                value = (1 - mine) * (1 - part) + mine * part
            index = index + value * (1 << self.order[stage])
        return pl.ds(pl.multiple_of(index * self.rows, 16), self.rows)

    def copy(self, stage, k):
        me, core = lax.axis_index("dp"), lax.axis_index("mp")
        to = me + (1 - 2 * self.bit(stage)) * (1 << self.order[stage])
        at = sum(self.counts[:stage]) + k
        src = self.source.at[self.block(k, False), :] if stage == 0 else self.bufs[stage - 1].at[k]
        return pltpu.make_async_remote_copy(
            src_ref=src,
            dst_ref=self.bufs[stage].at[k],
            send_sem=self.sends.at[at],
            recv_sem=self.recvs.at[at],
            device_id=(to, core),
            device_id_type=MESH,
        )

    def begin(self):
        for k in self.first[: self.window]:
            self.copy(0, k).start()

    def step(self, stage, k):
        self.copy(stage, k).wait_recv()
        buf = self.bufs[stage]
        if stage == 0:
            own = self.source[self.block(k, True), :]
        else:
            own = self.bufs[stage - 1][pl.ds(self.counts[stage] + k, 1)][0]
        total = own.astype(F32) + buf[pl.ds(k, 1)][0].astype(F32)
        if stage == self.stages - 1:
            self.out[...] = total
            return
        buf[pl.ds(k, 1)] = total.astype(BF)[None]
        if k < self.counts[stage + 1]:
            self.copy(stage + 1, k).start()
        if stage == 0:
            ahead = self.first.index(k) + self.window
            if ahead < len(self.first):
                self.copy(0, self.first[ahead]).start()

    def drain(self):
        for stage, count in enumerate(self.counts):

            def finish(k, carry, stage=stage):
                self.copy(stage, k).wait_send()
                return carry

            lax.fori_loop(0, count, finish, 0)


def halving_plan(stages):
    counts = [1 << (stages - 1 - stage) for stage in range(stages)]
    times = {}
    for stage, count in enumerate(counts):
        for k in range(count):
            if stage == 0:
                bits = [(k >> i) & 1 for i in range(stages - 1)]
                times[stage, k] = 1 + sum(bit << (stages - 2 - i) for i, bit in enumerate(bits))
            else:
                times[stage, k] = 1.6 + max(times[stage - 1, k], times[stage - 1, count + k])
    return sorted(times, key=lambda key: (times[key], key))


def advance(chains, steps):
    for stage, k in steps:
        for chain in chains:
            chain.step(stage, k)


def half_erfc(value, bell):
    t = 1.0 / (1.0 + (0.3275911 * 0.5**0.5) * jnp.abs(value))
    poly = 1.061405429 * t - 1.453152027
    poly = poly * t + 1.421413741
    poly = poly * t - 0.284496736
    poly = poly * t + 0.254829592
    return 0.5 * poly * t * bell


def row_sums(value):
    return jnp.sum(value.reshape(value.shape[0] // 8, 8, value.shape[1]), axis=0)


def back_kernel(
    whole, orders, maps, gate, vectors, routes, route_cols,
    gathered_in, wo_own, wo_other, x_in, ct_in, we_own, we_other, wr_own, wr_other,
    w_own, w_other, proj_in, probs_in, buffer_in,
    expand_out, reduce_out, late_out, layer_out, tokens_out, sums_out,
    gathered, wo, x, ct, w_vmem, proj, probs, buffer,
    we, wr, attended, mean, inv, hidden, hidden_t, ct_t, mlp, mixed_grad, pre, act_grad, act, pre_grad,
    logit_grad, attended_grad, upstream, proj_grad, layer_own, tokens_got,
    expand_give, reduce_give, expand_got, reduce_got, sums, sums_got, layer_stage, tokens_stage,
    load_sem, we_sem, wr_sem, out_sem, pair_send, pair_recv, sums_send, sums_recv, free_sem,
    send_1, recv_1, send_2, recv_2, *rest,
):
    dp, core = lax.axis_index("dp"), lax.axis_index("mp")
    peers = lax.axis_size("dp")
    width, columns = expand_give.shape
    slots = buffer.shape[0]
    count = x.shape[0]
    chunk = pre.shape[1]
    steps = columns // chunk
    cols = w_own.shape[2]
    pairs = cols // 128
    attend_cols = 3 * cols
    half = columns // 2
    step_rows = 32
    kept_steps, all_steps = slots // step_rows, count // step_rows
    ready = greet(peers, with_pair=True)
    gain, shift, router, gain_2, shift_2 = (vectors.at[pl.ds(i, 1), :] for i in range(5))

    def chunk_loads(n):
        j, slot = n // 2, n % 2
        here_e, here_r = (we_other, wr_other) if n % 2 == 0 else (we_own, wr_own)
        part = pl.ds(j * chunk, chunk)
        return (
            pltpu.make_async_copy(here_e.at[:, part], we.at[slot], we_sem.at[slot]),
            pltpu.make_async_copy(here_r.at[part, :], wr.at[slot], wr_sem.at[slot]),
        )

    local = [
        (gathered_in, gathered),
        (wo_own, wo.at[0]),
        (wo_other, wo.at[1]),
        (x_in, x),
        (ct_in, ct),
        (proj_in, proj),
        (probs_in, probs),
        (w_own, w_vmem.at[0]),
        (w_other, w_vmem.at[1]),
        (buffer_in, buffer),
    ]
    loads = [
        pltpu.make_async_copy(here, there, load_sem.at[i]) for i, (here, there) in enumerate(local)
    ]
    for load in (*loads[:5], *chunk_loads(0), *loads[5:]):
        load.start()

    kinds = 2 if whole else 1
    given_1, taken_1, given_2, taken_2 = split_blocks(rest[: 4 * kinds])
    rest = rest[4 * kinds :]
    late_give, late_got = reduce_give, expand_give
    chains = []
    plan = []
    if orders is not None:
        stages = len(orders[0])
        plan = halving_plan(stages)
        parts_of = []
        for j in range(steps):
            part = pl.ds(j * chunk, chunk)
            parts_of.append((expand_got.at[:, part], expand_out.at[:, part], orders[0], 8))
            parts_of.append((reduce_got.at[:, part], reduce_out.at[:, part], orders[1], 8))
        for j in range(2):
            part = pl.ds(j * half, half)
            parts_of.append((late_got.at[:, part], late_out.at[:, part], orders[j], 4))
        for i, (source, out, order, window) in enumerate(parts_of):
            mine = rest[i * (stages + 2) : (i + 1) * (stages + 2)]
            chains.append(Halving(source, mine[2:], mine[0], mine[1], order, out, window))
    done = [0] * (steps + 1)

    def run(group, number):
        if chains:
            advance(chains[2 * group : 2 * group + 2], plan[done[group] : done[group] + number])
            done[group] += number

    def begin(group):
        for chain in chains[2 * group : 2 * group + 2]:
            chain.begin()

    def pair_copy(at, give, got):
        return pltpu.make_async_remote_copy(
            src_ref=give,
            dst_ref=got,
            send_sem=pair_send.at[at],
            recv_sem=pair_recv.at[at],
            device_id=(dp, 1 - core),
            device_id_type=MESH,
        )

    def weight_copy(i, j):
        give, got = ((expand_give, expand_got), (reduce_give, reduce_got))[i]
        part = pl.ds(j * chunk, chunk)
        return pair_copy(i * steps + j, give.at[:, part], got.at[:, part])

    own_cols = pl.ds(pl.multiple_of(core * cols, 128), cols)
    other_cols = pl.ds(pl.multiple_of((1 - core) * cols, 128), cols)
    for load in loads[:3]:
        load.wait()
    attended[...] = mm(gathered[:, own_cols], wo[0], ((1,), (0,))) + mm(
        gathered[:, other_cols], wo[1], ((1,), (0,))
    )
    for load in loads[3:5]:
        load.wait()

    def rows_of(r):
        return pl.ds(pl.multiple_of(r * step_rows, step_rows), step_rows)

    def mixed_rows(rows, kept):
        value = x[rows, :].astype(F32)
        return value + gate[rows, :] * attended[rows, :] if kept else value

    def norm_rows(r, carry, kept):
        rows = rows_of(r)
        if kept:
            attended[rows, :] = jnp.where(route_cols[rows, 1:2] > 0.5, attended[rows, :], 0.0)
        value = mixed_rows(rows, kept)
        middle = jnp.mean(value, axis=-1, keepdims=True)
        center = value - middle
        scale = lax.rsqrt(jnp.mean(center * center, axis=-1, keepdims=True) + EPSILON)
        mean[rows, :] = middle
        inv[rows, :] = scale
        hidden[rows, :] = (center * scale * gain_2[...] + shift_2[...]).astype(BF)
        mlp[rows, :] = jnp.zeros((step_rows, width), F32)
        mixed_grad[rows, :] = jnp.zeros((step_rows, width), F32)
        return carry

    lax.fori_loop(0, kept_steps, functools.partial(norm_rows, kept=True), 0)
    lax.fori_loop(kept_steps, all_steps, functools.partial(norm_rows, kept=False), 0)
    hidden_t[...] = hidden[...].T
    ct_t[...] = ct[...].T

    def gelu_rows(r, carry):
        rows = pl.ds(pl.multiple_of(r * 16, 16), 16)
        value = pre[rows, :]
        bell = jnp.exp(-0.5 * value * value)
        tail = half_erfc(value, bell)
        phi = jnp.where(value < 0.0, tail, 1.0 - tail)
        act[rows, :] = (value * phi).astype(BF)
        slope = phi + value * bell * 0.3989422804014327
        pre_grad[rows, :] = (act_grad[rows, :] * slope).astype(BF)
        return carry

    for n in range(2 * steps):
        j, slot, is_own = n // 2, n % 2, n % 2 == 1
        part = pl.ds(j * chunk, chunk)
        for load in chunk_loads(n):
            load.wait()
        if n + 1 < 2 * steps:
            for load in chunk_loads(n + 1):
                load.start()

        def point(n=n, j=j, is_own=is_own):
            for group in range(j):
                run(group, 1)

        pre[...] = mm(hidden[...], we[slot], ((1,), (0,)))
        act_grad[...] = mm(ct[...], wr[slot], ((1,), (1,)))
        point()
        lax.fori_loop(0, count // 16, gelu_rows, 0, unroll=2)
        point()
        mlp[...] += mm(act[...], wr[slot], ((1,), (0,)))
        mixed_grad[...] += mm(pre_grad[...], we[slot], ((1,), (1,)))
        point()
        for i, (left, right, give, got) in enumerate(
            (
                (hidden_t, pre_grad, expand_give, expand_got),
                (ct_t, act, reduce_give, reduce_got),
            )
        ):
            value = mm(left[...], right[...], ((1,), (0,)))
            if is_own:
                weight_copy(i, j).wait_recv()
                got[:, part] = (value + got[:, part].astype(F32)).astype(BF)
            else:
                give[:, part] = value.astype(BF)
                if n == 0 and i == 0:
                    ready()
                weight_copy(i, j).start()
        point()
        if is_own:
            begin(j)

    def back_rows(r, carry, kept):
        rows = rows_of(r)
        mixed = mixed_rows(rows, kept)
        layer_own[rows, :] = (mixed + mlp[rows, :]).astype(BF)
        grad = mixed_grad[rows, :]
        scale = inv[rows, :]
        normal = (mixed - mean[rows, :]) * scale
        total = ct[rows, :].astype(F32) + norm_pull(grad * gain_2[...], normal, scale)
        mixed_grad[rows, :] = total
        if kept:
            open_by = gate[rows, :]
            attended_grad[rows, :] = jnp.where(route_cols[rows, 1:2] > 0.5, open_by * total, 0.0).astype(BF)
            logit_grad[rows, :] = (
                jnp.sum(total * attended[rows, :], axis=-1, keepdims=True) * open_by * (1.0 - open_by)
            )
        else:
            logit_grad[rows, :] = jnp.zeros((step_rows, 1), F32)
        return (carry[0] + row_sums(grad * normal), carry[1] + row_sums(grad))

    zeros = jnp.zeros((8, width), F32)
    carry = lax.fori_loop(0, kept_steps, functools.partial(back_rows, kept=True), (zeros, zeros))
    for group in range(steps - 1):
        run(group, 2)
    for at, w in ((own_cols, wo[0]), (other_cols, wo[1])):
        upstream[:, at] = mm(attended_grad[...], w, ((1,), (1,))).astype(BF)
    pack(upstream[...], given_1, maps, whole)
    first = list(zip(given_1, taken_1))
    send_all(first, send_1, recv_1)
    carry = lax.fori_loop(kept_steps, all_steps, functools.partial(back_rows, kept=False), carry)
    for i in range(2):
        sums[0, 3 + i : 4 + i, :] = jnp.sum(carry[i], axis=0, keepdims=True)
    sums[0, 5:8, :] = jnp.zeros((3, width), F32)

    for i in range(2):
        for j in range(steps):
            weight_copy(i, j).wait_send()
    pl.semaphore_signal(free_sem, inc=1, device_id=(dp, 1 - core), device_id_type=MESH)
    late_give[:, attend_cols:] = mm(
        attended_grad[...], gathered[:, other_cols], ((0,), (0,))
    ).astype(BF)
    output_own = mm(attended_grad[...], gathered[:, own_cols], ((0,), (0,)))
    pl.semaphore_wait(free_sem, 1)
    layer_copy = pair_copy(2 * steps + 3, layer_own, ct)
    layer_copy.start()
    output_copy, attend_copy = (
        pair_copy(2 * steps + i, late_give.at[:, part], late_got.at[:, part])
        for i, part in enumerate(
            (pl.ds(attend_cols, columns - attend_cols), pl.ds(0, attend_cols))
        )
    )
    output_copy.start()
    output_copy.wait_recv()
    late_got[:, attend_cols:] = (output_own + late_got[:, attend_cols:].astype(F32)).astype(BF)
    for group in range(steps - 1):
        run(group, 15)
    run(steps - 1, 2)

    wait_all(first, send_1, recv_1)
    unpack(taken_1, maps, whole, upstream)
    for load in loads[5:]:
        load.wait()
    masks = lane_masks()
    zero = jnp.zeros((), BF)
    for i in range(2):
        canonical = core if i == 0 else 1 - core

        def pair_step(p, carry, i=i, canonical=canonical):
            def place_of(which):
                return pl.ds(pl.multiple_of(which * cols + p * 128, 128), 128)

            q, k, v = (proj[i, :, place_of(which)] for which in range(3))
            up = upstream[:, place_of(canonical)]
            q_grad = k_grad = v_grad = 0.0
            for e, lanes in enumerate(masks):
                low = probs[(i * pairs + p) * 2 + e]
                wide = low.astype(F32)
                probs_grad = mm(up, jnp.where(lanes, v, zero), ((1,), (1,)))
                delta = jnp.sum(wide * probs_grad, axis=-1, keepdims=True)
                scores_grad = (wide * (probs_grad - delta)).astype(BF)
                v_grad = v_grad + mm(low, jnp.where(lanes, up, zero), ((0,), (0,)))
                q_grad = q_grad + mm(scores_grad, jnp.where(lanes, k, zero), ((1,), (0,)))
                k_grad = k_grad + mm(scores_grad, jnp.where(lanes, q, zero), ((0,), (0,)))
            proj_grad[i, :, place_of(0)] = (q_grad * HD ** (-0.5)).astype(BF)
            proj_grad[i, :, place_of(1)] = (k_grad * HD ** (-0.5)).astype(BF)
            proj_grad[i, :, place_of(2)] = v_grad.astype(BF)
            return carry

        lax.fori_loop(0, pairs, pair_step, 0)
        run(steps - 1, 2)
    upstream[...] = sum(
        mm(proj_grad[i, :, which * cols : (which + 1) * cols], w_vmem[i, which], ((1,), (1,)))
        for i in range(2)
        for which in range(3)
    ).astype(BF)
    pack(upstream[...], given_2, maps, whole)
    second = list(zip(given_2, taken_2))
    send_all(second, send_2, recv_2)

    def attend_at(which):
        return pl.ds(pl.multiple_of(which * cols, 128), cols)

    def late_other(which, carry):
        value = mm(buffer[...], proj_grad[1, :, attend_at(which)], ((0,), (0,)))
        late_give[:, attend_at(which)] = value.astype(BF)
        return carry

    def late_own(which, carry):
        value = mm(buffer[...], proj_grad[0, :, attend_at(which)], ((0,), (0,)))
        got = late_got[:, attend_at(which)].astype(F32)
        late_got[:, attend_at(which)] = (value + got).astype(BF)
        return carry

    lax.fori_loop(0, 3, late_other, 0)
    attend_copy.start()
    run(steps - 1, 2)
    attend_copy.wait_recv()
    lax.fori_loop(0, 3, late_own, 0)
    begin(steps)
    run(steps - 1, 4)

    wait_all(second, send_2, recv_2)
    unpack(taken_2, maps, whole, upstream)
    tokens_own = hidden

    def first_rows(r, carry, kept):
        rows = rows_of(r)
        normal, scale = norm_stats(x[rows, :].astype(F32))
        normed = (normal * gain[...] + shift[...]).astype(BF).astype(F32)
        logit = logit_grad[rows, :]
        grad = logit * router[...]
        if kept:
            grad = grad + jnp.where(route_cols[rows, 1:2] > 0.5, upstream[rows, :].astype(F32), 0.0)
        total = mixed_grad[rows, :] + norm_pull(grad * gain[...], normal, scale)
        tokens_own[rows, :] = total.astype(BF)
        return (
            carry[0] + row_sums(grad * normal),
            carry[1] + row_sums(grad),
            carry[2] + row_sums(logit * normed),
        )

    carry = (zeros, zeros, zeros)
    carry = lax.fori_loop(0, kept_steps, functools.partial(first_rows, kept=True), carry)
    carry = lax.fori_loop(kept_steps, all_steps, functools.partial(first_rows, kept=False), carry)
    tokens_copy = pair_copy(2 * steps + 2, tokens_own, tokens_got)
    tokens_copy.start()
    for i in range(3):
        sums[0, i : i + 1, :] = jnp.sum(carry[i], axis=0, keepdims=True)

    def sums_copy(stage):
        if stage < sums_got.shape[0] - 1:
            bit = lax.rem(lax.div(dp, 1 << stage), 2)
            to = (dp + (1 - 2 * bit) * (1 << stage), core)
        else:
            to = (dp, 1 - core)
        return pltpu.make_async_remote_copy(
            src_ref=sums.at[stage],
            dst_ref=sums_got.at[stage],
            send_sem=sums_send.at[stage],
            recv_sem=sums_recv.at[stage],
            device_id=to,
            device_id_type=MESH,
        )

    sums_stages = sums_got.shape[0]
    sums_copy(0).start()

    def sums_step(stage):
        sums_copy(stage).wait_recv()
        total = sums[stage] + sums_got[stage]
        if stage + 1 < sums_stages:
            sums[stage + 1] = total
            sums_copy(stage + 1).start()
        else:
            sums_out[...] = total

    def unpick(own, other, out, stage, sems):
        total = out.shape[0]
        block = stage.shape[1]
        full = total // block
        tail = total - full * block

        def out_copy(r, size):
            slot = lax.rem(r, 2)
            rows = pl.ds(pl.multiple_of(r * block, block), size)
            return pltpu.make_async_copy(
                stage.at[slot, pl.ds(0, size), :], out.at[rows, :], sems.at[slot]
            )

        def emit(r, size):
            rows = pl.ds(pl.multiple_of(r * block, block), size)
            hit = (route_cols[rows, 2:3] == routes[0:1, :]).astype(F32).astype(BF)
            value = mm(hit[:, :count], own[...], ((1,), (0,))) + mm(
                hit[:, count : 2 * count], other[...], ((1,), (0,))
            )
            stage[lax.rem(r, 2), pl.ds(0, size), :] = value.astype(out.dtype)
            out_copy(r, size).start()

        def body(r, carry):
            @pl.when(r >= 2)
            def _():
                out_copy(r - 2, block).wait()

            emit(r, block)
            return carry

        lax.fori_loop(0, full, body, 0)
        if tail:
            out_copy(full - 2, block).wait()
            emit(full, tail)
            out_copy(full - 1, block).wait()
            out_copy(full, tail).wait()
        else:
            out_copy(full - 2, block).wait()
            out_copy(full - 1, block).wait()

    run(steps - 1, 3)
    run(steps, 4)
    sums_step(0)
    layer_copy.wait_recv()
    unpick(layer_own, ct, layer_out, layer_stage, out_sem.at[0])
    sums_step(1)
    run(steps - 1, 15)
    run(steps, 2)
    sums_step(2)
    tokens_copy.wait_recv()
    unpick(tokens_own, tokens_got, tokens_out, tokens_stage, out_sem.at[1])
    sums_step(3)
    run(steps, 2)
    for stage in range(4, sums_stages):
        sums_step(stage)
    run(steps, 15)
    for chain in chains:
        chain.drain()
    if not chains:
        finals = [
            pltpu.make_async_copy(here, there, load_sem.at[i])
            for i, (here, there) in enumerate(
                ((expand_got, expand_out), (reduce_got, reduce_out), (late_got, late_out))
            )
        ]
        for final in finals:
            final.start()
        for final in finals:
            final.wait()
    for copy in (output_copy, attend_copy, layer_copy, tokens_copy):
        copy.wait_send()
    for stage in range(sums_stages):
        sums_copy(stage).wait_send()


def split_blocks(blocks):
    step = len(blocks) // 4
    return [blocks[i * step : (i + 1) * step] for i in range(4)]


def block_scratch(peers, whole, left, parts, width):
    shapes = [(peers, whole, width)] if whole else []
    shapes.append((peers, 16, width // parts))
    return [pltpu.VMEM(shape, BF) for _ in range(4) for shape in shapes], len(shapes)


def exchange_call(
    kernel, name, collective_id, capacity, width, args, spaces, outs, scratch, after=(), out_spaces=None
):
    peers = lax.axis_size("dp")
    whole, left, parts = block_plan(capacity, width)
    blocks, kinds = block_scratch(peers, whole, left, parts, width)
    return pl.pallas_call(
        functools.partial(kernel, whole),
        out_shape=[jax.ShapeDtypeStruct(*out) for out in outs],
        in_specs=[pl.BlockSpec(memory_space=space) for space in spaces],
        out_specs=[
            pl.BlockSpec(memory_space=space) for space in out_spaces or [pltpu.VMEM] * len(outs)
        ],
        scratch_shapes=[
            *scratch,
            *[pltpu.SemaphoreType.DMA((kinds, peers))] * 4,
            *blocks,
            *after,
        ],
        compiler_params=pltpu.CompilerParams(
            collective_id=collective_id, has_side_effects=True, vmem_limit_bytes=58 * 2**20
        ),
        name=name,
    )(*args)


def slot_layout(peers, capacity, whole, own, own_pad, total):
    left = capacity - whole
    spot = np.arange(total) % own_pad
    side = np.arange(total) // own_pad
    main = spot < peers * whole
    rest = spot - peers * whole
    device = np.where(main, spot // max(whole, 1), rest // left)
    slot = np.where(main, spot % max(whole, 1), whole + rest % left)
    is_slot = spot < peers * capacity
    rows = [
        np.where(is_slot, device, 0),
        np.where(is_slot, slot, 4 * capacity),
        np.where((spot < own) & (side < 2), spot, -1),
        np.minimum(side, 1),
    ]
    return jnp.asarray(np.stack(rows + [np.zeros(total)] * 4), jnp.int32)


def attend(info, vectors, maps, tokens, cotangent, w_own, w_other, capacity, own, own_pad):
    peers = lax.axis_size("dp")
    count, width = tokens.shape
    slots = peers * capacity
    cols = w_own.shape[2]
    heads = 2 * cols // HD
    total = info.shape[1]
    whole = block_plan(capacity, width)[0]
    layout = slot_layout(peers, capacity, whole, own, own_pad, total)
    vmem = pltpu.VMEM
    return exchange_call(
        lambda whole, *refs: attend_kernel(whole, capacity, *refs), "attend", 0, capacity, width,
        (info, layout, vectors, maps, tokens, cotangent, w_own, w_other),
        (vmem,) * 4 + (pl.ANY,) * 4,
        [
            ((slots, width), BF), ((slots, width), BF), ((2, slots, 3 * cols), BF),
            ((heads, slots, slots), BF), ((own_pad, width), BF), ((own_pad, width), BF),
            ((own_pad, 1), F32), ((8, total), F32), ((total, 8), F32),
        ],
        [
            vmem((count, width), BF), vmem((count, width), BF),
            vmem((total, 8), F32), vmem((8, total), F32),
            vmem((2, *w_own.shape), BF),
            vmem((slots, width), BF),
            vmem((8, slots), F32),
            pltpu.SemaphoreType.DMA((4,)),
        ],
    )


def back(small, large, probs, capacity, orders, place_rows):
    gathered, wo, _, x, ct, we, _, wr, _, w, _, proj, _, buffer = large
    slots, width = buffer.shape
    count, hidden = x.shape[0], we.shape[1]
    peers = lax.axis_size("dp")
    vmem, hbm = pltpu.VMEM, pl.ANY
    dma = pltpu.SemaphoreType.DMA
    chunk = 512 if hidden % 512 == 0 else hidden
    steps = hidden // chunk
    rows = width // peers
    after = []
    if orders is None:
        outs = [((width, hidden), BF)] * 3
        out_spaces = (hbm,) * 5 + (vmem,)
    else:
        outs = [((rows, hidden), F32)] * 3
        out_spaces = (vmem,) * 3 + (hbm,) * 2 + (vmem,)
        counts = [peers >> (stage + 1) for stage in range(len(orders[0]))]
        for size in [chunk] * (2 * steps) + [hidden // 2] * 2:
            after += [dma((sum(counts),))] * 2
            after += [vmem((n, rows, size), BF) for n in counts]
    outs += [((place_rows, width), BF), ((place_rows, width), F32), ((8, width), F32)]
    sums_stages = peers.bit_length()
    low = vmem((count, width), BF)
    wide = vmem((count, width), F32)
    turned = vmem((width, count), BF)
    column = vmem((count, 1), F32)
    slot_rows = vmem((slots, width), BF)
    gradient = vmem((width, hidden), BF)
    return exchange_call(
        lambda whole, *refs: back_kernel(whole, orders, *refs), "back", 1, capacity, width,
        (*small, *large),
        (vmem,) * len(small) + (hbm,) * len(large),
        outs,
        [
            slot_rows, vmem((2, *wo.shape), BF), low, low, vmem((2, *w.shape), BF),
            vmem(proj.shape, BF), vmem(probs.shape, BF), slot_rows,
            vmem((2, width, chunk), BF), vmem((2, chunk, width), BF),
            vmem((slots, width), F32), column, column, low, turned, turned, wide, wide,
            vmem((count, chunk), F32), vmem((count, chunk), F32),
            vmem((count, chunk), BF), vmem((count, chunk), BF),
            column, slot_rows, slot_rows, vmem(proj.shape, BF), low, low,
            gradient, gradient, gradient, gradient,
            vmem((sums_stages, 8, width), F32), vmem((sums_stages, 8, width), F32),
            vmem((2, 128, width), BF), vmem((2, 128, width), F32),
            dma((10,)), dma((2,)), dma((2,)), dma((2, 2)),
            dma((2 * steps + 4,)), dma((2 * steps + 4,)), dma((sums_stages,)), dma((sums_stages,)),
            pltpu.SemaphoreType.REGULAR,
        ],
        after,
        out_spaces,
    )


def shards(
    tokens,
    row_ids,
    select,
    priority,
    first_gain,
    first_shift,
    router,
    w_attend,
    w_output,
    second_gain,
    second_shift,
    w_expand,
    w_reduce,
    cotangent,
):
    dp_count = lax.axis_size("dp")
    mp_count = lax.axis_size("mp")
    core = lax.axis_index("mp")
    bits = dp_count.bit_length() - 1
    order_a = list(range(bits))
    order_b = [1, 0] + list(range(bits - 1, 1, -1))
    capacity = 5 * ROW_LEN // (8 * dp_count)
    count, width = tokens.shape
    own = count // mp_count
    own_pad = -(-own // 128) * 128
    heads_cols = w_attend.shape[2]
    whole, left, parts = block_plan(capacity, width)
    maps = rest_map(dp_count, left, parts)

    w_attend = w_attend.transpose(1, 0, 2)
    w_attend_2 = (w_attend, swap(w_attend))
    w_output_2 = (w_output, swap(w_output))
    w_expand_2 = (w_expand, swap(w_expand))
    w_reduce_2 = (w_reduce, swap(w_reduce))

    total = max(-(-count // 128) * 128, mp_count * own_pad)
    info = jnp.pad(jnp.stack([row_ids, select, priority]), ((0, 5), (0, total - count)))
    vectors = jnp.pad(
        jnp.stack([first_gain, first_shift, router, second_gain, second_shift]), ((0, 3), (0, 0))
    )
    gathered, buffer, proj, probs, x, ct, gate, routes, route_cols = attend(
        info, vectors, maps, tokens, cotangent, *w_attend_2, capacity, own, own_pad
    )
    orders = (order_a, order_b) if width // dp_count % 16 == 0 else None
    expand_sum, reduce_sum, late_sum, layer_out, tokens_grad, vectors = back(
        (maps, gate, vectors, routes, route_cols),
        (gathered, *w_output_2, x, ct, *w_expand_2, *w_reduce_2, *w_attend_2, proj, probs, buffer),
        probs, capacity, orders, -(-count // 16) * 16,
    )
    if orders is None:
        expand_sum = scatter_sum(expand_sum, order_a)
        reduce_sum = scatter_sum(reduce_sum, order_b)
        late_sum = scatter_sum(late_sum, order_a)
    rows_here = width // dp_count
    vectors = lax.dynamic_slice_in_dim(vectors, lax.axis_index("dp") * rows_here, rows_here, 1)

    attend_cols = 3 * heads_cols
    return (
        layer_out[:count],
        tokens_grad[:count],
        vectors[0],
        vectors[1],
        vectors[2],
        late_sum[:, :attend_cols].reshape(-1, 3, heads_cols),
        late_sum[:, attend_cols:].T,
        vectors[3],
        vectors[4],
        expand_sum,
        reduce_sum.T,
    )


def solution(mesh):
    in_specs = (
        P("dp", None),
        P("dp"),
        P("dp"),
        P("dp"),
        P(),
        P(),
        P(),
        P(None, None, "mp"),
        P("mp", None),
        P(),
        P(),
        P(None, "mp"),
        P("mp", None),
        P("dp", None),
    )
    out_specs = (
        P("dp", None),
        P("dp", None),
        P("dp"),
        P("dp"),
        P("dp"),
        P("dp", None, "mp"),
        P("mp", "dp"),
        P("dp"),
        P("dp"),
        P("dp", "mp"),
        P("mp", "dp"),
    )
    return jax.shard_map(shards, mesh=mesh, in_specs=in_specs, out_specs=out_specs, check_vma=False)
```

```python
import functools

import jax
import jax.numpy as jnp
import numpy as np
from jax import lax
from jax.experimental import pallas as pl
from jax.experimental.pallas import tpu as pltpu
from jax.sharding import PartitionSpec as P

HD = 64
ROW_LEN = 577
EPSILON = 1e-06
MASKED_SCORE = -1000000000.0
EMPTY = 1e30
BF = jnp.bfloat16
F32 = jnp.float32
MESH = pl.DeviceIdType.MESH


def mm(a, b, dims):
    return lax.dot_general(a, b, (dims, ((), ())), preferred_element_type=F32)


def norm_stats(value):
    center = value - jnp.mean(value, axis=-1, keepdims=True)
    inv = lax.rsqrt(jnp.mean(center * center, axis=-1, keepdims=True) + EPSILON)
    return center * inv, inv


def norm_pull(e, nhat, inv):
    return (e - jnp.mean(e, axis=-1, keepdims=True) - nhat * jnp.mean(e * nhat, axis=-1, keepdims=True)) * inv


def swap(value):
    return lax.ppermute(value, "mp", [(0, 1), (1, 0)])


def scatter_sum(grad, order):
    count = lax.axis_size("dp")
    me = lax.axis_index("dp")
    bits = count.bit_length() - 1
    width = grad.shape[0] // count
    dims = [2] * bits
    value = grad.reshape(dims + [width, grad.shape[1]])
    out = None
    for step in order:
        axis = bits - 1 - step
        mine = (me >> step) & 1
        give = lax.dynamic_slice_in_dim(value, 1 - mine, 1, axis)
        keep = lax.dynamic_slice_in_dim(value, mine, 1, axis)
        got = lax.ppermute(give, "dp", [(i, i ^ (1 << step)) for i in range(count)])
        out = keep.astype(F32) + got.astype(F32)
        value = out.astype(grad.dtype)
    return out.reshape(width, grad.shape[1])


def block_plan(capacity, width):
    whole = capacity // 16 * 16
    left = capacity - whole
    parts = max(s for s in (1, 2, 3, 6) if left * s <= 16 and width % (128 * s) == 0)
    return whole, left, parts


def rest_map(peers, left, parts):
    at = jnp.arange(peers * 16)[None, :, None]
    row = jnp.arange(peers * left)[None, None, :]
    part = jnp.arange(parts)[:, None, None]
    return ((at // 16 == row // left) & (at % 16 == part * left + row % left)).astype(BF)


def greet(peers, with_pair=False):
    me, core = lax.axis_index("dp"), lax.axis_index("mp")
    barrier = pltpu.get_barrier_semaphore()

    def hello(d, carry):
        pl.semaphore_signal(
            barrier, inc=1, device_id=(lax.rem(me + d, peers), core), device_id_type=MESH
        )
        return carry

    lax.fori_loop(1, peers, hello, 0)
    if with_pair:
        pl.semaphore_signal(barrier, inc=1, device_id=(me, 1 - core), device_id_type=MESH)
    return lambda: pl.semaphore_wait(barrier, peers if with_pair else peers - 1)


def pack(value, blocks, maps, whole):
    rest = blocks[-1]
    peers, lanes = rest.shape[0], rest.shape[2]
    if whole:
        blocks[0][...] = value[: peers * whole].reshape(peers, whole, value.shape[1])
    tail = value[peers * whole :]
    total = sum(
        mm(maps[i], tail[:, i * lanes : (i + 1) * lanes], ((1,), (0,)))
        for i in range(maps.shape[0])
    )
    rest[...] = total.astype(BF).reshape(peers, 16, lanes)


def unpack(blocks, maps, whole, out):
    rest = blocks[-1]
    peers, lanes = rest.shape[0], rest.shape[2]
    if whole:
        out[: peers * whole, :] = blocks[0][...].reshape(peers * whole, out.shape[1])
    left = rest[...].reshape(peers * 16, lanes)
    for i in range(maps.shape[0]):
        out[peers * whole :, i * lanes : (i + 1) * lanes] = mm(
            maps[i], left, ((0,), (0,))
        ).astype(BF)


def copies(d, pairs, sends, recvs, back=False):
    me, core = lax.axis_index("dp"), lax.axis_index("mp")
    peers = pairs[0][0].shape[0]
    to, source = lax.rem(me + d, peers), lax.rem(me + peers - d, peers)
    return [
        pltpu.make_async_remote_copy(
            src_ref=here.at[to],
            dst_ref=there.at[source if back else me],
            send_sem=sends.at[i, d],
            recv_sem=recvs.at[i, d],
            device_id=(to, core),
            device_id_type=MESH,
        )
        for i, (here, there) in enumerate(pairs)
    ]


def send_all(pairs, sends, recvs):
    me = lax.axis_index("dp")

    def start(d, carry):
        for copy in copies(d, pairs, sends, recvs):
            copy.start()
        return carry

    lax.fori_loop(1, pairs[0][0].shape[0], start, 0)
    for here, there in pairs:
        there[pl.ds(me, 1)] = here[pl.ds(me, 1)]


def wait_all(pairs, sends, recvs):
    def finish(d, carry):
        for copy in copies(d, pairs, sends, recvs, back=True):
            copy.wait_recv()
        return carry

    def drain(d, carry):
        for copy in copies(d, pairs, sends, recvs):
            copy.wait_send()
        return carry

    lax.fori_loop(1, pairs[0][0].shape[0], finish, 0)
    lax.fori_loop(1, pairs[0][0].shape[0], drain, 0)


def lane_masks():
    low = lax.broadcasted_iota(jnp.int32, (1, 128), 1) < HD
    return low, jnp.logical_not(low)


def routing(info, layout, capacity, count, wide_cols, hit_rows, routes, route_cols):
    core = lax.axis_index("mp").astype(F32)
    cores = lax.axis_size("mp")
    total = info.shape[1]
    blocks = total // 128
    row, chosen, priority = (info[i : i + 1, :].astype(F32) for i in range(3))
    device, slot, spot, side = (layout[i : i + 1, :].astype(F32) for i in range(4))
    core_of = core + side * (1.0 - 2.0 * core)
    row_of = device * cores + core_of
    spot_of = jnp.where(spot >= 0.0, core_of * total + spot, -1.0)
    low = row * 2048.0
    key = low + priority
    picked = chosen > 0.5
    hit_rows[...] = jnp.zeros(hit_rows.shape, F32)
    hit_rows[0:1, :] = jnp.where(picked, key, -1.0)
    hit_rows[1:2, :] = jnp.where(picked, row, -1.0)
    wide_cols[...] = hit_rows[...].T

    def fold(hit):
        return jnp.sum(jnp.where(hit, 1.0, 0.0).reshape(16, 8, total), axis=0)

    def count_rows(b, carry):
        at = pl.ds(pl.multiple_of(b * 128, 128), 128)
        keys, rows = wide_cols[at, 0:1], wide_cols[at, 1:2]
        return (
            carry[0] + fold((keys >= low) & (keys < key)),
            carry[1] + fold(rows == row_of),
        )

    zeros = jnp.zeros((8, total), F32)
    ranks, sizes = lax.fori_loop(0, blocks, count_rows, (zeros, zeros))
    rank = jnp.sum(ranks, axis=0, keepdims=True)
    size = jnp.sum(sizes, axis=0, keepdims=True)
    kept = picked & (rank < capacity)
    filled = slot < jnp.minimum(size, float(capacity))
    index = lax.broadcasted_iota(jnp.int32, (1, total), 1).astype(F32)
    rest = (index < count) & jnp.logical_not(kept)
    free = (spot_of >= 0.0) & jnp.logical_not(filled)
    hit_rows[0:1, :] = jnp.where(rest, index, 1e9)
    hit_rows[1:2, :] = jnp.where(free, spot_of, 1e9)
    wide_cols[...] = hit_rows[...].T

    def count_rest(b, carry):
        at = pl.ds(pl.multiple_of(b * 128, 128), 128)
        return (
            carry[0] + fold(wide_cols[at, 0:1] < index),
            carry[1] + fold(wide_cols[at, 1:2] < spot_of),
        )

    before, ahead = lax.fori_loop(0, blocks, count_rest, (zeros, zeros))
    base = float(lax.axis_size("dp") * cores * capacity)
    before = base + jnp.sum(before, axis=0, keepdims=True)
    ahead = base + jnp.sum(ahead, axis=0, keepdims=True)
    routes[...] = jnp.zeros(routes.shape, F32)
    routes[0:1, :] = jnp.where(
        filled, row_of * capacity + slot, jnp.where(spot_of >= 0.0, ahead, -1.0)
    )
    routes[1:2, :] = jnp.where(filled, 1.0, 0.0)
    routes[2:3, :] = jnp.where(kept, row * capacity + rank, jnp.where(rest, before, -2.0))
    route_cols[...] = routes[...].T


def each_rows(body, first, last, carry, **kept):
    for r in range(first, last):
        carry = body(r, carry, **kept)
    return carry


def attend_kernel(
    whole, capacity, row_ids, select, priority, first_gain, first_shift, router_in, second_gain, second_shift,
    layout, maps, tokens_in, cotangent_in, w_own, wo_own, we_own, wr_own,
    gathered, gate, routes, route_cols, vectors, buffer_out, proj_out, probs_out, x_out, ct_out,
    w_out, wo_out, we_out, wr_out,
    buffer, proj, probs, x, ct, swap_send, swap_recv, out_sem, tokens, cotangent, info, wide_cols, hit_rows,
    w_vmem, context, key_mask, w_sem, send_1, recv_1, send_2, recv_2, *blocks,
):
    core = lax.axis_index("mp")
    loads = [
        pltpu.make_async_copy(here, there, w_sem.at[i])
        for i, (here, there) in enumerate(
            (
                (tokens_in, tokens),
                (cotangent_in, cotangent),
                (w_own, w_vmem.at[0]),
            )
        )
    ]
    for load in loads:
        load.start()
    given_1, taken_1, given_2, taken_2 = split_blocks(blocks)
    ready = greet(given_1[-1].shape[0], with_pair=True)
    swaps = [
        pltpu.make_async_remote_copy(
            src_ref=here,
            dst_ref=there,
            send_sem=swap_send.at[i],
            recv_sem=swap_recv.at[i],
            device_id=(lax.axis_index("dp"), 1 - core),
            device_id_type=MESH,
        )
        for i, (here, there) in enumerate(
            ((w_own, w_vmem.at[1]), (wo_own, wo_out), (we_own, we_out), (wr_own, wr_out))
        )
    ]
    leaving = [
        pltpu.make_async_copy(here, there, out_sem.at[i])
        for i, (here, there) in enumerate(
            (
                (x, x_out),
                (ct, ct_out),
                (buffer, buffer_out),
                (proj, proj_out),
                (probs, probs_out),
                (w_vmem.at[1], w_out),
            )
        )
    ]
    count, width = tokens.shape
    slots = buffer.shape[0]
    total_rows = x.shape[0]
    info[...] = jnp.zeros(info.shape, jnp.int32)
    for i, source in enumerate((row_ids, select, priority)):
        info[i : i + 1, :count] = source[...].reshape(1, count)
    vectors[...] = jnp.zeros(vectors.shape, F32)
    for i, source in enumerate((first_gain, first_shift, router_in, second_gain, second_shift)):
        vectors[i : i + 1, :] = source[...].reshape(1, width)
    routing(info, layout, capacity, count, wide_cols, hit_rows, routes, route_cols)
    ready()
    swaps[0].start()
    loads[0].wait()

    def pick(r, source, out):
        at = pl.ds(pl.multiple_of(r * 128, 128), 128)
        hit = (route_cols[at, 0:1] == routes[2:3, :count]).astype(F32).astype(BF)
        out[at, :] = mm(hit, source[...], ((1,), (0,))).astype(BF)

    def norm_rows(r, carry, sent):
        at = pl.ds(pl.multiple_of(r * 32, 32), 32)
        normal, _ = norm_stats(x[at, :].astype(F32))
        normed = (normal * vectors[0:1, :] + vectors[1:2, :]).astype(BF)
        wide = normed.astype(F32)
        gate[at, :] = jax.nn.sigmoid(jnp.sum(wide * vectors[2:3, :], axis=-1, keepdims=True))
        if sent:
            context[at, :] = jnp.where(route_cols[at, 1:2] > 0.5, wide, EMPTY).astype(BF)
        return carry

    def picks(first, last, source, out):
        def body(r, carry):
            pick(r, source, out)
            return carry

        lax.fori_loop(first, last, body, 0)

    kept_blocks = -(-slots // 128)
    picks(0, kept_blocks, tokens, x)
    each_rows(norm_rows, 0, slots // 32, 0, sent=True)
    pack(context[...], given_1, maps, whole)
    first = list(zip(given_1, taken_1))
    send_all(first, send_1, recv_1)
    for copy in swaps[1:]:
        copy.start()
    picks(kept_blocks, total_rows // 128, tokens, x)
    each_rows(norm_rows, slots // 32, total_rows // 32, 0, sent=False)
    loads[1].wait()
    picks(0, total_rows // 128, cotangent, ct)
    leaving[0].start()
    leaving[1].start()
    swaps[0].wait_recv()
    leaving[5].start()
    wait_all(first, send_1, recv_1)
    unpack(taken_1, maps, whole, buffer)
    lane = (lax.broadcasted_iota(jnp.int32, (8, 128), 1) == 0).astype(F32).astype(BF)
    key_mask[...] = jnp.where(
        mm(lane, buffer[:, :128], ((1,), (1,))) < 0.5 * EMPTY, 1.0, 0.0
    )
    received = buffer[...].astype(F32)
    buffer[...] = jnp.where(received[:, :1] < 0.5 * EMPTY, received, 0.0).astype(BF)
    cols = w_own.shape[2]
    pairs = cols // 128
    masks = lane_masks()
    zero = jnp.zeros((), BF)
    for i in range(2):
        if i == 0:
            loads[2].wait()
        for which in range(3):
            proj[i, :, which * cols : (which + 1) * cols] = mm(
                buffer[...], w_vmem[i, which], ((1,), (0,))
            ).astype(BF)
        canonical = core if i == 0 else 1 - core

        def pair_step(p, carry, i=i, canonical=canonical):
            def part(which):
                return proj[i, :, pl.ds(pl.multiple_of(which * cols + p * 128, 128), 128)]

            q, k, v = part(0), part(1), part(2)
            total = 0.0
            for e, lanes in enumerate(masks):
                scores = mm(q, jnp.where(lanes, k, zero), ((1,), (1,))) * HD ** (-0.5)
                scores = jnp.where(key_mask[:1, :] > 0.5, scores, MASKED_SCORE)
                weights = jnp.exp(scores - jnp.max(scores, axis=-1, keepdims=True))
                low = (weights * (1.0 / jnp.sum(weights, axis=-1, keepdims=True))).astype(BF)
                probs[(i * pairs + p) * 2 + e] = low
                total = total + mm(low, jnp.where(lanes, v, zero), ((1,), (0,)))
            context[:, pl.ds(pl.multiple_of(canonical * cols + p * 128, 128), 128)] = total.astype(BF)
            return carry

        lax.fori_loop(0, pairs, pair_step, 0)
    pack(context[...], given_2, maps, whole)
    second = list(zip(given_2, taken_2))
    send_all(second, send_2, recv_2)
    for copy in leaving[2:5]:
        copy.start()
    wait_all(second, send_2, recv_2)
    unpack(taken_2, maps, whole, gathered)
    for copy in leaving:
        copy.wait()
    for copy in swaps[1:]:
        copy.wait_recv()
    for copy in swaps:
        copy.wait_send()


class Halving:
    def __init__(self, source, bufs, sends, recvs, order, out, window):
        self.source, self.bufs, self.sends, self.recvs = source, bufs, sends, recvs
        self.order, self.out, self.window = order, out, window
        self.stages = len(order)
        self.rows = bufs[0].shape[1]
        self.counts = [buf.shape[0] for buf in bufs]
        self.first = [k for stage, k in halving_plan(self.stages) if stage == 0]

    def bit(self, stage):
        return lax.rem(lax.div(lax.axis_index("dp"), 1 << self.order[stage]), 2)

    def block(self, k, kept):
        index = 0
        for stage in range(self.stages):
            mine = self.bit(stage)
            if stage == 0:
                value = mine if kept else 1 - mine
            else:
                part = lax.rem(lax.div(k, self.counts[stage]), 2)
                value = (1 - mine) * (1 - part) + mine * part
            index = index + value * (1 << self.order[stage])
        return pl.ds(pl.multiple_of(index * self.rows, 16), self.rows)

    def copy(self, stage, k):
        me, core = lax.axis_index("dp"), lax.axis_index("mp")
        to = me + (1 - 2 * self.bit(stage)) * (1 << self.order[stage])
        at = sum(self.counts[:stage]) + k
        src = self.source.at[self.block(k, False), :] if stage == 0 else self.bufs[stage - 1].at[k]
        return pltpu.make_async_remote_copy(
            src_ref=src,
            dst_ref=self.bufs[stage].at[k],
            send_sem=self.sends.at[at],
            recv_sem=self.recvs.at[at],
            device_id=(to, core),
            device_id_type=MESH,
        )

    def begin(self):
        for k in self.first[: self.window]:
            self.copy(0, k).start()

    def step(self, stage, k):
        self.copy(stage, k).wait_recv()
        buf = self.bufs[stage]
        if stage == 0:
            own = self.source[self.block(k, True), :]
        else:
            own = self.bufs[stage - 1][pl.ds(self.counts[stage] + k, 1)][0]
        total = own.astype(F32) + buf[pl.ds(k, 1)][0].astype(F32)
        if stage == self.stages - 1:
            self.out[...] = total
            return
        buf[pl.ds(k, 1)] = total.astype(BF)[None]
        if k < self.counts[stage + 1]:
            self.copy(stage + 1, k).start()
        if stage == 0:
            ahead = self.first.index(k) + self.window
            if ahead < len(self.first):
                self.copy(0, self.first[ahead]).start()

    def drain(self):
        for stage, count in enumerate(self.counts):

            def finish(k, carry, stage=stage):
                self.copy(stage, k).wait_send()
                return carry

            lax.fori_loop(0, count, finish, 0)


def halving_plan(stages):
    counts = [1 << (stages - 1 - stage) for stage in range(stages)]
    times = {}
    for stage, count in enumerate(counts):
        for k in range(count):
            if stage == 0:
                bits = [(k >> i) & 1 for i in range(stages - 1)]
                times[stage, k] = 1 + sum(bit << (stages - 2 - i) for i, bit in enumerate(bits))
            else:
                times[stage, k] = 1.6 + max(times[stage - 1, k], times[stage - 1, count + k])
    return sorted(times, key=lambda key: (times[key], key))


def advance(chains, steps):
    for stage, k in steps:
        for chain in chains:
            chain.step(stage, k)


def half_erfc(value, bell):
    t = 1.0 / (1.0 + (0.3275911 * 0.5**0.5) * jnp.abs(value))
    poly = 1.061405429 * t - 1.453152027
    poly = poly * t + 1.421413741
    poly = poly * t - 0.284496736
    poly = poly * t + 0.254829592
    return 0.5 * poly * t * bell


def row_sums(value):
    return jnp.sum(value.reshape(value.shape[0] // 8, 8, value.shape[1]), axis=0)


def back_kernel(
    whole, orders, maps, gate, vectors, routes, route_cols,
    gathered_in, wo_own, wo_other, x_in, ct_in, we_own, we_other, wr_own, wr_other,
    w_own, w_other, proj_in, probs_in, buffer_in,
    expand_out, reduce_out, late_out, output_out, layer_out, tokens_out, sums_out,
    gathered, wo, x, ct, w_vmem, proj, probs, buffer,
    we, wr, attended, mean, inv, hidden, hidden_t, ct_t, mlp, mixed_grad, pre, act_grad, act, pre_grad,
    logit_grad, attended_grad, upstream, proj_grad, layer_own, tokens_got,
    expand_give, reduce_give, expand_got, reduce_got, sums, sums_got, sums_parts,
    load_sem, we_sem, wr_sem, out_sem, pair_send, pair_recv, sums_send, sums_recv, free_sem,
    send_1, recv_1, send_2, recv_2, *rest,
):
    dp, core = lax.axis_index("dp"), lax.axis_index("mp")
    peers = lax.axis_size("dp")
    width, columns = expand_give.shape
    slots = buffer.shape[0]
    count = x.shape[0]
    chunk = pre.shape[1]
    steps = columns // chunk
    cols = w_own.shape[2]
    pairs = cols // 128
    attend_cols = 3 * cols
    left_cols = -(-attend_cols // 256) * 128
    halves = ((0, left_cols), (left_cols, attend_cols - left_cols))
    step_rows = 32
    kept_steps, all_steps = slots // step_rows, count // step_rows
    ready = greet(peers, with_pair=True)
    gain, shift, router, gain_2, shift_2 = (vectors.at[pl.ds(i, 1), :] for i in range(5))

    def chunk_loads(n):
        j, slot = n // 2, n % 2
        here_e, here_r = (we_other, wr_other) if n % 2 == 0 else (we_own, wr_own)
        part = pl.ds(j * chunk, chunk)
        return (
            pltpu.make_async_copy(here_e.at[:, part], we.at[slot], we_sem.at[slot]),
            pltpu.make_async_copy(here_r.at[part, :], wr.at[slot], wr_sem.at[slot]),
        )

    local = [
        (gathered_in, gathered),
        (wo_own, wo.at[0]),
        (wo_other, wo.at[1]),
        (x_in, x),
        (ct_in, ct),
        (proj_in, proj),
        (probs_in, probs),
        (w_own, w_vmem.at[0]),
        (w_other, w_vmem.at[1]),
        (buffer_in, buffer),
    ]
    loads = [
        pltpu.make_async_copy(here, there, load_sem.at[i]) for i, (here, there) in enumerate(local)
    ]
    for load in (*loads[:5], *chunk_loads(0), *loads[5:]):
        load.start()

    kinds = 2 if whole else 1
    given_1, taken_1, given_2, taken_2 = split_blocks(rest[: 4 * kinds])
    rest = rest[4 * kinds :]
    late_give, late_got = reduce_give, expand_give
    chains = []
    plan = []
    if orders is not None:
        stages = len(orders[0])
        plan = halving_plan(stages)
        parts_of = []
        for j in range(steps):
            part = pl.ds(j * chunk, chunk)
            parts_of.append((expand_got.at[:, part], expand_out.at[:, part], orders[0], 4))
            parts_of.append((reduce_got.at[:, part], reduce_out.at[:, part], orders[1], 4))
        groups = [[2 * j, 2 * j + 1] for j in range(steps)] + [[2 * steps], [2 * steps + 1, 2 * steps + 2]]
        output_part = pl.ds(attend_cols, columns - attend_cols)
        parts_of.append((late_got.at[:, output_part], output_out, orders[0], 8))
        for j, (first_col, size) in enumerate(halves):
            part = pl.ds(first_col, size)
            parts_of.append((late_got.at[:, part], late_out.at[:, part], orders[j], 4))
        for i, (source, out, order, window) in enumerate(parts_of):
            mine = rest[i * (stages + 2) : (i + 1) * (stages + 2)]
            chains.append(Halving(source, mine[2:], mine[0], mine[1], order, out, window))
    done = [0] * (steps + 2)

    def run(group, number):
        if chains:
            advance([chains[i] for i in groups[group]], plan[done[group] : done[group] + number])
            done[group] += number

    def begin(group):
        if chains:
            for i in groups[group]:
                chains[i].begin()

    def pair_copy(at, give, got):
        return pltpu.make_async_remote_copy(
            src_ref=give,
            dst_ref=got,
            send_sem=pair_send.at[at],
            recv_sem=pair_recv.at[at],
            device_id=(dp, 1 - core),
            device_id_type=MESH,
        )

    def weight_copy(i, j):
        give, got = ((expand_give, expand_got), (reduce_give, reduce_got))[i]
        part = pl.ds(j * chunk, chunk)
        return pair_copy(i * steps + j, give.at[:, part], got.at[:, part])

    own_cols = pl.ds(pl.multiple_of(core * cols, 128), cols)
    other_cols = pl.ds(pl.multiple_of((1 - core) * cols, 128), cols)
    for load in loads[:3]:
        load.wait()
    attended[...] = mm(gathered[:, own_cols], wo[0], ((1,), (0,))) + mm(
        gathered[:, other_cols], wo[1], ((1,), (0,))
    )
    for load in loads[3:5]:
        load.wait()

    def rows_of(r):
        return pl.ds(pl.multiple_of(r * step_rows, step_rows), step_rows)

    def mixed_rows(rows, kept):
        value = x[rows, :].astype(F32)
        return value + gate[rows, :] * attended[rows, :] if kept else value

    def norm_rows(r, carry, kept):
        rows = rows_of(r)
        if kept:
            attended[rows, :] = jnp.where(route_cols[rows, 1:2] > 0.5, attended[rows, :], 0.0)
        value = mixed_rows(rows, kept)
        middle = jnp.mean(value, axis=-1, keepdims=True)
        center = value - middle
        scale = lax.rsqrt(jnp.mean(center * center, axis=-1, keepdims=True) + EPSILON)
        mean[rows, :] = middle
        inv[rows, :] = scale
        hidden[rows, :] = (center * scale * gain_2[...] + shift_2[...]).astype(BF)
        mlp[rows, :] = jnp.zeros((step_rows, width), F32)
        mixed_grad[rows, :] = jnp.zeros((step_rows, width), F32)
        return carry

    each_rows(norm_rows, 0, kept_steps, 0, kept=True)
    each_rows(norm_rows, kept_steps, all_steps, 0, kept=False)
    hidden_t[...] = hidden[...].T
    ct_t[...] = ct[...].T

    def gelu_rows(r, carry):
        rows = pl.ds(pl.multiple_of(r * 16, 16), 16)
        value = pre[rows, :]
        bell = jnp.exp(-0.5 * value * value)
        tail = half_erfc(value, bell)
        phi = jnp.where(value < 0.0, tail, 1.0 - tail)
        act[rows, :] = (value * phi).astype(BF)
        slope = phi + value * bell * 0.3989422804014327
        pre_grad[rows, :] = (act_grad[rows, :] * slope).astype(BF)
        return carry

    for n in range(2 * steps):
        j, slot, is_own = n // 2, n % 2, n % 2 == 1
        part = pl.ds(j * chunk, chunk)
        for load in chunk_loads(n):
            load.wait()
        if n + 1 < 2 * steps:
            for load in chunk_loads(n + 1):
                load.start()

        def point(n=n, j=j, is_own=is_own):
            for group in range(j):
                run(group, 1)

        pre[...] = mm(hidden[...], we[slot], ((1,), (0,)))
        act_grad[...] = mm(ct[...], wr[slot], ((1,), (1,)))
        point()
        lax.fori_loop(0, count // 16, gelu_rows, 0, unroll=2)
        point()
        mlp[...] += mm(act[...], wr[slot], ((1,), (0,)))
        mixed_grad[...] += mm(pre_grad[...], we[slot], ((1,), (1,)))
        point()
        for i, (left, right, give, got) in enumerate(
            (
                (hidden_t, pre_grad, expand_give, expand_got),
                (ct_t, act, reduce_give, reduce_got),
            )
        ):
            value = mm(left[...], right[...], ((1,), (0,)))
            if is_own:
                weight_copy(i, j).wait_recv()
                got[:, part] = (value + got[:, part].astype(F32)).astype(BF)
            else:
                give[:, part] = value.astype(BF)
                if n == 0 and i == 0:
                    ready()
                weight_copy(i, j).start()
        point()
        if is_own and j < steps - 1:
            begin(j)

    def back_rows(r, carry, kept):
        rows = rows_of(r)
        mixed = mixed_rows(rows, kept)
        layer_own[rows, :] = (mixed + mlp[rows, :]).astype(BF)
        grad = mixed_grad[rows, :]
        scale = inv[rows, :]
        normal = (mixed - mean[rows, :]) * scale
        total = ct[rows, :].astype(F32) + norm_pull(grad * gain_2[...], normal, scale)
        mixed_grad[rows, :] = total
        if kept:
            open_by = gate[rows, :]
            attended_grad[rows, :] = jnp.where(route_cols[rows, 1:2] > 0.5, open_by * total, 0.0).astype(BF)
            logit_grad[rows, :] = (
                jnp.sum(total * attended[rows, :], axis=-1, keepdims=True) * open_by * (1.0 - open_by)
            )
        else:
            logit_grad[rows, :] = jnp.zeros((step_rows, 1), F32)
        return (carry[0] + row_sums(grad * normal), carry[1] + row_sums(grad))

    zeros = jnp.zeros((8, width), F32)
    carry = each_rows(back_rows, 0, kept_steps, (zeros, zeros), kept=True)
    for group in range(steps - 1):
        run(group, 2)
    for at, w in ((own_cols, wo[0]), (other_cols, wo[1])):
        upstream[:, at] = mm(attended_grad[...], w, ((1,), (1,))).astype(BF)
    pack(upstream[...], given_1, maps, whole)
    first = list(zip(given_1, taken_1))
    send_all(first, send_1, recv_1)
    begin(steps - 1)
    carry = each_rows(back_rows, kept_steps, all_steps, carry, kept=False)
    sums[...] = jnp.zeros(sums.shape, F32)
    for i in range(2):
        sums[0, 3 + i : 4 + i, :width] = jnp.sum(carry[i], axis=0, keepdims=True)

    for i in range(2):
        for j in range(steps):
            weight_copy(i, j).wait_send()
    pl.semaphore_signal(free_sem, inc=1, device_id=(dp, 1 - core), device_id_type=MESH)
    late_give[:, attend_cols:] = mm(
        attended_grad[...], gathered[:, other_cols], ((0,), (0,))
    ).astype(BF)
    output_own = mm(attended_grad[...], gathered[:, own_cols], ((0,), (0,)))
    pl.semaphore_wait(free_sem, 1)
    layer_copy = pair_copy(2 * steps + 3, layer_own, ct)
    layer_copy.start()
    output_copy, attend_copy = (
        pair_copy(2 * steps + i, late_give.at[:, part], late_got.at[:, part])
        for i, part in enumerate(
            (pl.ds(attend_cols, columns - attend_cols), pl.ds(0, attend_cols))
        )
    )
    output_copy.start()
    output_copy.wait_recv()
    late_got[:, attend_cols:] = (output_own + late_got[:, attend_cols:].astype(F32)).astype(BF)
    begin(steps)
    for group in range(steps - 2):
        run(group, 15)
    run(steps - 2, 5)
    run(steps - 1, 3)

    wait_all(first, send_1, recv_1)
    unpack(taken_1, maps, whole, upstream)
    for load in loads[5:]:
        load.wait()
    masks = lane_masks()
    zero = jnp.zeros((), BF)
    def attend_at(which):
        return pl.ds(pl.multiple_of(which * cols, 128), cols)

    def late_other(which, carry):
        value = mm(buffer[...], proj_grad[1, :, attend_at(which)], ((0,), (0,)))
        late_give[:, attend_at(which)] = value.astype(BF)
        return carry

    def late_own(which, carry):
        value = mm(buffer[...], proj_grad[0, :, attend_at(which)], ((0,), (0,)))
        got = late_got[:, attend_at(which)].astype(F32)
        late_got[:, attend_at(which)] = (value + got).astype(BF)
        return carry

    for i in (1, 0):
        canonical = core if i == 0 else 1 - core

        def pair_step(p, carry, i=i, canonical=canonical):
            def place_of(which):
                return pl.ds(pl.multiple_of(which * cols + p * 128, 128), 128)

            q, k, v = (proj[i, :, place_of(which)] for which in range(3))
            up = upstream[:, place_of(canonical)]
            q_grad = k_grad = v_grad = 0.0
            for e, lanes in enumerate(masks):
                low = probs[(i * pairs + p) * 2 + e]
                wide = low.astype(F32)
                probs_grad = mm(up, jnp.where(lanes, v, zero), ((1,), (1,)))
                delta = jnp.sum(wide * probs_grad, axis=-1, keepdims=True)
                scores_grad = (wide * (probs_grad - delta)).astype(BF)
                v_grad = v_grad + mm(low, jnp.where(lanes, up, zero), ((0,), (0,)))
                q_grad = q_grad + mm(scores_grad, jnp.where(lanes, k, zero), ((1,), (0,)))
                k_grad = k_grad + mm(scores_grad, jnp.where(lanes, q, zero), ((0,), (0,)))
            proj_grad[i, :, place_of(0)] = (q_grad * HD ** (-0.5)).astype(BF)
            proj_grad[i, :, place_of(1)] = (k_grad * HD ** (-0.5)).astype(BF)
            proj_grad[i, :, place_of(2)] = v_grad.astype(BF)
            return carry

        lax.fori_loop(0, pairs, pair_step, 0)
        if i == 1:
            lax.fori_loop(0, 3, late_other, 0)
            attend_copy.start()
        run(steps - 2, 15)
        run(steps - 1, 3)
    upstream[...] = sum(
        mm(proj_grad[i, :, which * cols : (which + 1) * cols], w_vmem[i, which], ((1,), (1,)))
        for i in range(2)
        for which in range(3)
    ).astype(BF)
    pack(upstream[...], given_2, maps, whole)
    second = list(zip(given_2, taken_2))
    send_all(second, send_2, recv_2)

    attend_copy.wait_recv()
    lax.fori_loop(0, 3, late_own, 0)
    begin(steps + 1)
    run(steps - 1, 4)

    wait_all(second, send_2, recv_2)
    unpack(taken_2, maps, whole, upstream)
    tokens_own = hidden

    def first_rows(r, carry, kept):
        rows = rows_of(r)
        normal, scale = norm_stats(x[rows, :].astype(F32))
        normed = (normal * gain[...] + shift[...]).astype(BF).astype(F32)
        logit = logit_grad[rows, :]
        grad = logit * router[...]
        if kept:
            grad = grad + jnp.where(route_cols[rows, 1:2] > 0.5, upstream[rows, :].astype(F32), 0.0)
        total = mixed_grad[rows, :] + norm_pull(grad * gain[...], normal, scale)
        tokens_own[rows, :] = total.astype(BF)
        return (
            carry[0] + row_sums(grad * normal),
            carry[1] + row_sums(grad),
            carry[2] + row_sums(logit * normed),
        )

    carry = (zeros, zeros, zeros)
    carry = each_rows(first_rows, 0, kept_steps, carry, kept=True)
    carry = each_rows(first_rows, kept_steps, all_steps, carry, kept=False)
    tokens_copy = pair_copy(2 * steps + 2, tokens_own, tokens_got)
    tokens_copy.start()
    for i in range(3):
        sums[0, i : i + 1, :width] = jnp.sum(carry[i], axis=0, keepdims=True)

    sums_pair = pair_copy(2 * steps + 4, sums.at[0], sums_got)
    sums_pair.start()

    def sums_window(device):
        return pl.ds(pl.multiple_of(device * (width // peers) // 128 * 128, 128), 256)

    def sums_copy(d, back):
        to, source = lax.rem(dp + d, peers), lax.rem(dp + peers - d, peers)
        return pltpu.make_async_remote_copy(
            src_ref=sums.at[1, :, sums_window(to)],
            dst_ref=sums_parts.at[source if back else dp],
            send_sem=sums_send.at[d],
            recv_sem=sums_recv.at[d],
            device_id=(to, core),
            device_id_type=MESH,
        )

    def sums_begin():
        sums_pair.wait_recv()
        sums[1] = sums[0] + sums_got[...]

        def start(d, carry):
            sums_copy(d, False).start()
            return carry

        lax.fori_loop(1, peers, start, 0)
        sums_parts[pl.ds(dp, 1)] = sums[1, :, sums_window(dp)][None]

    def sums_finish():
        def arrived(d, carry):
            sums_copy(d, True).wait_recv()
            return carry

        lax.fori_loop(1, peers, arrived, 0)
        sums_out[...] = jnp.sum(sums_parts[...], axis=0)

    def sums_sent(d, carry):
        sums_copy(d, False).wait_send()
        return carry

    block = count // 2

    def unpick(own, other, out, stages, first_sem):
        for r, stage in enumerate(stages):
            size = min(block, out.shape[0] - r * block)
            rows = pl.ds(r * block, size)
            hit = (route_cols[rows, 2:3] == routes[0:1, :]).astype(F32).astype(BF)
            value = mm(hit[:, :count], own[...], ((1,), (0,))) + mm(
                hit[:, count : 2 * count], other[...], ((1,), (0,))
            )
            stage[pl.ds(0, size), :] = value.astype(out.dtype)
            even = size // 8 * 8
            for i, (at, part) in enumerate(((0, even), (even, size - even))):
                if part:
                    copy = pltpu.make_async_copy(
                        stage.at[pl.ds(at, part), :],
                        out.at[pl.ds(r * block + at, part), :],
                        out_sem.at[first_sem + r + i],
                    )
                    copy.start()
                    finals.append(copy)

    finals = []
    output_copy.wait_send()
    attend_copy.wait_send()
    layer_stages = [
        reduce_give.at[pl.ds(r * block, block), pl.ds(side * width, width)]
        for side in range(2)
        for r in range(2)
    ]
    tokens_stages = [
        ref.at[pl.ds(r * block, block), :] for ref in (mlp, mixed_grad) for r in range(2)
    ]
    run(steps - 1, 15)
    sums_begin()
    run(steps, 8)
    run(steps + 1, 2)
    layer_copy.wait_recv()
    unpick(layer_own, ct, layer_out, layer_stages, 0)
    run(steps, 15)
    run(steps + 1, 4)
    tokens_copy.wait_recv()
    unpick(tokens_own, tokens_got, tokens_out, tokens_stages, 4)
    run(steps + 1, 3)
    sums_finish()
    run(steps + 1, 15)
    for chain in chains:
        chain.drain()
    if not chains:
        for i, (here, there) in enumerate(
            (
                (expand_got, expand_out),
                (reduce_got, reduce_out),
                (late_got.at[:, pl.ds(0, attend_cols)], late_out),
                (late_got.at[:, pl.ds(attend_cols, columns - attend_cols)], output_out),
            )
        ):
            finals.append(pltpu.make_async_copy(here, there, load_sem.at[i]))
            finals[-1].start()
    for copy in finals:
        copy.wait()
    for copy in (layer_copy, tokens_copy, sums_pair):
        copy.wait_send()
    lax.fori_loop(1, peers, sums_sent, 0)


def split_blocks(blocks):
    step = len(blocks) // 4
    return [blocks[i * step : (i + 1) * step] for i in range(4)]


def block_scratch(peers, whole, left, parts, width):
    shapes = [(peers, whole, width)] if whole else []
    shapes.append((peers, 16, width // parts))
    return [pltpu.VMEM(shape, BF) for _ in range(4) for shape in shapes], len(shapes)


def exchange_call(
    kernel, name, collective_id, capacity, width, args, spaces, outs, scratch, after=(), out_spaces=None
):
    peers = lax.axis_size("dp")
    whole, left, parts = block_plan(capacity, width)
    blocks, kinds = block_scratch(peers, whole, left, parts, width)
    return pl.pallas_call(
        functools.partial(kernel, whole),
        out_shape=[jax.ShapeDtypeStruct(*out) for out in outs],
        in_specs=[pl.BlockSpec(memory_space=space) for space in spaces],
        out_specs=[
            pl.BlockSpec(memory_space=space) for space in out_spaces or [pltpu.VMEM] * len(outs)
        ],
        scratch_shapes=[
            *scratch,
            *[pltpu.SemaphoreType.DMA((kinds, peers))] * 4,
            *blocks,
            *after,
        ],
        compiler_params=pltpu.CompilerParams(
            collective_id=collective_id, has_side_effects=True, vmem_limit_bytes=58 * 2**20
        ),
        name=name,
    )(*args)


def slot_layout(peers, capacity, whole, own, own_pad, total):
    left = capacity - whole
    spot = np.arange(total) % own_pad
    side = np.arange(total) // own_pad
    main = spot < peers * whole
    rest = spot - peers * whole
    device = np.where(main, spot // max(whole, 1), rest // left)
    slot = np.where(main, spot % max(whole, 1), whole + rest % left)
    is_slot = spot < peers * capacity
    rows = [
        np.where(is_slot, device, 0),
        np.where(is_slot, slot, 4 * capacity),
        np.where((spot < own) & (side < 2), spot, -1),
        np.minimum(side, 1),
    ]
    return jnp.asarray(np.stack(rows + [np.zeros(total)] * 4), jnp.int32)


def attend(
    row_ids, select, priority, vectors, maps, tokens, cotangent, w_own, wo, we, wr, capacity, own, own_pad, total
):
    peers = lax.axis_size("dp")
    count, width = tokens.shape
    slots = peers * capacity
    cols = w_own.shape[2]
    heads = 2 * cols // HD
    whole = block_plan(capacity, width)[0]
    layout = slot_layout(peers, capacity, whole, own, own_pad, total)
    vmem, hbm = pltpu.VMEM, pl.ANY
    kept = [
        ((slots, width), BF), ((2, slots, 3 * cols), BF), ((heads, slots, slots), BF),
        ((own_pad, width), BF), ((own_pad, width), BF),
    ]
    return exchange_call(
        lambda whole, *refs: attend_kernel(whole, capacity, *refs), "attend", 0, capacity, width,
        (row_ids, select, priority, *vectors, layout, maps, tokens, cotangent, w_own, wo, we, wr),
        (vmem,) * 10 + (hbm,) * 6,
        [
            ((slots, width), BF), ((own_pad, 1), F32), ((8, total), F32), ((total, 8), F32),
            ((8, width), F32), *kept, *[(value.shape, BF) for value in (w_own, wo, we, wr)],
        ],
        [
            *[vmem(*value) for value in kept],
            pltpu.SemaphoreType.DMA((4,)), pltpu.SemaphoreType.DMA((4,)), pltpu.SemaphoreType.DMA((6,)),
            vmem((count, width), BF), vmem((count, width), BF),
            vmem((8, total), jnp.int32), vmem((total, 8), F32), vmem((8, total), F32),
            vmem((2, *w_own.shape), BF),
            vmem((slots, width), BF),
            vmem((8, slots), F32),
            pltpu.SemaphoreType.DMA((4,)),
        ],
        (),
        (vmem,) * 5 + (hbm,) * 9,
    )


def back(small, large, probs, capacity, orders, place_rows):
    gathered, wo, _, x, ct, we, _, wr, _, w, _, proj, _, buffer = large
    slots, width = buffer.shape
    count, hidden = x.shape[0], we.shape[1]
    peers = lax.axis_size("dp")
    vmem, hbm = pltpu.VMEM, pl.ANY
    dma = pltpu.SemaphoreType.DMA
    chunk = 512 if hidden % 512 == 0 else hidden
    steps = hidden // chunk
    rows = width // peers
    after = []
    sizes = (hidden, hidden, 3 * w.shape[2], wo.shape[0])
    if orders is None:
        outs = [((width, size), BF) for size in sizes]
        out_spaces = (hbm,) * 6 + (vmem,)
    else:
        outs = [((rows, size), F32) for size in sizes]
        out_spaces = (vmem,) * 4 + (hbm,) * 2 + (vmem,)
        counts = [peers >> (stage + 1) for stage in range(len(orders[0]))]
        left_cols = -(-sizes[2] // 256) * 128
        for size in [chunk] * (2 * steps) + [sizes[3], left_cols, sizes[2] - left_cols]:
            after += [dma((sum(counts),))] * 2
            after += [vmem((n, rows, size), BF) for n in counts]
    outs += [((-(-place_rows // 16) * 16, width), BF), ((place_rows, width), F32), ((8, 256), F32)]
    low = vmem((count, width), BF)
    wide = vmem((count, width), F32)
    turned = vmem((width, count), BF)
    column = vmem((count, 1), F32)
    slot_rows = vmem((slots, width), BF)
    gradient = vmem((width, hidden), BF)
    return exchange_call(
        lambda whole, *refs: back_kernel(whole, orders, *refs), "back", 1, capacity, width,
        (*small, *large),
        (vmem,) * len(small) + (hbm,) * len(large),
        outs,
        [
            slot_rows, vmem((2, *wo.shape), BF), low, low, vmem((2, *w.shape), BF),
            vmem(proj.shape, BF), vmem(probs.shape, BF), slot_rows,
            vmem((2, width, chunk), BF), vmem((2, chunk, width), BF),
            vmem((slots, width), F32), column, column, low, turned, turned, wide, wide,
            vmem((count, chunk), F32), vmem((count, chunk), F32),
            vmem((count, chunk), BF), vmem((count, chunk), BF),
            column, slot_rows, slot_rows, vmem(proj.shape, BF), low, low,
            gradient, gradient, gradient, gradient,
            vmem((2, 8, width + 256), F32), vmem((8, width + 256), F32), vmem((peers, 8, 256), F32),
            dma((10,)), dma((2,)), dma((2,)), dma((10,)),
            dma((2 * steps + 5,)), dma((2 * steps + 5,)), dma((peers,)), dma((peers,)),
            pltpu.SemaphoreType.REGULAR,
        ],
        after,
        out_spaces,
    )


def shards(
    tokens,
    row_ids,
    select,
    priority,
    first_gain,
    first_shift,
    router,
    w_attend,
    w_output,
    second_gain,
    second_shift,
    w_expand,
    w_reduce,
    cotangent,
):
    dp_count = lax.axis_size("dp")
    mp_count = lax.axis_size("mp")
    core = lax.axis_index("mp")
    bits = dp_count.bit_length() - 1
    order_a = list(range(bits))
    order_b = [1, 0] + list(range(bits - 1, 1, -1))
    capacity = 5 * ROW_LEN // (8 * dp_count)
    count, width = tokens.shape
    own = count // mp_count
    own_pad = -(-own // 128) * 128
    heads_cols = w_attend.shape[2]
    whole, left, parts = block_plan(capacity, width)
    maps = rest_map(dp_count, left, parts)

    w_attend = w_attend.transpose(1, 0, 2)

    total = max(-(-count // 128) * 128, mp_count * own_pad)
    (gathered, gate, routes, route_cols, vectors, buffer, proj, probs, x, ct,
     w_other, wo_other, we_other, wr_other) = attend(
        row_ids, select, priority, (first_gain, first_shift, router, second_gain, second_shift),
        maps, tokens, cotangent, w_attend, w_output, w_expand, w_reduce, capacity, own, own_pad, total,
    )
    orders = (order_a, order_b) if width // dp_count % 16 == 0 else None
    expand_sum, reduce_sum, attend_sum, output_sum, layer_out, tokens_grad, vectors = back(
        (maps, gate, vectors, routes, route_cols),
        (gathered, w_output, wo_other, x, ct, w_expand, we_other, w_reduce, wr_other, w_attend, w_other,
         proj, probs, buffer),
        probs, capacity, orders, count,
    )
    if orders is None:
        expand_sum = scatter_sum(expand_sum, order_a)
        reduce_sum = scatter_sum(reduce_sum, order_b)
        attend_sum = scatter_sum(attend_sum, order_a)
        output_sum = scatter_sum(output_sum, order_b)
    rows_here = width // dp_count
    vectors = lax.dynamic_slice_in_dim(vectors, lax.axis_index("dp") * rows_here % 128, rows_here, 1)

    return (
        layer_out[:count],
        tokens_grad,
        vectors[0],
        vectors[1],
        vectors[2],
        attend_sum.reshape(-1, 3, heads_cols),
        output_sum.T,
        vectors[3],
        vectors[4],
        expand_sum,
        reduce_sum.T,
    )


def solution(mesh):
    in_specs = (
        P("dp", None),
        P("dp"),
        P("dp"),
        P("dp"),
        P(),
        P(),
        P(),
        P(None, None, "mp"),
        P("mp", None),
        P(),
        P(),
        P(None, "mp"),
        P("mp", None),
        P("dp", None),
    )
    out_specs = (
        P("dp", None),
        P("dp", None),
        P("dp"),
        P("dp"),
        P("dp"),
        P("dp", None, "mp"),
        P("mp", "dp"),
        P("dp"),
        P("dp"),
        P("dp", "mp"),
        P("mp", "dp"),
    )
    return jax.shard_map(shards, mesh=mesh, in_specs=in_specs, out_specs=out_specs, check_vma=False)
```

```python
import functools

import jax
import jax.numpy as jnp
import numpy as np
from jax import lax
from jax.experimental import pallas as pl
from jax.experimental.pallas import tpu as pltpu
from jax.sharding import PartitionSpec as P

HD = 64
ROW_LEN = 577
EPSILON = 1e-06
MASKED_SCORE = -1000000000.0
EMPTY = 1e30
BF = jnp.bfloat16
F32 = jnp.float32
MESH = pl.DeviceIdType.MESH


def mm(a, b, dims):
    return lax.dot_general(a, b, (dims, ((), ())), preferred_element_type=F32)


def norm_stats(value):
    center = value - jnp.mean(value, axis=-1, keepdims=True)
    inv = lax.rsqrt(jnp.mean(center * center, axis=-1, keepdims=True) + EPSILON)
    return center * inv, inv


def norm_pull(e, nhat, inv):
    return (e - jnp.mean(e, axis=-1, keepdims=True) - nhat * jnp.mean(e * nhat, axis=-1, keepdims=True)) * inv


def swap(value):
    return lax.ppermute(value, "mp", [(0, 1), (1, 0)])


def scatter_sum(grad, order):
    count = lax.axis_size("dp")
    me = lax.axis_index("dp")
    bits = count.bit_length() - 1
    width = grad.shape[0] // count
    dims = [2] * bits
    value = grad.reshape(dims + [width, grad.shape[1]])
    out = None
    for step in order:
        axis = bits - 1 - step
        mine = (me >> step) & 1
        give = lax.dynamic_slice_in_dim(value, 1 - mine, 1, axis)
        keep = lax.dynamic_slice_in_dim(value, mine, 1, axis)
        got = lax.ppermute(give, "dp", [(i, i ^ (1 << step)) for i in range(count)])
        out = keep.astype(F32) + got.astype(F32)
        value = out.astype(grad.dtype)
    return out.reshape(width, grad.shape[1])


def block_plan(capacity, width):
    whole = capacity // 16 * 16
    left = capacity - whole
    parts = max(s for s in (1, 2, 3, 6) if left * s <= 16 and width % (128 * s) == 0)
    return whole, left, parts


def rest_map(peers, left, parts):
    at = np.arange(peers * 16)[None, :, None]
    row = np.arange(peers * left)[None, None, :]
    part = np.arange(parts)[:, None, None]
    hit = (at // 16 == row // left) & (at % 16 == part * left + row % left)
    return jnp.asarray(hit.astype(np.float32), BF)


def greet(peers, with_pair=False):
    me, core = lax.axis_index("dp"), lax.axis_index("mp")
    barrier = pltpu.get_barrier_semaphore()

    def hello(d, carry):
        pl.semaphore_signal(
            barrier, inc=1, device_id=(lax.rem(me + d, peers), core), device_id_type=MESH
        )
        return carry

    lax.fori_loop(1, peers, hello, 0)
    if with_pair:
        pl.semaphore_signal(barrier, inc=1, device_id=(me, 1 - core), device_id_type=MESH)
    return lambda: pl.semaphore_wait(barrier, peers if with_pair else peers - 1)


def pack(value, blocks, maps, whole):
    rest = blocks[-1]
    peers, lanes = rest.shape[0], rest.shape[2]
    if whole:
        blocks[0][...] = value[: peers * whole].reshape(peers, whole, value.shape[1])
    tail = value[peers * whole :]
    total = sum(
        mm(maps[i], tail[:, i * lanes : (i + 1) * lanes], ((1,), (0,)))
        for i in range(maps.shape[0])
    )
    rest[...] = total.astype(BF).reshape(peers, 16, lanes)


def unpack(blocks, maps, whole, out):
    rest = blocks[-1]
    peers, lanes = rest.shape[0], rest.shape[2]
    if whole:
        out[: peers * whole, :] = blocks[0][...].reshape(peers * whole, out.shape[1])
    left = rest[...].reshape(peers * 16, lanes)
    for i in range(maps.shape[0]):
        out[peers * whole :, i * lanes : (i + 1) * lanes] = mm(
            maps[i], left, ((0,), (0,))
        ).astype(BF)


def copies(d, pairs, sends, recvs, back=False):
    me, core = lax.axis_index("dp"), lax.axis_index("mp")
    peers = pairs[0][0].shape[0]
    to, source = lax.rem(me + d, peers), lax.rem(me + peers - d, peers)
    return [
        pltpu.make_async_remote_copy(
            src_ref=here.at[to],
            dst_ref=there.at[source if back else me],
            send_sem=sends.at[i, d],
            recv_sem=recvs.at[i, d],
            device_id=(to, core),
            device_id_type=MESH,
        )
        for i, (here, there) in enumerate(pairs)
    ]


def send_all(pairs, sends, recvs):
    me = lax.axis_index("dp")

    def start(d, carry):
        for copy in copies(d, pairs, sends, recvs):
            copy.start()
        return carry

    lax.fori_loop(1, pairs[0][0].shape[0], start, 0)
    for here, there in pairs:
        there[pl.ds(me, 1)] = here[pl.ds(me, 1)]


def wait_all(pairs, sends, recvs):
    def finish(d, carry):
        for copy in copies(d, pairs, sends, recvs, back=True):
            copy.wait_recv()
        return carry

    def drain(d, carry):
        for copy in copies(d, pairs, sends, recvs):
            copy.wait_send()
        return carry

    lax.fori_loop(1, pairs[0][0].shape[0], finish, 0)
    lax.fori_loop(1, pairs[0][0].shape[0], drain, 0)


def lane_masks():
    low = lax.broadcasted_iota(jnp.int32, (1, 128), 1) < HD
    return low, jnp.logical_not(low)


def routing(info, layout, capacity, count, wide_cols, hit_rows, routes, route_cols):
    core = lax.axis_index("mp").astype(F32)
    cores = lax.axis_size("mp")
    total = info.shape[1]
    blocks = total // 128
    row, chosen, priority = (info[i : i + 1, :].astype(F32) for i in range(3))
    device, slot, spot, side = (layout[i : i + 1, :].astype(F32) for i in range(4))
    core_of = core + side * (1.0 - 2.0 * core)
    row_of = device * cores + core_of
    spot_of = jnp.where(spot >= 0.0, core_of * total + spot, -1.0)
    low = row * 2048.0
    key = low + priority
    picked = chosen > 0.5
    hit_rows[...] = jnp.zeros(hit_rows.shape, F32)
    hit_rows[0:1, :] = jnp.where(picked, key, -1.0)
    hit_rows[1:2, :] = jnp.where(picked, row, -1.0)
    wide_cols[...] = hit_rows[...].T

    def fold(hit):
        return jnp.sum(jnp.where(hit, 1.0, 0.0).reshape(16, 8, total), axis=0)

    def count_rows(b, carry):
        at = pl.ds(pl.multiple_of(b * 128, 128), 128)
        keys, rows = wide_cols[at, 0:1], wide_cols[at, 1:2]
        return (
            carry[0] + fold((keys >= low) & (keys < key)),
            carry[1] + fold(rows == row_of),
        )

    zeros = jnp.zeros((8, total), F32)
    ranks, sizes = lax.fori_loop(0, blocks, count_rows, (zeros, zeros))
    rank = jnp.sum(ranks, axis=0, keepdims=True)
    size = jnp.sum(sizes, axis=0, keepdims=True)
    kept = picked & (rank < capacity)
    filled = slot < jnp.minimum(size, float(capacity))
    index = lax.broadcasted_iota(jnp.int32, (1, total), 1).astype(F32)
    rest = (index < count) & jnp.logical_not(kept)
    free = (spot_of >= 0.0) & jnp.logical_not(filled)
    hit_rows[0:1, :] = jnp.where(rest, index, 1e9)
    hit_rows[1:2, :] = jnp.where(free, spot_of, 1e9)
    wide_cols[...] = hit_rows[...].T

    def count_rest(b, carry):
        at = pl.ds(pl.multiple_of(b * 128, 128), 128)
        return (
            carry[0] + fold(wide_cols[at, 0:1] < index),
            carry[1] + fold(wide_cols[at, 1:2] < spot_of),
        )

    before, ahead = lax.fori_loop(0, blocks, count_rest, (zeros, zeros))
    base = float(lax.axis_size("dp") * cores * capacity)
    before = base + jnp.sum(before, axis=0, keepdims=True)
    ahead = base + jnp.sum(ahead, axis=0, keepdims=True)
    routes[...] = jnp.zeros(routes.shape, F32)
    routes[0:1, :] = jnp.where(
        filled, row_of * capacity + slot, jnp.where(spot_of >= 0.0, ahead, -1.0)
    )
    routes[1:2, :] = jnp.where(filled, 1.0, 0.0)
    routes[2:3, :] = jnp.where(kept, row * capacity + rank, jnp.where(rest, before, -2.0))
    route_cols[...] = routes[...].T


def each_rows(body, first, last, carry, **kept):
    for r in range(first, last):
        carry = body(r, carry, **kept)
    return carry


def attend_kernel(
    whole, capacity, row_ids, select, priority, first_gain, first_shift, router_in, second_gain, second_shift,
    layout, maps, tokens_in, cotangent_in, w_own, wo_own, we_own, wr_own,
    gathered, gate, routes, route_cols, vectors, buffer_out, proj_out, probs_out, x_out, ct_out,
    w_out, wo_out, we_out, wr_out,
    buffer, proj, probs, x, ct, swap_send, swap_recv, out_sem, tokens, cotangent, info, wide_cols, hit_rows,
    w_vmem, context, key_mask, w_sem, send_1, recv_1, send_2, recv_2, *blocks,
):
    core = lax.axis_index("mp")
    loads = [
        pltpu.make_async_copy(here, there, w_sem.at[i])
        for i, (here, there) in enumerate(
            (
                (tokens_in, tokens),
                (cotangent_in, cotangent),
                (w_own, w_vmem.at[0]),
            )
        )
    ]
    for load in loads:
        load.start()
    given_1, taken_1, given_2, taken_2 = split_blocks(blocks)
    ready = greet(given_1[-1].shape[0], with_pair=True)
    swaps = [
        pltpu.make_async_remote_copy(
            src_ref=here,
            dst_ref=there,
            send_sem=swap_send.at[i],
            recv_sem=swap_recv.at[i],
            device_id=(lax.axis_index("dp"), 1 - core),
            device_id_type=MESH,
        )
        for i, (here, there) in enumerate(
            ((w_own, w_vmem.at[1]), (wo_own, wo_out), (we_own, we_out), (wr_own, wr_out))
        )
    ]
    leaving = [
        pltpu.make_async_copy(here, there, out_sem.at[i])
        for i, (here, there) in enumerate(
            (
                (x, x_out),
                (ct, ct_out),
                (buffer, buffer_out),
                (proj, proj_out),
                (probs, probs_out),
                (w_vmem.at[1], w_out),
            )
        )
    ]
    count, width = tokens.shape
    slots = buffer.shape[0]
    total_rows = x.shape[0]
    info[...] = jnp.zeros(info.shape, jnp.int32)
    for i, source in enumerate((row_ids, select, priority)):
        info[i : i + 1, :count] = source[...].reshape(1, count)
    vectors[...] = jnp.zeros(vectors.shape, F32)
    for i, source in enumerate((first_gain, first_shift, router_in, second_gain, second_shift)):
        vectors[i : i + 1, :] = source[...].reshape(1, width)
    routing(info, layout, capacity, count, wide_cols, hit_rows, routes, route_cols)
    ready()
    swaps[0].start()
    loads[0].wait()

    def pick(r, source, out):
        at = pl.ds(pl.multiple_of(r * 128, 128), 128)
        hit = (route_cols[at, 0:1] == routes[2:3, :count]).astype(F32).astype(BF)
        out[at, :] = mm(hit, source[...], ((1,), (0,))).astype(BF)

    def norm_rows(r, carry, sent):
        at = pl.ds(pl.multiple_of(r * 32, 32), 32)
        normal, _ = norm_stats(x[at, :].astype(F32))
        normed = (normal * vectors[0:1, :] + vectors[1:2, :]).astype(BF)
        wide = normed.astype(F32)
        gate[at, :] = jax.nn.sigmoid(jnp.sum(wide * vectors[2:3, :], axis=-1, keepdims=True))
        if sent:
            context[at, :] = jnp.where(route_cols[at, 1:2] > 0.5, wide, EMPTY).astype(BF)
        return carry

    def picks(first, last, source, out):
        def body(r, carry):
            pick(r, source, out)
            return carry

        lax.fori_loop(first, last, body, 0)

    kept_blocks = -(-slots // 128)
    picks(0, kept_blocks, tokens, x)
    each_rows(norm_rows, 0, slots // 32, 0, sent=True)
    pack(context[...], given_1, maps, whole)
    first = list(zip(given_1, taken_1))
    send_all(first, send_1, recv_1)
    for copy in swaps[1:]:
        copy.start()
    picks(kept_blocks, total_rows // 128, tokens, x)
    each_rows(norm_rows, slots // 32, total_rows // 32, 0, sent=False)
    loads[1].wait()
    picks(0, total_rows // 128, cotangent, ct)
    leaving[0].start()
    leaving[1].start()
    swaps[0].wait_recv()
    leaving[5].start()
    wait_all(first, send_1, recv_1)
    unpack(taken_1, maps, whole, buffer)
    lane = (lax.broadcasted_iota(jnp.int32, (8, 128), 1) == 0).astype(F32).astype(BF)
    key_mask[...] = jnp.where(
        mm(lane, buffer[:, :128], ((1,), (1,))) < 0.5 * EMPTY, 1.0, 0.0
    )
    received = buffer[...].astype(F32)
    buffer[...] = jnp.where(received[:, :1] < 0.5 * EMPTY, received, 0.0).astype(BF)
    cols = w_own.shape[2]
    pairs = cols // 128
    masks = lane_masks()
    zero = jnp.zeros((), BF)
    for i in range(2):
        if i == 0:
            loads[2].wait()
        for which in range(3):
            proj[i, :, which * cols : (which + 1) * cols] = mm(
                buffer[...], w_vmem[i, which], ((1,), (0,))
            ).astype(BF)
        canonical = core if i == 0 else 1 - core

        def pair_step(p, carry, i=i, canonical=canonical):
            def part(which):
                return proj[i, :, pl.ds(pl.multiple_of(which * cols + p * 128, 128), 128)]

            q, k, v = part(0), part(1), part(2)
            total = 0.0
            for e, lanes in enumerate(masks):
                scores = mm(q, jnp.where(lanes, k, zero), ((1,), (1,))) * HD ** (-0.5)
                scores = jnp.where(key_mask[:1, :] > 0.5, scores, MASKED_SCORE)
                weights = jnp.exp(scores - jnp.max(scores, axis=-1, keepdims=True))
                low = (weights * (1.0 / jnp.sum(weights, axis=-1, keepdims=True))).astype(BF)
                probs[(i * pairs + p) * 2 + e] = low
                total = total + mm(low, jnp.where(lanes, v, zero), ((1,), (0,)))
            context[:, pl.ds(pl.multiple_of(canonical * cols + p * 128, 128), 128)] = total.astype(BF)
            return carry

        lax.fori_loop(0, pairs, pair_step, 0)
    pack(context[...], given_2, maps, whole)
    second = list(zip(given_2, taken_2))
    send_all(second, send_2, recv_2)
    for copy in leaving[2:5]:
        copy.start()
    wait_all(second, send_2, recv_2)
    unpack(taken_2, maps, whole, gathered)
    for copy in leaving:
        copy.wait()
    for copy in swaps[1:]:
        copy.wait_recv()
    for copy in swaps:
        copy.wait_send()


class Halving:
    def __init__(self, source, bufs, sends, recvs, order, out, window):
        self.source, self.bufs, self.sends, self.recvs = source, bufs, sends, recvs
        self.order, self.out, self.window = order, out, window
        self.stages = len(order)
        self.rows = bufs[0].shape[1]
        self.counts = [buf.shape[0] for buf in bufs]
        self.first = [k for stage, k in halving_plan(self.stages) if stage == 0]

    def bit(self, stage):
        return lax.rem(lax.div(lax.axis_index("dp"), 1 << self.order[stage]), 2)

    def block(self, k, kept):
        index = 0
        for stage in range(self.stages):
            mine = self.bit(stage)
            if stage == 0:
                value = mine if kept else 1 - mine
            else:
                part = lax.rem(lax.div(k, self.counts[stage]), 2)
                value = (1 - mine) * (1 - part) + mine * part
            index = index + value * (1 << self.order[stage])
        return pl.ds(pl.multiple_of(index * self.rows, 16), self.rows)

    def copy(self, stage, k):
        me, core = lax.axis_index("dp"), lax.axis_index("mp")
        to = me + (1 - 2 * self.bit(stage)) * (1 << self.order[stage])
        at = sum(self.counts[:stage]) + k
        src = self.source.at[self.block(k, False), :] if stage == 0 else self.bufs[stage - 1].at[k]
        return pltpu.make_async_remote_copy(
            src_ref=src,
            dst_ref=self.bufs[stage].at[k],
            send_sem=self.sends.at[at],
            recv_sem=self.recvs.at[at],
            device_id=(to, core),
            device_id_type=MESH,
        )

    def begin(self):
        for k in self.first[: self.window]:
            self.copy(0, k).start()

    def step(self, stage, k):
        self.copy(stage, k).wait_recv()
        buf = self.bufs[stage]
        if stage == 0:
            own = self.source[self.block(k, True), :]
        else:
            own = self.bufs[stage - 1][pl.ds(self.counts[stage] + k, 1)][0]
        total = own.astype(F32) + buf[pl.ds(k, 1)][0].astype(F32)
        if stage == self.stages - 1:
            self.out[...] = total
            return
        buf[pl.ds(k, 1)] = total.astype(BF)[None]
        if k < self.counts[stage + 1]:
            self.copy(stage + 1, k).start()
        if stage == 0:
            ahead = self.first.index(k) + self.window
            if ahead < len(self.first):
                self.copy(0, self.first[ahead]).start()

    def drain(self):
        for stage, count in enumerate(self.counts):

            def finish(k, carry, stage=stage):
                self.copy(stage, k).wait_send()
                return carry

            lax.fori_loop(0, count, finish, 0)


def halving_plan(stages):
    counts = [1 << (stages - 1 - stage) for stage in range(stages)]
    times = {}
    for stage, count in enumerate(counts):
        for k in range(count):
            if stage == 0:
                bits = [(k >> i) & 1 for i in range(stages - 1)]
                times[stage, k] = 1 + sum(bit << (stages - 2 - i) for i, bit in enumerate(bits))
            else:
                times[stage, k] = 1.6 + max(times[stage - 1, k], times[stage - 1, count + k])
    return sorted(times, key=lambda key: (times[key], key))


def advance(chains, steps):
    for stage, k in steps:
        for chain in chains:
            chain.step(stage, k)


def half_erfc(value, bell):
    t = 1.0 / (1.0 + (0.3275911 * 0.5**0.5) * jnp.abs(value))
    poly = 1.061405429 * t - 1.453152027
    poly = poly * t + 1.421413741
    poly = poly * t - 0.284496736
    poly = poly * t + 0.254829592
    return 0.5 * poly * t * bell


def row_sums(value):
    return jnp.sum(value.reshape(value.shape[0] // 8, 8, value.shape[1]), axis=0)


def back_kernel(
    whole, orders, maps, gate, vectors, routes, route_cols,
    gathered_in, wo_own, wo_other, x_in, ct_in, we_own, we_other, wr_own, wr_other,
    w_own, w_other, proj_in, probs_in, buffer_in,
    expand_out, reduce_out, late_out, output_out, layer_out, tokens_out, sums_out,
    gathered, wo, x, ct, w_vmem, proj, probs, buffer,
    we, wr, attended, mean, inv, hidden, hidden_t, ct_t, mlp, mixed_grad, pre, act_grad, act, pre_grad,
    logit_grad, attended_grad, upstream, proj_grad, layer_own, tokens_got,
    expand_give, reduce_give, expand_got, reduce_got, sums, sums_got, sums_parts,
    load_sem, we_sem, wr_sem, out_sem, pair_send, pair_recv, sums_send, sums_recv, free_sem,
    send_1, recv_1, send_2, recv_2, *rest,
):
    dp, core = lax.axis_index("dp"), lax.axis_index("mp")
    peers = lax.axis_size("dp")
    width, columns = expand_give.shape
    slots = buffer.shape[0]
    count = x.shape[0]
    chunk = pre.shape[1]
    steps = columns // chunk
    cols = w_own.shape[2]
    pairs = cols // 128
    attend_cols = 3 * cols
    left_cols = -(-attend_cols // 256) * 128
    halves = ((0, left_cols), (left_cols, attend_cols - left_cols))
    step_rows = 32
    kept_steps, all_steps = slots // step_rows, count // step_rows
    ready = greet(peers, with_pair=True)
    gain, shift, router, gain_2, shift_2 = (vectors.at[pl.ds(i, 1), :] for i in range(5))

    def chunk_loads(n):
        j, slot = n // 2, n % 2
        here_e, here_r = (we_other, wr_other) if n % 2 == 0 else (we_own, wr_own)
        part = pl.ds(j * chunk, chunk)
        return (
            pltpu.make_async_copy(here_e.at[:, part], we.at[slot], we_sem.at[slot]),
            pltpu.make_async_copy(here_r.at[part, :], wr.at[slot], wr_sem.at[slot]),
        )

    local = [
        (gathered_in, gathered),
        (wo_own, wo.at[0]),
        (wo_other, wo.at[1]),
        (x_in, x),
        (ct_in, ct),
        (proj_in, proj),
        (probs_in, probs),
        (w_own, w_vmem.at[0]),
        (w_other, w_vmem.at[1]),
        (buffer_in, buffer),
    ]
    loads = [
        pltpu.make_async_copy(here, there, load_sem.at[i]) for i, (here, there) in enumerate(local)
    ]
    for load in (*loads[:5], *chunk_loads(0), *loads[5:]):
        load.start()

    kinds = 2 if whole else 1
    given_1, taken_1, given_2, taken_2 = split_blocks(rest[: 4 * kinds])
    rest = rest[4 * kinds :]
    late_give, late_got = reduce_give, expand_give
    chains = []
    plan = []
    if orders is not None:
        stages = len(orders[0])
        plan = halving_plan(stages)
        parts_of = []
        for j in range(steps):
            part = pl.ds(j * chunk, chunk)
            parts_of.append((expand_got.at[:, part], expand_out.at[:, part], orders[0], 4))
            parts_of.append((reduce_got.at[:, part], reduce_out.at[:, part], orders[1], 4))
        groups = [[2 * j, 2 * j + 1] for j in range(steps)] + [[2 * steps], [2 * steps + 1, 2 * steps + 2]]
        output_part = pl.ds(attend_cols, columns - attend_cols)
        parts_of.append((late_got.at[:, output_part], output_out, orders[0], 8))
        for j, (first_col, size) in enumerate(halves):
            part = pl.ds(first_col, size)
            parts_of.append((late_got.at[:, part], late_out.at[:, part], orders[j], 4))
        for i, (source, out, order, window) in enumerate(parts_of):
            mine = rest[i * (stages + 2) : (i + 1) * (stages + 2)]
            chains.append(Halving(source, mine[2:], mine[0], mine[1], order, out, window))
    done = [0] * (steps + 2)

    def run(group, number):
        if chains:
            advance([chains[i] for i in groups[group]], plan[done[group] : done[group] + number])
            done[group] += number

    def begin(group):
        if chains:
            for i in groups[group]:
                chains[i].begin()

    def pair_copy(at, give, got):
        return pltpu.make_async_remote_copy(
            src_ref=give,
            dst_ref=got,
            send_sem=pair_send.at[at],
            recv_sem=pair_recv.at[at],
            device_id=(dp, 1 - core),
            device_id_type=MESH,
        )

    def weight_copy(i, j):
        give, got = ((expand_give, expand_got), (reduce_give, reduce_got))[i]
        part = pl.ds(j * chunk, chunk)
        return pair_copy(i * steps + j, give.at[:, part], got.at[:, part])

    own_cols = pl.ds(pl.multiple_of(core * cols, 128), cols)
    other_cols = pl.ds(pl.multiple_of((1 - core) * cols, 128), cols)
    for load in loads[:3]:
        load.wait()
    attended[...] = mm(gathered[:, own_cols], wo[0], ((1,), (0,))) + mm(
        gathered[:, other_cols], wo[1], ((1,), (0,))
    )
    for load in loads[3:5]:
        load.wait()

    def rows_of(r):
        return pl.ds(pl.multiple_of(r * step_rows, step_rows), step_rows)

    def mixed_rows(rows, kept):
        value = x[rows, :].astype(F32)
        return value + gate[rows, :] * attended[rows, :] if kept else value

    def norm_rows(r, carry, kept):
        rows = rows_of(r)
        if kept:
            attended[rows, :] = jnp.where(route_cols[rows, 1:2] > 0.5, attended[rows, :], 0.0)
        value = mixed_rows(rows, kept)
        middle = jnp.mean(value, axis=-1, keepdims=True)
        center = value - middle
        scale = lax.rsqrt(jnp.mean(center * center, axis=-1, keepdims=True) + EPSILON)
        mean[rows, :] = middle
        inv[rows, :] = scale
        hidden[rows, :] = (center * scale * gain_2[...] + shift_2[...]).astype(BF)
        mlp[rows, :] = jnp.zeros((step_rows, width), F32)
        mixed_grad[rows, :] = jnp.zeros((step_rows, width), F32)
        return carry

    each_rows(norm_rows, 0, kept_steps, 0, kept=True)
    each_rows(norm_rows, kept_steps, all_steps, 0, kept=False)
    hidden_t[...] = hidden[...].T
    ct_t[...] = ct[...].T

    def gelu_rows(r, carry):
        rows = pl.ds(pl.multiple_of(r * 16, 16), 16)
        value = pre[rows, :]
        bell = jnp.exp(-0.5 * value * value)
        tail = half_erfc(value, bell)
        phi = jnp.where(value < 0.0, tail, 1.0 - tail)
        act[rows, :] = (value * phi).astype(BF)
        slope = phi + value * bell * 0.3989422804014327
        pre_grad[rows, :] = (act_grad[rows, :] * slope).astype(BF)
        return carry

    for n in range(2 * steps):
        j, slot, is_own = n // 2, n % 2, n % 2 == 1
        part = pl.ds(j * chunk, chunk)
        for load in chunk_loads(n):
            load.wait()
        if n + 1 < 2 * steps:
            for load in chunk_loads(n + 1):
                load.start()

        def point(n=n, j=j, is_own=is_own):
            for group in range(j):
                run(group, 1)

        pre[...] = mm(hidden[...], we[slot], ((1,), (0,)))
        act_grad[...] = mm(ct[...], wr[slot], ((1,), (1,)))
        lax.fori_loop(0, count // 16, gelu_rows, 0, unroll=2)
        point()
        mlp[...] += mm(act[...], wr[slot], ((1,), (0,)))
        mixed_grad[...] += mm(pre_grad[...], we[slot], ((1,), (1,)))
        point()
        for i, (left, right, give, got) in enumerate(
            (
                (hidden_t, pre_grad, expand_give, expand_got),
                (ct_t, act, reduce_give, reduce_got),
            )
        ):
            value = mm(left[...], right[...], ((1,), (0,)))
            if is_own:
                weight_copy(i, j).wait_recv()
                got[:, part] = (value + got[:, part].astype(F32)).astype(BF)
            else:
                give[:, part] = value.astype(BF)
                if n == 0 and i == 0:
                    ready()
                weight_copy(i, j).start()
        point()
        if is_own and j < steps - 1:
            begin(j)

    def back_rows(r, carry, kept):
        rows = rows_of(r)
        mixed = mixed_rows(rows, kept)
        layer_own[rows, :] = (mixed + mlp[rows, :]).astype(BF)
        grad = mixed_grad[rows, :]
        scale = inv[rows, :]
        normal = (mixed - mean[rows, :]) * scale
        total = ct[rows, :].astype(F32) + norm_pull(grad * gain_2[...], normal, scale)
        mixed_grad[rows, :] = total
        if kept:
            open_by = gate[rows, :]
            attended_grad[rows, :] = jnp.where(route_cols[rows, 1:2] > 0.5, open_by * total, 0.0).astype(BF)
            logit_grad[rows, :] = (
                jnp.sum(total * attended[rows, :], axis=-1, keepdims=True) * open_by * (1.0 - open_by)
            )
        else:
            logit_grad[rows, :] = jnp.zeros((step_rows, 1), F32)
        return (carry[0] + row_sums(grad * normal), carry[1] + row_sums(grad))

    zeros = jnp.zeros((8, width), F32)
    carry = each_rows(back_rows, 0, kept_steps, (zeros, zeros), kept=True)
    for group in range(steps - 1):
        run(group, 2)
    for at, w in ((own_cols, wo[0]), (other_cols, wo[1])):
        upstream[:, at] = mm(attended_grad[...], w, ((1,), (1,))).astype(BF)
    pack(upstream[...], given_1, maps, whole)
    first = list(zip(given_1, taken_1))
    send_all(first, send_1, recv_1)
    begin(steps - 1)
    carry = each_rows(back_rows, kept_steps, all_steps, carry, kept=False)
    sums[...] = jnp.zeros(sums.shape, F32)
    for i in range(2):
        sums[0, 3 + i : 4 + i, :width] = jnp.sum(carry[i], axis=0, keepdims=True)

    block = count // 2
    finals = []

    def unpick(own, other, out, stages, first_sem):
        sent = []
        for r in range(-(-out.shape[0] // block)):
            stage = stages[r % len(stages)]
            size = min(block, out.shape[0] - r * block)
            rows = pl.ds(r * block, size)
            hit = (route_cols[rows, 2:3] == routes[0:1, :]).astype(F32).astype(BF)
            value = mm(hit[:, :count], own[...], ((1,), (0,))) + mm(
                hit[:, count : 2 * count], other[...], ((1,), (0,))
            )
            if r >= len(stages):
                sent[r - len(stages)].wait()
            stage[pl.ds(0, size), :] = value.astype(out.dtype)
            copy = pltpu.make_async_copy(
                stage.at[pl.ds(0, size), :], out.at[rows, :], out_sem.at[first_sem + r]
            )
            copy.start()
            sent.append(copy)
        return sent[-len(stages) :]

    for i in range(2):
        for j in range(steps):
            weight_copy(i, j).wait_send()
    pl.semaphore_signal(free_sem, inc=1, device_id=(dp, 1 - core), device_id_type=MESH)
    late_give[:, attend_cols:] = mm(
        attended_grad[...], gathered[:, other_cols], ((0,), (0,))
    ).astype(BF)
    output_own = mm(attended_grad[...], gathered[:, own_cols], ((0,), (0,)))
    pl.semaphore_wait(free_sem, 1)
    layer_copy = pair_copy(2 * steps + 3, layer_own, ct)
    layer_copy.start()
    output_copy, attend_copy = (
        pair_copy(2 * steps + i, late_give.at[:, part], late_got.at[:, part])
        for i, part in enumerate(
            (pl.ds(attend_cols, columns - attend_cols), pl.ds(0, attend_cols))
        )
    )
    output_copy.start()
    output_copy.wait_recv()
    late_got[:, attend_cols:] = (output_own + late_got[:, attend_cols:].astype(F32)).astype(BF)
    begin(steps)
    for group in range(steps - 2):
        run(group, 15)
    run(steps - 2, 2)
    layer_copy.wait_recv()
    hidden_blocks = [hidden.at[pl.ds(r * block, block), :] for r in range(2)]
    layer_finals = unpick(layer_own, ct, layer_out, hidden_blocks, 0)
    run(steps - 2, 1)

    wait_all(first, send_1, recv_1)
    unpack(taken_1, maps, whole, upstream)
    for load in loads[5:]:
        load.wait()
    masks = lane_masks()
    zero = jnp.zeros((), BF)
    def attend_at(which):
        return pl.ds(pl.multiple_of(which * cols, 128), cols)

    def late_other(which, carry):
        value = mm(buffer[...], proj_grad[1, :, attend_at(which)], ((0,), (0,)))
        late_give[:, attend_at(which)] = value.astype(BF)
        return carry

    def late_own(which, carry):
        value = mm(buffer[...], proj_grad[0, :, attend_at(which)], ((0,), (0,)))
        got = late_got[:, attend_at(which)].astype(F32)
        late_got[:, attend_at(which)] = (value + got).astype(BF)
        return carry

    for i in (1, 0):
        canonical = core if i == 0 else 1 - core

        def pair_step(p, carry, i=i, canonical=canonical):
            def place_of(which):
                return pl.ds(pl.multiple_of(which * cols + p * 128, 128), 128)

            q, k, v = (proj[i, :, place_of(which)] for which in range(3))
            up = upstream[:, place_of(canonical)]
            q_grad = k_grad = v_grad = 0.0
            for e, lanes in enumerate(masks):
                low = probs[(i * pairs + p) * 2 + e]
                wide = low.astype(F32)
                probs_grad = mm(up, jnp.where(lanes, v, zero), ((1,), (1,)))
                delta = jnp.sum(wide * probs_grad, axis=-1, keepdims=True)
                scores_grad = (wide * (probs_grad - delta)).astype(BF)
                v_grad = v_grad + mm(low, jnp.where(lanes, up, zero), ((0,), (0,)))
                q_grad = q_grad + mm(scores_grad, jnp.where(lanes, k, zero), ((1,), (0,)))
                k_grad = k_grad + mm(scores_grad, jnp.where(lanes, q, zero), ((0,), (0,)))
            proj_grad[i, :, place_of(0)] = (q_grad * HD ** (-0.5)).astype(BF)
            proj_grad[i, :, place_of(1)] = (k_grad * HD ** (-0.5)).astype(BF)
            proj_grad[i, :, place_of(2)] = v_grad.astype(BF)
            return carry

        lax.fori_loop(0, pairs, pair_step, 0)
        if i == 1:
            lax.fori_loop(0, 3, late_other, 0)
            attend_copy.start()
        run(steps - 2, 2)
        run(steps - 1, 3)
    attend_copy.wait_recv()
    lax.fori_loop(0, 3, late_own, 0)
    begin(steps + 1)
    upstream[...] = sum(
        mm(proj_grad[i, :, which * cols : (which + 1) * cols], w_vmem[i, which], ((1,), (1,)))
        for i in range(2)
        for which in range(3)
    ).astype(BF)
    pack(upstream[...], given_2, maps, whole)
    second = list(zip(given_2, taken_2))
    send_all(second, send_2, recv_2)

    run(steps - 2, 15)
    run(steps - 1, 4)
    run(steps, 4)

    wait_all(second, send_2, recv_2)
    unpack(taken_2, maps, whole, upstream)
    tokens_own = hidden
    for copy in layer_finals:
        copy.wait()

    def first_rows(r, carry, kept):
        rows = rows_of(r)
        normal, scale = norm_stats(x[rows, :].astype(F32))
        normed = (normal * gain[...] + shift[...]).astype(BF).astype(F32)
        logit = logit_grad[rows, :]
        grad = logit * router[...]
        if kept:
            grad = grad + jnp.where(route_cols[rows, 1:2] > 0.5, upstream[rows, :].astype(F32), 0.0)
        total = mixed_grad[rows, :] + norm_pull(grad * gain[...], normal, scale)
        tokens_own[rows, :] = total.astype(BF)
        return (
            carry[0] + row_sums(grad * normal),
            carry[1] + row_sums(grad),
            carry[2] + row_sums(logit * normed),
        )

    carry = (zeros, zeros, zeros)
    carry = each_rows(first_rows, 0, kept_steps, carry, kept=True)
    carry = each_rows(first_rows, kept_steps, all_steps, carry, kept=False)
    tokens_copy = pair_copy(2 * steps + 2, tokens_own, tokens_got)
    tokens_copy.start()
    for i in range(3):
        sums[0, i : i + 1, :width] = jnp.sum(carry[i], axis=0, keepdims=True)

    sums_pair = pair_copy(2 * steps + 4, sums.at[0], sums_got)
    sums_pair.start()

    def sums_window(device):
        return pl.ds(pl.multiple_of(device * (width // peers) // 128 * 128, 128), 256)

    def sums_copy(d, back):
        to, source = lax.rem(dp + d, peers), lax.rem(dp + peers - d, peers)
        return pltpu.make_async_remote_copy(
            src_ref=sums.at[1, :, sums_window(to)],
            dst_ref=sums_parts.at[source if back else dp],
            send_sem=sums_send.at[d],
            recv_sem=sums_recv.at[d],
            device_id=(to, core),
            device_id_type=MESH,
        )

    def sums_begin():
        sums_pair.wait_recv()
        sums[1] = sums[0] + sums_got[...]

        def start(d, carry):
            sums_copy(d, False).start()
            return carry

        lax.fori_loop(1, peers, start, 0)
        sums_parts[pl.ds(dp, 1)] = sums[1, :, sums_window(dp)][None]

    def sums_finish():
        def arrived(d, carry):
            sums_copy(d, True).wait_recv()
            return carry

        lax.fori_loop(1, peers, arrived, 0)
        sums_out[...] = jnp.sum(sums_parts[...], axis=0)

    def sums_sent(d, carry):
        sums_copy(d, False).wait_send()
        return carry

    output_copy.wait_send()
    attend_copy.wait_send()
    tokens_stages = [
        reduce_give.at[pl.ds(r * block, block), pl.ds(side * width, width)]
        for side in range(2)
        for r in range(2)
    ]
    run(steps - 1, 15)
    sums_begin()
    run(steps, 8)
    run(steps + 1, 2)
    run(steps, 15)
    run(steps + 1, 4)
    tokens_copy.wait_recv()
    finals += unpick(tokens_own, tokens_got, tokens_out, tokens_stages, 4)
    run(steps + 1, 3)
    sums_finish()
    run(steps + 1, 15)
    for chain in chains:
        chain.drain()
    if not chains:
        for i, (here, there) in enumerate(
            (
                (expand_got, expand_out),
                (reduce_got, reduce_out),
                (late_got.at[:, pl.ds(0, attend_cols)], late_out),
                (late_got.at[:, pl.ds(attend_cols, columns - attend_cols)], output_out),
            )
        ):
            finals.append(pltpu.make_async_copy(here, there, load_sem.at[i]))
            finals[-1].start()
    for copy in finals:
        copy.wait()
    for copy in (layer_copy, tokens_copy, sums_pair):
        copy.wait_send()
    lax.fori_loop(1, peers, sums_sent, 0)


def split_blocks(blocks):
    step = len(blocks) // 4
    return [blocks[i * step : (i + 1) * step] for i in range(4)]


def block_scratch(peers, whole, left, parts, width):
    shapes = [(peers, whole, width)] if whole else []
    shapes.append((peers, 16, width // parts))
    return [pltpu.VMEM(shape, BF) for _ in range(4) for shape in shapes], len(shapes)


def exchange_call(
    kernel, name, collective_id, capacity, width, args, spaces, outs, scratch, after=(), out_spaces=None
):
    peers = lax.axis_size("dp")
    whole, left, parts = block_plan(capacity, width)
    blocks, kinds = block_scratch(peers, whole, left, parts, width)
    return pl.pallas_call(
        functools.partial(kernel, whole),
        out_shape=[jax.ShapeDtypeStruct(*out) for out in outs],
        in_specs=[pl.BlockSpec(memory_space=space) for space in spaces],
        out_specs=[
            pl.BlockSpec(memory_space=space) for space in out_spaces or [pltpu.VMEM] * len(outs)
        ],
        scratch_shapes=[
            *scratch,
            *[pltpu.SemaphoreType.DMA((kinds, peers))] * 4,
            *blocks,
            *after,
        ],
        compiler_params=pltpu.CompilerParams(
            collective_id=collective_id, has_side_effects=True, vmem_limit_bytes=58 * 2**20
        ),
        name=name,
    )(*args)


def slot_layout(peers, capacity, whole, own, own_pad, total):
    left = capacity - whole
    spot = np.arange(total) % own_pad
    side = np.arange(total) // own_pad
    main = spot < peers * whole
    rest = spot - peers * whole
    device = np.where(main, spot // max(whole, 1), rest // left)
    slot = np.where(main, spot % max(whole, 1), whole + rest % left)
    is_slot = spot < peers * capacity
    rows = [
        np.where(is_slot, device, 0),
        np.where(is_slot, slot, 4 * capacity),
        np.where((spot < own) & (side < 2), spot, -1),
        np.minimum(side, 1),
    ]
    return jnp.asarray(np.stack(rows + [np.zeros(total)] * 4), jnp.int32)


def attend(
    row_ids, select, priority, vectors, maps, tokens, cotangent, w_own, wo, we, wr, capacity, own, own_pad, total
):
    peers = lax.axis_size("dp")
    count, width = tokens.shape
    slots = peers * capacity
    cols = w_own.shape[2]
    heads = 2 * cols // HD
    whole = block_plan(capacity, width)[0]
    layout = slot_layout(peers, capacity, whole, own, own_pad, total)
    vmem, hbm = pltpu.VMEM, pl.ANY
    kept = [
        ((slots, width), BF), ((2, slots, 3 * cols), BF), ((heads, slots, slots), BF),
        ((own_pad, width), BF), ((own_pad, width), BF),
    ]
    return exchange_call(
        lambda whole, *refs: attend_kernel(whole, capacity, *refs), "attend", 0, capacity, width,
        (row_ids, select, priority, *vectors, layout, maps, tokens, cotangent, w_own, wo, we, wr),
        (vmem,) * 10 + (hbm,) * 6,
        [
            ((slots, width), BF), ((own_pad, 1), F32), ((8, total), F32), ((total, 8), F32),
            ((8, width), F32), *kept, *[(value.shape, BF) for value in (w_own, wo, we, wr)],
        ],
        [
            *[vmem(*value) for value in kept],
            pltpu.SemaphoreType.DMA((4,)), pltpu.SemaphoreType.DMA((4,)), pltpu.SemaphoreType.DMA((6,)),
            vmem((count, width), BF), vmem((count, width), BF),
            vmem((8, total), jnp.int32), vmem((total, 8), F32), vmem((8, total), F32),
            vmem((2, *w_own.shape), BF),
            vmem((slots, width), BF),
            vmem((8, slots), F32),
            pltpu.SemaphoreType.DMA((4,)),
        ],
        (),
        (vmem,) * 5 + (hbm,) * 9,
    )


def back(small, large, probs, capacity, orders, place_rows):
    gathered, wo, _, x, ct, we, _, wr, _, w, _, proj, _, buffer = large
    slots, width = buffer.shape
    count, hidden = x.shape[0], we.shape[1]
    peers = lax.axis_size("dp")
    vmem, hbm = pltpu.VMEM, pl.ANY
    dma = pltpu.SemaphoreType.DMA
    chunk = 512 if hidden % 512 == 0 else hidden
    steps = hidden // chunk
    rows = width // peers
    after = []
    sizes = (hidden, hidden, 3 * w.shape[2], wo.shape[0])
    if orders is None:
        outs = [((width, size), BF) for size in sizes]
        out_spaces = (hbm,) * 6 + (vmem,)
    else:
        outs = [((rows, size), F32) for size in sizes]
        out_spaces = (vmem,) * 4 + (hbm,) * 2 + (vmem,)
        counts = [peers >> (stage + 1) for stage in range(len(orders[0]))]
        left_cols = -(-sizes[2] // 256) * 128
        for size in [chunk] * (2 * steps) + [sizes[3], left_cols, sizes[2] - left_cols]:
            after += [dma((sum(counts),))] * 2
            after += [vmem((n, rows, size), BF) for n in counts]
    outs += [((-(-place_rows // 16) * 16, width), BF), ((-(-place_rows // 16) * 16, width), BF), ((8, 256), F32)]
    low = vmem((count, width), BF)
    wide = vmem((count, width), F32)
    turned = vmem((width, count), BF)
    column = vmem((count, 1), F32)
    slot_rows = vmem((slots, width), BF)
    gradient = vmem((width, hidden), BF)
    return exchange_call(
        lambda whole, *refs: back_kernel(whole, orders, *refs), "back", 1, capacity, width,
        (*small, *large),
        (vmem,) * len(small) + (hbm,) * len(large),
        outs,
        [
            slot_rows, vmem((2, *wo.shape), BF), low, low, vmem((2, *w.shape), BF),
            vmem(proj.shape, BF), vmem(probs.shape, BF), slot_rows,
            vmem((2, width, chunk), BF), vmem((2, chunk, width), BF),
            vmem((slots, width), F32), column, column, low, turned, turned, wide, wide,
            vmem((count, chunk), F32), vmem((count, chunk), F32),
            vmem((count, chunk), BF), vmem((count, chunk), BF),
            column, slot_rows, slot_rows, vmem(proj.shape, BF), low, low,
            gradient, gradient, gradient, gradient,
            vmem((2, 8, width + 256), F32), vmem((8, width + 256), F32), vmem((peers, 8, 256), F32),
            dma((10,)), dma((2,)), dma((2,)), dma((10,)),
            dma((2 * steps + 5,)), dma((2 * steps + 5,)), dma((peers,)), dma((peers,)),
            pltpu.SemaphoreType.REGULAR,
        ],
        after,
        out_spaces,
    )


def shards(
    tokens,
    row_ids,
    select,
    priority,
    first_gain,
    first_shift,
    router,
    w_attend,
    w_output,
    second_gain,
    second_shift,
    w_expand,
    w_reduce,
    cotangent,
):
    dp_count = lax.axis_size("dp")
    mp_count = lax.axis_size("mp")
    core = lax.axis_index("mp")
    bits = dp_count.bit_length() - 1
    order_a = list(range(bits))
    order_b = [1, 0] + list(range(bits - 1, 1, -1))
    capacity = 5 * ROW_LEN // (8 * dp_count)
    count, width = tokens.shape
    own = count // mp_count
    own_pad = -(-own // 128) * 128
    heads_cols = w_attend.shape[2]
    whole, left, parts = block_plan(capacity, width)
    maps = rest_map(dp_count, left, parts)

    w_attend = w_attend.transpose(1, 0, 2)

    total = max(-(-count // 128) * 128, mp_count * own_pad)
    (gathered, gate, routes, route_cols, vectors, buffer, proj, probs, x, ct,
     w_other, wo_other, we_other, wr_other) = attend(
        row_ids, select, priority, (first_gain, first_shift, router, second_gain, second_shift),
        maps, tokens, cotangent, w_attend, w_output, w_expand, w_reduce, capacity, own, own_pad, total,
    )
    orders = (order_a, order_b) if width // dp_count % 16 == 0 else None
    expand_sum, reduce_sum, attend_sum, output_sum, layer_out, tokens_grad, vectors = back(
        (maps, gate, vectors, routes, route_cols),
        (gathered, w_output, wo_other, x, ct, w_expand, we_other, w_reduce, wr_other, w_attend, w_other,
         proj, probs, buffer),
        probs, capacity, orders, count,
    )
    if orders is None:
        expand_sum = scatter_sum(expand_sum, order_a)
        reduce_sum = scatter_sum(reduce_sum, order_b)
        attend_sum = scatter_sum(attend_sum, order_a)
        output_sum = scatter_sum(output_sum, order_b)
    rows_here = width // dp_count
    vectors = lax.dynamic_slice_in_dim(vectors, lax.axis_index("dp") * rows_here % 128, rows_here, 1)

    return (
        layer_out[:count],
        tokens_grad[:count].astype(F32),
        vectors[0],
        vectors[1],
        vectors[2],
        attend_sum.reshape(-1, 3, heads_cols),
        output_sum.T,
        vectors[3],
        vectors[4],
        expand_sum,
        reduce_sum.T,
    )


def solution(mesh):
    in_specs = (
        P("dp", None),
        P("dp"),
        P("dp"),
        P("dp"),
        P(),
        P(),
        P(),
        P(None, None, "mp"),
        P("mp", None),
        P(),
        P(),
        P(None, "mp"),
        P("mp", None),
        P("dp", None),
    )
    out_specs = (
        P("dp", None),
        P("dp", None),
        P("dp"),
        P("dp"),
        P("dp"),
        P("dp", None, "mp"),
        P("mp", "dp"),
        P("dp"),
        P("dp"),
        P("dp", "mp"),
        P("mp", "dp"),
    )
    return jax.shard_map(shards, mesh=mesh, in_specs=in_specs, out_specs=out_specs, check_vma=False)
```

```python
import functools

import jax
import jax.numpy as jnp
import numpy as np
from jax import lax
from jax.experimental import pallas as pl
from jax.experimental.pallas import tpu as pltpu
from jax.sharding import PartitionSpec as P

HD = 64
ROW_LEN = 577
EPSILON = 1e-06
MASKED_SCORE = -1000000000.0
EMPTY = 1e30
BF = jnp.bfloat16
F32 = jnp.float32
MESH = pl.DeviceIdType.MESH


def mm(a, b, dims):
    return lax.dot_general(a, b, (dims, ((), ())), preferred_element_type=F32)


def norm_stats(value):
    center = value - jnp.mean(value, axis=-1, keepdims=True)
    inv = lax.rsqrt(jnp.mean(center * center, axis=-1, keepdims=True) + EPSILON)
    return center * inv, inv


def norm_pull(e, nhat, inv):
    return (e - jnp.mean(e, axis=-1, keepdims=True) - nhat * jnp.mean(e * nhat, axis=-1, keepdims=True)) * inv


def swap(value):
    return lax.ppermute(value, "mp", [(0, 1), (1, 0)])


def scatter_sum(grad, order):
    count = lax.axis_size("dp")
    me = lax.axis_index("dp")
    bits = count.bit_length() - 1
    width = grad.shape[0] // count
    dims = [2] * bits
    value = grad.reshape(dims + [width, grad.shape[1]])
    out = None
    for step in order:
        axis = bits - 1 - step
        mine = (me >> step) & 1
        give = lax.dynamic_slice_in_dim(value, 1 - mine, 1, axis)
        keep = lax.dynamic_slice_in_dim(value, mine, 1, axis)
        got = lax.ppermute(give, "dp", [(i, i ^ (1 << step)) for i in range(count)])
        out = keep.astype(F32) + got.astype(F32)
        value = out.astype(grad.dtype)
    return out.reshape(width, grad.shape[1])


def block_plan(capacity, width):
    whole = capacity // 16 * 16
    left = capacity - whole
    parts = max(s for s in (1, 2, 3, 6) if left * s <= 16 and width % (128 * s) == 0)
    return whole, left, parts


def rest_map(peers, left, parts):
    at = np.arange(peers * 16)[None, :, None]
    row = np.arange(peers * left)[None, None, :]
    part = np.arange(parts)[:, None, None]
    hit = (at // 16 == row // left) & (at % 16 == part * left + row % left)
    return jnp.asarray(hit.astype(np.float32), BF)


def greet(peers, with_pair=False):
    me, core = lax.axis_index("dp"), lax.axis_index("mp")
    barrier = pltpu.get_barrier_semaphore()

    def hello(d, carry):
        pl.semaphore_signal(
            barrier, inc=1, device_id=(lax.rem(me + d, peers), core), device_id_type=MESH
        )
        return carry

    lax.fori_loop(1, peers, hello, 0)
    if with_pair:
        pl.semaphore_signal(barrier, inc=1, device_id=(me, 1 - core), device_id_type=MESH)
    return lambda: pl.semaphore_wait(barrier, peers if with_pair else peers - 1)


def pack(value, blocks, maps, whole):
    rest = blocks[-1]
    peers, lanes = rest.shape[0], rest.shape[2]
    if whole:
        blocks[0][...] = value[: peers * whole].reshape(peers, whole, value.shape[1])
    tail = value[peers * whole :]
    total = sum(
        mm(maps[i], tail[:, i * lanes : (i + 1) * lanes], ((1,), (0,)))
        for i in range(maps.shape[0])
    )
    rest[...] = total.astype(BF).reshape(peers, 16, lanes)


def unpack(blocks, maps, whole, out):
    rest = blocks[-1]
    peers, lanes = rest.shape[0], rest.shape[2]
    if whole:
        out[: peers * whole, :] = blocks[0][...].reshape(peers * whole, out.shape[1])
    left = rest[...].reshape(peers * 16, lanes)
    for i in range(maps.shape[0]):
        out[peers * whole :, i * lanes : (i + 1) * lanes] = mm(
            maps[i], left, ((0,), (0,))
        ).astype(BF)


def copies(d, pairs, sends, recvs, back=False):
    me, core = lax.axis_index("dp"), lax.axis_index("mp")
    peers = pairs[0][0].shape[0]
    to, source = lax.rem(me + d, peers), lax.rem(me + peers - d, peers)
    return [
        pltpu.make_async_remote_copy(
            src_ref=here.at[to],
            dst_ref=there.at[source if back else me],
            send_sem=sends.at[i, d],
            recv_sem=recvs.at[i, d],
            device_id=(to, core),
            device_id_type=MESH,
        )
        for i, (here, there) in enumerate(pairs)
    ]


def send_all(pairs, sends, recvs):
    me = lax.axis_index("dp")

    def start(d, carry):
        for copy in copies(d, pairs, sends, recvs):
            copy.start()
        return carry

    lax.fori_loop(1, pairs[0][0].shape[0], start, 0)
    for here, there in pairs:
        there[pl.ds(me, 1)] = here[pl.ds(me, 1)]


def wait_all(pairs, sends, recvs):
    def finish(d, carry):
        for copy in copies(d, pairs, sends, recvs, back=True):
            copy.wait_recv()
        return carry

    def drain(d, carry):
        for copy in copies(d, pairs, sends, recvs):
            copy.wait_send()
        return carry

    lax.fori_loop(1, pairs[0][0].shape[0], finish, 0)
    lax.fori_loop(1, pairs[0][0].shape[0], drain, 0)


def lane_masks():
    low = lax.broadcasted_iota(jnp.int32, (1, 128), 1) < HD
    return low, jnp.logical_not(low)


def routing(info, layout, capacity, count, wide_cols, hit_rows, routes, route_cols):
    core = lax.axis_index("mp").astype(F32)
    cores = lax.axis_size("mp")
    total = info.shape[1]
    blocks = total // 128
    row, chosen, priority = (info[i : i + 1, :].astype(F32) for i in range(3))
    device, slot, spot, side = (layout[i : i + 1, :].astype(F32) for i in range(4))
    core_of = core + side * (1.0 - 2.0 * core)
    row_of = device * cores + core_of
    spot_of = jnp.where(spot >= 0.0, core_of * total + spot, -1.0)
    low = row * 2048.0
    key = low + priority
    picked = chosen > 0.5
    hit_rows[...] = jnp.zeros(hit_rows.shape, F32)
    hit_rows[0:1, :] = jnp.where(picked, key, -1.0)
    hit_rows[1:2, :] = jnp.where(picked, row, -1.0)
    wide_cols[...] = hit_rows[...].T

    def fold(hit):
        return jnp.sum(jnp.where(hit, 1.0, 0.0).reshape(16, 8, total), axis=0)

    def count_rows(b, carry):
        at = pl.ds(pl.multiple_of(b * 128, 128), 128)
        keys, rows = wide_cols[at, 0:1], wide_cols[at, 1:2]
        return (
            carry[0] + fold((keys >= low) & (keys < key)),
            carry[1] + fold(rows == row_of),
        )

    zeros = jnp.zeros((8, total), F32)
    ranks, sizes = lax.fori_loop(0, blocks, count_rows, (zeros, zeros))
    rank = jnp.sum(ranks, axis=0, keepdims=True)
    size = jnp.sum(sizes, axis=0, keepdims=True)
    kept = picked & (rank < capacity)
    filled = slot < jnp.minimum(size, float(capacity))
    index = lax.broadcasted_iota(jnp.int32, (1, total), 1).astype(F32)
    rest = (index < count) & jnp.logical_not(kept)
    free = (spot_of >= 0.0) & jnp.logical_not(filled)
    hit_rows[0:1, :] = jnp.where(rest, index, 1e9)
    hit_rows[1:2, :] = jnp.where(free, spot_of, 1e9)
    wide_cols[...] = hit_rows[...].T

    def count_rest(b, carry):
        at = pl.ds(pl.multiple_of(b * 128, 128), 128)
        return (
            carry[0] + fold(wide_cols[at, 0:1] < index),
            carry[1] + fold(wide_cols[at, 1:2] < spot_of),
        )

    before, ahead = lax.fori_loop(0, blocks, count_rest, (zeros, zeros))
    base = float(lax.axis_size("dp") * cores * capacity)
    before = base + jnp.sum(before, axis=0, keepdims=True)
    ahead = base + jnp.sum(ahead, axis=0, keepdims=True)
    routes[...] = jnp.zeros(routes.shape, F32)
    routes[0:1, :] = jnp.where(
        filled, row_of * capacity + slot, jnp.where(spot_of >= 0.0, ahead, -1.0)
    )
    routes[1:2, :] = jnp.where(filled, 1.0, 0.0)
    routes[2:3, :] = jnp.where(kept, row * capacity + rank, jnp.where(rest, before, -2.0))
    route_cols[...] = routes[...].T


def each_rows(body, first, last, carry, **kept):
    for r in range(first, last):
        carry = body(r, carry, **kept)
    return carry


def attend_kernel(
    whole, capacity, row_ids, select, priority, first_gain, first_shift, router_in, second_gain, second_shift,
    layout, maps, tokens_in, cotangent_in, w_own, wo_own, we_own, wr_own,
    gathered, gate, routes, route_cols, vectors, buffer_out, proj_out, probs_out, x_out, ct_out,
    w_out, wo_out, we_out, wr_out,
    buffer, proj, probs, x, ct, swap_send, swap_recv, out_sem, tokens, cotangent, info, wide_cols, hit_rows,
    w_vmem, context, key_mask, w_sem, send_1, recv_1, send_2, recv_2, *blocks,
):
    core = lax.axis_index("mp")
    loads = [
        pltpu.make_async_copy(here, there, w_sem.at[i])
        for i, (here, there) in enumerate(
            (
                (tokens_in, tokens),
                (cotangent_in, cotangent),
                (w_own, w_vmem.at[0]),
            )
        )
    ]
    for load in loads:
        load.start()
    given_1, taken_1, given_2, taken_2 = split_blocks(blocks)
    ready = greet(given_1[-1].shape[0], with_pair=True)
    swaps = [
        pltpu.make_async_remote_copy(
            src_ref=here,
            dst_ref=there,
            send_sem=swap_send.at[i],
            recv_sem=swap_recv.at[i],
            device_id=(lax.axis_index("dp"), 1 - core),
            device_id_type=MESH,
        )
        for i, (here, there) in enumerate(
            ((w_own, w_vmem.at[1]), (wo_own, wo_out), (we_own, we_out), (wr_own, wr_out))
        )
    ]
    leaving = [
        pltpu.make_async_copy(here, there, out_sem.at[i])
        for i, (here, there) in enumerate(
            (
                (x, x_out),
                (ct, ct_out),
                (buffer, buffer_out),
                (proj, proj_out),
                (probs, probs_out),
                (w_vmem.at[1], w_out),
            )
        )
    ]
    count, width = tokens.shape
    slots = buffer.shape[0]
    total_rows = x.shape[0]
    info[...] = jnp.zeros(info.shape, jnp.int32)
    for i, source in enumerate((row_ids, select, priority)):
        info[i : i + 1, :count] = source[...].reshape(1, count)
    vectors[...] = jnp.zeros(vectors.shape, F32)
    for i, source in enumerate((first_gain, first_shift, router_in, second_gain, second_shift)):
        vectors[i : i + 1, :] = source[...].reshape(1, width)
    routing(info, layout, capacity, count, wide_cols, hit_rows, routes, route_cols)
    ready()
    swaps[0].start()
    loads[0].wait()

    def pick(first, last, source, out):
        at = pl.ds(first, last - first)
        hit = (route_cols[at, 0:1] == routes[2:3, :count]).astype(F32).astype(BF)
        out[at, :] = mm(hit, source[...], ((1,), (0,))).astype(BF)

    def norm_rows(r, carry, sent):
        at = pl.ds(pl.multiple_of(r * 32, 32), 32)
        normal, _ = norm_stats(x[at, :].astype(F32))
        normed = (normal * vectors[0:1, :] + vectors[1:2, :]).astype(BF)
        wide = normed.astype(F32)
        gate[at, :] = jax.nn.sigmoid(jnp.sum(wide * vectors[2:3, :], axis=-1, keepdims=True))
        if sent:
            context[at, :] = jnp.where(route_cols[at, 1:2] > 0.5, wide, EMPTY).astype(BF)
        return carry

    kept_rows = -(-slots // 128) * 128
    pick(0, kept_rows, tokens, x)
    each_rows(norm_rows, 0, slots // 32, 0, sent=True)
    pack(context[...], given_1, maps, whole)
    first = list(zip(given_1, taken_1))
    send_all(first, send_1, recv_1)
    for copy in swaps[1:]:
        copy.start()
    pick(kept_rows, total_rows, tokens, x)
    each_rows(norm_rows, slots // 32, total_rows // 32, 0, sent=False)
    loads[1].wait()
    pick(0, kept_rows, cotangent, ct)
    pick(kept_rows, total_rows, cotangent, ct)
    leaving[0].start()
    leaving[1].start()
    swaps[0].wait_recv()
    leaving[5].start()
    wait_all(first, send_1, recv_1)
    unpack(taken_1, maps, whole, buffer)
    lane = (lax.broadcasted_iota(jnp.int32, (8, 128), 1) == 0).astype(F32).astype(BF)
    key_mask[...] = jnp.where(
        mm(lane, buffer[:, :128], ((1,), (1,))) < 0.5 * EMPTY, 1.0, 0.0
    )
    received = buffer[...].astype(F32)
    buffer[...] = jnp.where(received[:, :1] < 0.5 * EMPTY, received, 0.0).astype(BF)
    cols = w_own.shape[2]
    pairs = cols // 128
    masks = lane_masks()
    zero = jnp.zeros((), BF)
    for i in range(2):
        if i == 0:
            loads[2].wait()
        for which in range(3):
            proj[i, :, which * cols : (which + 1) * cols] = mm(
                buffer[...], w_vmem[i, which], ((1,), (0,))
            ).astype(BF)
        canonical = core if i == 0 else 1 - core

        def pair_step(p, carry, i=i, canonical=canonical):
            def part(which):
                return proj[i, :, pl.ds(pl.multiple_of(which * cols + p * 128, 128), 128)]

            q, k, v = part(0), part(1), part(2)
            total = 0.0
            for e, lanes in enumerate(masks):
                scores = mm(q, jnp.where(lanes, k, zero), ((1,), (1,))) * HD ** (-0.5)
                scores = jnp.where(key_mask[:1, :] > 0.5, scores, MASKED_SCORE)
                weights = jnp.exp(scores - jnp.max(scores, axis=-1, keepdims=True))
                low = (weights * (1.0 / jnp.sum(weights, axis=-1, keepdims=True))).astype(BF)
                probs[(i * pairs + p) * 2 + e] = low
                total = total + mm(low, jnp.where(lanes, v, zero), ((1,), (0,)))
            context[:, pl.ds(pl.multiple_of(canonical * cols + p * 128, 128), 128)] = total.astype(BF)
            return carry

        lax.fori_loop(0, pairs, pair_step, 0)
    pack(context[...], given_2, maps, whole)
    second = list(zip(given_2, taken_2))
    send_all(second, send_2, recv_2)
    for copy in leaving[2:5]:
        copy.start()
    wait_all(second, send_2, recv_2)
    unpack(taken_2, maps, whole, gathered)
    for copy in leaving:
        copy.wait()
    for copy in swaps[1:]:
        copy.wait_recv()
    for copy in swaps:
        copy.wait_send()


class Halving:
    def __init__(self, source, bufs, sends, recvs, order, out, window):
        self.source, self.bufs, self.sends, self.recvs = source, bufs, sends, recvs
        self.order, self.out, self.window = order, out, window
        self.stages = len(order)
        self.rows = bufs[0].shape[1]
        self.counts = [buf.shape[0] for buf in bufs]
        self.first = [k for stage, k in halving_plan(self.stages) if stage == 0]

    def bit(self, stage):
        return lax.rem(lax.div(lax.axis_index("dp"), 1 << self.order[stage]), 2)

    def block(self, k, kept):
        index = 0
        for stage in range(self.stages):
            mine = self.bit(stage)
            if stage == 0:
                value = mine if kept else 1 - mine
            else:
                part = lax.rem(lax.div(k, self.counts[stage]), 2)
                value = (1 - mine) * (1 - part) + mine * part
            index = index + value * (1 << self.order[stage])
        return pl.ds(pl.multiple_of(index * self.rows, 16), self.rows)

    def copy(self, stage, k):
        me, core = lax.axis_index("dp"), lax.axis_index("mp")
        to = me + (1 - 2 * self.bit(stage)) * (1 << self.order[stage])
        at = sum(self.counts[:stage]) + k
        src = self.source.at[self.block(k, False), :] if stage == 0 else self.bufs[stage - 1].at[k]
        return pltpu.make_async_remote_copy(
            src_ref=src,
            dst_ref=self.bufs[stage].at[k],
            send_sem=self.sends.at[at],
            recv_sem=self.recvs.at[at],
            device_id=(to, core),
            device_id_type=MESH,
        )

    def begin(self):
        for k in self.first[: self.window]:
            self.copy(0, k).start()

    def step(self, stage, k):
        self.copy(stage, k).wait_recv()
        buf = self.bufs[stage]
        if stage == 0:
            own = self.source[self.block(k, True), :]
        else:
            own = self.bufs[stage - 1][pl.ds(self.counts[stage] + k, 1)][0]
        total = own.astype(F32) + buf[pl.ds(k, 1)][0].astype(F32)
        if stage == self.stages - 1:
            self.out[...] = total
            return
        buf[pl.ds(k, 1)] = total.astype(BF)[None]
        if k < self.counts[stage + 1]:
            self.copy(stage + 1, k).start()
        if stage == 0:
            ahead = self.first.index(k) + self.window
            if ahead < len(self.first):
                self.copy(0, self.first[ahead]).start()

    def drain(self):
        for stage, count in enumerate(self.counts):

            def finish(k, carry, stage=stage):
                self.copy(stage, k).wait_send()
                return carry

            lax.fori_loop(0, count, finish, 0)


def halving_plan(stages):
    counts = [1 << (stages - 1 - stage) for stage in range(stages)]
    times = {}
    for stage, count in enumerate(counts):
        for k in range(count):
            if stage == 0:
                bits = [(k >> i) & 1 for i in range(stages - 1)]
                times[stage, k] = 1 + sum(bit << (stages - 2 - i) for i, bit in enumerate(bits))
            else:
                times[stage, k] = 1.6 + max(times[stage - 1, k], times[stage - 1, count + k])
    return sorted(times, key=lambda key: (times[key], key))


def advance(chains, steps):
    for stage, k in steps:
        for chain in chains:
            chain.step(stage, k)


def half_erfc(value, bell):
    t = 1.0 / (1.0 + (0.3275911 * 0.5**0.5) * jnp.abs(value))
    poly = 1.061405429 * t - 1.453152027
    poly = poly * t + 1.421413741
    poly = poly * t - 0.284496736
    poly = poly * t + 0.254829592
    return 0.5 * poly * t * bell


def row_sums(value):
    return jnp.sum(value.reshape(value.shape[0] // 8, 8, value.shape[1]), axis=0)


def back_kernel(
    whole, orders, maps, gate, vectors, routes, route_cols,
    gathered_in, wo_own, wo_other, x_in, ct_in, we_own, we_other, wr_own, wr_other,
    w_own, w_other, proj_in, probs_in, buffer_in,
    expand_out, reduce_out, late_out, output_out, layer_out, tokens_out, sums_out,
    gathered, wo, x, ct, w_vmem, proj, probs, buffer,
    we, wr, attended, mean, inv, hidden, hidden_t, ct_t, mlp, mixed_grad, pre, act_grad, act, pre_grad,
    logit_grad, attended_grad, upstream, proj_grad, layer_own, tokens_got,
    expand_give, reduce_give, expand_got, reduce_got, sums, sums_got, sums_parts,
    load_sem, we_sem, wr_sem, out_sem, pair_send, pair_recv, sums_send, sums_recv, free_sem,
    send_1, recv_1, send_2, recv_2, *rest,
):
    dp, core = lax.axis_index("dp"), lax.axis_index("mp")
    peers = lax.axis_size("dp")
    width, columns = expand_give.shape
    slots = buffer.shape[0]
    count = x.shape[0]
    chunk = pre.shape[1]
    steps = columns // chunk
    cols = w_own.shape[2]
    pairs = cols // 128
    attend_cols = 3 * cols
    left_cols = -(-attend_cols // 256) * 128
    halves = ((0, left_cols), (left_cols, attend_cols - left_cols))
    step_rows = 32
    kept_steps, all_steps = slots // step_rows, count // step_rows
    ready = greet(peers, with_pair=True)
    gain, shift, router, gain_2, shift_2 = (vectors.at[pl.ds(i, 1), :] for i in range(5))

    def chunk_loads(n):
        j, slot = n // 2, n % 2
        here_e, here_r = (we_other, wr_other) if n % 2 == 0 else (we_own, wr_own)
        part = pl.ds(j * chunk, chunk)
        return (
            pltpu.make_async_copy(here_e.at[:, part], we.at[slot], we_sem.at[slot]),
            pltpu.make_async_copy(here_r.at[part, :], wr.at[slot], wr_sem.at[slot]),
        )

    local = [
        (gathered_in, gathered),
        (wo_own, wo.at[0]),
        (wo_other, wo.at[1]),
        (x_in, x),
        (ct_in, ct),
        (proj_in, proj),
        (probs_in, probs),
        (w_own, w_vmem.at[0]),
        (w_other, w_vmem.at[1]),
        (buffer_in, buffer),
    ]
    loads = [
        pltpu.make_async_copy(here, there, load_sem.at[i]) for i, (here, there) in enumerate(local)
    ]
    for load in (*loads[:5], *chunk_loads(0), *loads[5:]):
        load.start()

    kinds = 2 if whole else 1
    given_1, taken_1, given_2, taken_2 = split_blocks(rest[: 4 * kinds])
    rest = rest[4 * kinds :]
    late_give, late_got = reduce_give, expand_give
    chains = []
    plan = []
    if orders is not None:
        stages = len(orders[0])
        plan = halving_plan(stages)
        parts_of = []
        for j in range(steps):
            part = pl.ds(j * chunk, chunk)
            parts_of.append((expand_got.at[:, part], expand_out.at[:, part], orders[0], 4))
            parts_of.append((reduce_got.at[:, part], reduce_out.at[:, part], orders[1], 4))
        groups = [[2 * j, 2 * j + 1] for j in range(steps)] + [[2 * steps], [2 * steps + 1, 2 * steps + 2]]
        output_part = pl.ds(attend_cols, columns - attend_cols)
        parts_of.append((late_got.at[:, output_part], output_out, orders[0], 8))
        for j, (first_col, size) in enumerate(halves):
            part = pl.ds(first_col, size)
            parts_of.append((late_got.at[:, part], late_out.at[:, part], orders[j], 4))
        for i, (source, out, order, window) in enumerate(parts_of):
            mine = rest[i * (stages + 2) : (i + 1) * (stages + 2)]
            chains.append(Halving(source, mine[2:], mine[0], mine[1], order, out, window))
    done = [0] * (steps + 2)

    def run(group, number):
        if chains:
            advance([chains[i] for i in groups[group]], plan[done[group] : done[group] + number])
            done[group] += number

    def begin(group):
        if chains:
            for i in groups[group]:
                chains[i].begin()

    def pair_copy(at, give, got):
        return pltpu.make_async_remote_copy(
            src_ref=give,
            dst_ref=got,
            send_sem=pair_send.at[at],
            recv_sem=pair_recv.at[at],
            device_id=(dp, 1 - core),
            device_id_type=MESH,
        )

    def weight_copy(i, j):
        give, got = ((expand_give, expand_got), (reduce_give, reduce_got))[i]
        part = pl.ds(j * chunk, chunk)
        return pair_copy(i * steps + j, give.at[:, part], got.at[:, part])

    own_cols = pl.ds(pl.multiple_of(core * cols, 128), cols)
    other_cols = pl.ds(pl.multiple_of((1 - core) * cols, 128), cols)
    for load in loads[:3]:
        load.wait()
    attended[...] = mm(gathered[:, own_cols], wo[0], ((1,), (0,))) + mm(
        gathered[:, other_cols], wo[1], ((1,), (0,))
    )
    for load in loads[3:5]:
        load.wait()

    def rows_of(r):
        return pl.ds(pl.multiple_of(r * step_rows, step_rows), step_rows)

    def mixed_rows(rows, kept):
        value = x[rows, :].astype(F32)
        return value + gate[rows, :] * attended[rows, :] if kept else value

    def norm_rows(r, carry, kept):
        rows = rows_of(r)
        if kept:
            attended[rows, :] = jnp.where(route_cols[rows, 1:2] > 0.5, attended[rows, :], 0.0)
        value = mixed_rows(rows, kept)
        middle = jnp.mean(value, axis=-1, keepdims=True)
        center = value - middle
        scale = lax.rsqrt(jnp.mean(center * center, axis=-1, keepdims=True) + EPSILON)
        mean[rows, :] = middle
        inv[rows, :] = scale
        hidden[rows, :] = (center * scale * gain_2[...] + shift_2[...]).astype(BF)
        mlp[rows, :] = jnp.zeros((step_rows, width), F32)
        mixed_grad[rows, :] = jnp.zeros((step_rows, width), F32)
        return carry

    each_rows(norm_rows, 0, kept_steps, 0, kept=True)
    each_rows(norm_rows, kept_steps, all_steps, 0, kept=False)
    hidden_t[...] = hidden[...].T
    ct_t[...] = ct[...].T

    def gelu_rows(r, carry):
        rows = pl.ds(pl.multiple_of(r * 16, 16), 16)
        value = pre[rows, :]
        bell = jnp.exp(-0.5 * value * value)
        tail = half_erfc(value, bell)
        phi = jnp.where(value < 0.0, tail, 1.0 - tail)
        act[rows, :] = (value * phi).astype(BF)
        slope = phi + value * bell * 0.3989422804014327
        pre_grad[rows, :] = (act_grad[rows, :] * slope).astype(BF)
        return carry

    for n in range(2 * steps):
        j, slot, is_own = n // 2, n % 2, n % 2 == 1
        part = pl.ds(j * chunk, chunk)
        for load in chunk_loads(n):
            load.wait()
        if n + 1 < 2 * steps:
            for load in chunk_loads(n + 1):
                load.start()

        def point(n=n, j=j, is_own=is_own):
            for group in range(j):
                run(group, 1)

        pre[...] = mm(hidden[...], we[slot], ((1,), (0,)))
        act_grad[...] = mm(ct[...], wr[slot], ((1,), (1,)))
        lax.fori_loop(0, count // 16, gelu_rows, 0, unroll=2)
        point()
        mlp[...] += mm(act[...], wr[slot], ((1,), (0,)))
        mixed_grad[...] += mm(pre_grad[...], we[slot], ((1,), (1,)))
        point()
        for i, (left, right, give, got) in enumerate(
            (
                (hidden_t, pre_grad, expand_give, expand_got),
                (ct_t, act, reduce_give, reduce_got),
            )
        ):
            value = mm(left[...], right[...], ((1,), (0,)))
            if is_own:
                weight_copy(i, j).wait_recv()
                got[:, part] = (value + got[:, part].astype(F32)).astype(BF)
            else:
                give[:, part] = value.astype(BF)
                if n == 0 and i == 0:
                    ready()
                weight_copy(i, j).start()
        point()
        if is_own and j < steps - 1:
            begin(j)

    def back_rows(r, carry, kept):
        rows = rows_of(r)
        mixed = mixed_rows(rows, kept)
        layer_own[rows, :] = (mixed + mlp[rows, :]).astype(BF)
        grad = mixed_grad[rows, :]
        scale = inv[rows, :]
        normal = (mixed - mean[rows, :]) * scale
        total = ct[rows, :].astype(F32) + norm_pull(grad * gain_2[...], normal, scale)
        mixed_grad[rows, :] = total
        if kept:
            open_by = gate[rows, :]
            attended_grad[rows, :] = jnp.where(route_cols[rows, 1:2] > 0.5, open_by * total, 0.0).astype(BF)
            logit_grad[rows, :] = (
                jnp.sum(total * attended[rows, :], axis=-1, keepdims=True) * open_by * (1.0 - open_by)
            )
        else:
            logit_grad[rows, :] = jnp.zeros((step_rows, 1), F32)
        return (carry[0] + row_sums(grad * normal), carry[1] + row_sums(grad))

    zeros = jnp.zeros((8, width), F32)
    carry = each_rows(back_rows, 0, kept_steps, (zeros, zeros), kept=True)
    for group in range(steps - 1):
        run(group, 2)
    for at, w in ((own_cols, wo[0]), (other_cols, wo[1])):
        upstream[:, at] = mm(attended_grad[...], w, ((1,), (1,))).astype(BF)
    pack(upstream[...], given_1, maps, whole)
    first = list(zip(given_1, taken_1))
    send_all(first, send_1, recv_1)
    begin(steps - 1)
    carry = each_rows(back_rows, kept_steps, all_steps, carry, kept=False)
    sums[...] = jnp.zeros(sums.shape, F32)
    for i in range(2):
        sums[0, 3 + i : 4 + i, :width] = jnp.sum(carry[i], axis=0, keepdims=True)

    block = count // 2
    finals = []

    def unpick(own, other, out, stages, first_sem):
        sent = []
        for r in range(-(-out.shape[0] // block)):
            stage = stages[r % len(stages)]
            size = min(block, out.shape[0] - r * block)
            rows = pl.ds(r * block, size)
            hit = (route_cols[rows, 2:3] == routes[0:1, :]).astype(F32).astype(BF)
            value = mm(hit[:, :count], own[...], ((1,), (0,))) + mm(
                hit[:, count : 2 * count], other[...], ((1,), (0,))
            )
            if r >= len(stages):
                sent[r - len(stages)].wait()
            stage[pl.ds(0, size), :] = value.astype(out.dtype)
            copy = pltpu.make_async_copy(
                stage.at[pl.ds(0, size), :], out.at[rows, :], out_sem.at[first_sem + r]
            )
            copy.start()
            sent.append(copy)
        return sent[-len(stages) :]

    for i in range(2):
        for j in range(steps):
            weight_copy(i, j).wait_send()
    pl.semaphore_signal(free_sem, inc=1, device_id=(dp, 1 - core), device_id_type=MESH)
    late_give[:, attend_cols:] = mm(
        attended_grad[...], gathered[:, other_cols], ((0,), (0,))
    ).astype(BF)
    output_own = mm(attended_grad[...], gathered[:, own_cols], ((0,), (0,)))
    pl.semaphore_wait(free_sem, 1)
    layer_copy = pair_copy(2 * steps + 3, layer_own, ct)
    layer_copy.start()
    output_copy, attend_copy = (
        pair_copy(2 * steps + i, late_give.at[:, part], late_got.at[:, part])
        for i, part in enumerate(
            (pl.ds(attend_cols, columns - attend_cols), pl.ds(0, attend_cols))
        )
    )
    output_copy.start()
    output_copy.wait_recv()
    late_got[:, attend_cols:] = (output_own + late_got[:, attend_cols:].astype(F32)).astype(BF)
    begin(steps)
    for group in range(steps - 2):
        run(group, 15)
    run(steps - 2, 2)
    layer_copy.wait_recv()
    hidden_blocks = [hidden.at[pl.ds(r * block, block), :] for r in range(2)]
    layer_finals = unpick(layer_own, ct, layer_out, hidden_blocks, 0)
    run(steps - 2, 1)

    wait_all(first, send_1, recv_1)
    unpack(taken_1, maps, whole, upstream)
    for load in loads[5:]:
        load.wait()
    masks = lane_masks()
    zero = jnp.zeros((), BF)
    def attend_at(which):
        return pl.ds(pl.multiple_of(which * cols, 128), cols)

    def late_other(which, carry):
        value = mm(buffer[...], proj_grad[1, :, attend_at(which)], ((0,), (0,)))
        late_give[:, attend_at(which)] = value.astype(BF)
        return carry

    def late_own(which, carry):
        value = mm(buffer[...], proj_grad[0, :, attend_at(which)], ((0,), (0,)))
        got = late_got[:, attend_at(which)].astype(F32)
        late_got[:, attend_at(which)] = (value + got).astype(BF)
        return carry

    for i in (1, 0):
        canonical = core if i == 0 else 1 - core

        def pair_step(p, carry, i=i, canonical=canonical):
            def place_of(which):
                return pl.ds(pl.multiple_of(which * cols + p * 128, 128), 128)

            q, k, v = (proj[i, :, place_of(which)] for which in range(3))
            up = upstream[:, place_of(canonical)]
            q_grad = k_grad = v_grad = 0.0
            for e, lanes in enumerate(masks):
                low = probs[(i * pairs + p) * 2 + e]
                wide = low.astype(F32)
                probs_grad = mm(up, jnp.where(lanes, v, zero), ((1,), (1,)))
                delta = jnp.sum(wide * probs_grad, axis=-1, keepdims=True)
                scores_grad = (wide * (probs_grad - delta)).astype(BF)
                v_grad = v_grad + mm(low, jnp.where(lanes, up, zero), ((0,), (0,)))
                q_grad = q_grad + mm(scores_grad, jnp.where(lanes, k, zero), ((1,), (0,)))
                k_grad = k_grad + mm(scores_grad, jnp.where(lanes, q, zero), ((0,), (0,)))
            proj_grad[i, :, place_of(0)] = (q_grad * HD ** (-0.5)).astype(BF)
            proj_grad[i, :, place_of(1)] = (k_grad * HD ** (-0.5)).astype(BF)
            proj_grad[i, :, place_of(2)] = v_grad.astype(BF)
            return carry

        lax.fori_loop(0, pairs, pair_step, 0)
        if i == 1:
            lax.fori_loop(0, 3, late_other, 0)
            attend_copy.start()
        run(steps - 2, 2)
        run(steps - 1, 3)
    attend_copy.wait_recv()
    lax.fori_loop(0, 3, late_own, 0)
    begin(steps + 1)
    upstream[...] = sum(
        mm(proj_grad[i, :, which * cols : (which + 1) * cols], w_vmem[i, which], ((1,), (1,)))
        for i in range(2)
        for which in range(3)
    ).astype(BF)
    pack(upstream[...], given_2, maps, whole)
    second = list(zip(given_2, taken_2))
    send_all(second, send_2, recv_2)

    run(steps - 2, 15)
    run(steps - 1, 4)
    run(steps, 4)

    wait_all(second, send_2, recv_2)
    unpack(taken_2, maps, whole, upstream)
    tokens_own = hidden
    for copy in layer_finals:
        copy.wait()

    def first_rows(r, carry, kept):
        rows = rows_of(r)
        normal, scale = norm_stats(x[rows, :].astype(F32))
        normed = (normal * gain[...] + shift[...]).astype(BF).astype(F32)
        logit = logit_grad[rows, :]
        grad = logit * router[...]
        if kept:
            grad = grad + jnp.where(route_cols[rows, 1:2] > 0.5, upstream[rows, :].astype(F32), 0.0)
        total = mixed_grad[rows, :] + norm_pull(grad * gain[...], normal, scale)
        tokens_own[rows, :] = total.astype(BF)
        return (
            carry[0] + row_sums(grad * normal),
            carry[1] + row_sums(grad),
            carry[2] + row_sums(logit * normed),
        )

    carry = (zeros, zeros, zeros)
    carry = each_rows(first_rows, 0, kept_steps, carry, kept=True)
    carry = each_rows(first_rows, kept_steps, all_steps, carry, kept=False)
    tokens_copy = pair_copy(2 * steps + 2, tokens_own, tokens_got)
    tokens_copy.start()
    for i in range(3):
        sums[0, i : i + 1, :width] = jnp.sum(carry[i], axis=0, keepdims=True)

    sums_pair = pair_copy(2 * steps + 4, sums.at[0], sums_got)
    sums_pair.start()

    def sums_window(device):
        return pl.ds(pl.multiple_of(device * (width // peers) // 128 * 128, 128), 256)

    def sums_copy(d, back):
        to, source = lax.rem(dp + d, peers), lax.rem(dp + peers - d, peers)
        return pltpu.make_async_remote_copy(
            src_ref=sums.at[1, :, sums_window(to)],
            dst_ref=sums_parts.at[source if back else dp],
            send_sem=sums_send.at[d],
            recv_sem=sums_recv.at[d],
            device_id=(to, core),
            device_id_type=MESH,
        )

    def sums_begin():
        sums_pair.wait_recv()
        sums[1] = sums[0] + sums_got[...]

        def start(d, carry):
            sums_copy(d, False).start()
            return carry

        lax.fori_loop(1, peers, start, 0)
        sums_parts[pl.ds(dp, 1)] = sums[1, :, sums_window(dp)][None]

    def sums_finish():
        def arrived(d, carry):
            sums_copy(d, True).wait_recv()
            return carry

        lax.fori_loop(1, peers, arrived, 0)
        sums_out[...] = jnp.sum(sums_parts[...], axis=0)

    def sums_sent(d, carry):
        sums_copy(d, False).wait_send()
        return carry

    output_copy.wait_send()
    attend_copy.wait_send()
    tokens_stages = [
        reduce_give.at[pl.ds(r * block, block), pl.ds(side * width, width)]
        for side in range(2)
        for r in range(2)
    ]
    run(steps - 1, 15)
    sums_begin()
    run(steps, 8)
    run(steps + 1, 2)
    run(steps, 15)
    run(steps + 1, 4)
    tokens_copy.wait_recv()
    finals += unpick(tokens_own, tokens_got, tokens_out, tokens_stages, 4)
    run(steps + 1, 3)
    sums_finish()
    run(steps + 1, 15)
    for chain in chains:
        chain.drain()
    if not chains:
        for i, (here, there) in enumerate(
            (
                (expand_got, expand_out),
                (reduce_got, reduce_out),
                (late_got.at[:, pl.ds(0, attend_cols)], late_out),
                (late_got.at[:, pl.ds(attend_cols, columns - attend_cols)], output_out),
            )
        ):
            finals.append(pltpu.make_async_copy(here, there, load_sem.at[i]))
            finals[-1].start()
    for copy in finals:
        copy.wait()
    for copy in (layer_copy, tokens_copy, sums_pair):
        copy.wait_send()
    lax.fori_loop(1, peers, sums_sent, 0)


def split_blocks(blocks):
    step = len(blocks) // 4
    return [blocks[i * step : (i + 1) * step] for i in range(4)]


def block_scratch(peers, whole, left, parts, width):
    shapes = [(peers, whole, width)] if whole else []
    shapes.append((peers, 16, width // parts))
    return [pltpu.VMEM(shape, BF) for _ in range(4) for shape in shapes], len(shapes)


def exchange_call(
    kernel, name, collective_id, capacity, width, args, spaces, outs, scratch, after=(), out_spaces=None
):
    peers = lax.axis_size("dp")
    whole, left, parts = block_plan(capacity, width)
    blocks, kinds = block_scratch(peers, whole, left, parts, width)
    return pl.pallas_call(
        functools.partial(kernel, whole),
        out_shape=[jax.ShapeDtypeStruct(*out) for out in outs],
        in_specs=[pl.BlockSpec(memory_space=space) for space in spaces],
        out_specs=[
            pl.BlockSpec(memory_space=space) for space in out_spaces or [pltpu.VMEM] * len(outs)
        ],
        scratch_shapes=[
            *scratch,
            *[pltpu.SemaphoreType.DMA((kinds, peers))] * 4,
            *blocks,
            *after,
        ],
        compiler_params=pltpu.CompilerParams(
            collective_id=collective_id, has_side_effects=True, vmem_limit_bytes=58 * 2**20
        ),
        name=name,
    )(*args)


def slot_layout(peers, capacity, whole, own, own_pad, total):
    left = capacity - whole
    spot = np.arange(total) % own_pad
    side = np.arange(total) // own_pad
    main = spot < peers * whole
    rest = spot - peers * whole
    device = np.where(main, spot // max(whole, 1), rest // left)
    slot = np.where(main, spot % max(whole, 1), whole + rest % left)
    is_slot = spot < peers * capacity
    rows = [
        np.where(is_slot, device, 0),
        np.where(is_slot, slot, 4 * capacity),
        np.where((spot < own) & (side < 2), spot, -1),
        np.minimum(side, 1),
    ]
    return jnp.asarray(np.stack(rows + [np.zeros(total)] * 4), jnp.int32)


def attend(
    row_ids, select, priority, vectors, maps, tokens, cotangent, w_own, wo, we, wr, capacity, own, own_pad, total
):
    peers = lax.axis_size("dp")
    count, width = tokens.shape
    slots = peers * capacity
    cols = w_own.shape[2]
    heads = 2 * cols // HD
    whole = block_plan(capacity, width)[0]
    layout = slot_layout(peers, capacity, whole, own, own_pad, total)
    vmem, hbm = pltpu.VMEM, pl.ANY
    kept = [
        ((slots, width), BF), ((2, slots, 3 * cols), BF), ((heads, slots, slots), BF),
        ((own_pad, width), BF), ((own_pad, width), BF),
    ]
    return exchange_call(
        lambda whole, *refs: attend_kernel(whole, capacity, *refs), "attend", 0, capacity, width,
        (row_ids, select, priority, *vectors, layout, maps, tokens, cotangent, w_own, wo, we, wr),
        (vmem,) * 10 + (hbm,) * 6,
        [
            ((slots, width), BF), ((own_pad, 1), F32), ((8, total), F32), ((total, 8), F32),
            ((8, width), F32), *kept, *[(value.shape, BF) for value in (w_own, wo, we, wr)],
        ],
        [
            *[vmem(*value) for value in kept],
            pltpu.SemaphoreType.DMA((4,)), pltpu.SemaphoreType.DMA((4,)), pltpu.SemaphoreType.DMA((6,)),
            vmem((count, width), BF), vmem((count, width), BF),
            vmem((8, total), jnp.int32), vmem((total, 8), F32), vmem((8, total), F32),
            vmem((2, *w_own.shape), BF),
            vmem((slots, width), BF),
            vmem((8, slots), F32),
            pltpu.SemaphoreType.DMA((4,)),
        ],
        (),
        (vmem,) * 5 + (hbm,) * 9,
    )


def back(small, large, probs, capacity, orders, place_rows):
    gathered, wo, _, x, ct, we, _, wr, _, w, _, proj, _, buffer = large
    slots, width = buffer.shape
    count, hidden = x.shape[0], we.shape[1]
    peers = lax.axis_size("dp")
    vmem, hbm = pltpu.VMEM, pl.ANY
    dma = pltpu.SemaphoreType.DMA
    chunk = 512 if hidden % 512 == 0 else hidden
    steps = hidden // chunk
    rows = width // peers
    after = []
    sizes = (hidden, hidden, 3 * w.shape[2], wo.shape[0])
    if orders is None:
        outs = [((width, size), BF) for size in sizes]
        out_spaces = (hbm,) * 6 + (vmem,)
    else:
        outs = [((rows, size), F32) for size in sizes]
        out_spaces = (vmem,) * 4 + (hbm,) * 2 + (vmem,)
        counts = [peers >> (stage + 1) for stage in range(len(orders[0]))]
        left_cols = -(-sizes[2] // 256) * 128
        for size in [chunk] * (2 * steps) + [sizes[3], left_cols, sizes[2] - left_cols]:
            after += [dma((sum(counts),))] * 2
            after += [vmem((n, rows, size), BF) for n in counts]
    outs += [((-(-place_rows // 16) * 16, width), BF), ((-(-place_rows // 16) * 16, width), BF), ((8, 256), F32)]
    low = vmem((count, width), BF)
    wide = vmem((count, width), F32)
    turned = vmem((width, count), BF)
    column = vmem((count, 1), F32)
    slot_rows = vmem((slots, width), BF)
    gradient = vmem((width, hidden), BF)
    return exchange_call(
        lambda whole, *refs: back_kernel(whole, orders, *refs), "back", 1, capacity, width,
        (*small, *large),
        (vmem,) * len(small) + (hbm,) * len(large),
        outs,
        [
            slot_rows, vmem((2, *wo.shape), BF), low, low, vmem((2, *w.shape), BF),
            vmem(proj.shape, BF), vmem(probs.shape, BF), slot_rows,
            vmem((2, width, chunk), BF), vmem((2, chunk, width), BF),
            vmem((slots, width), F32), column, column, low, turned, turned, wide, wide,
            vmem((count, chunk), F32), vmem((count, chunk), F32),
            vmem((count, chunk), BF), vmem((count, chunk), BF),
            column, slot_rows, slot_rows, vmem(proj.shape, BF), low, low,
            gradient, gradient, gradient, gradient,
            vmem((2, 8, width + 256), F32), vmem((8, width + 256), F32), vmem((peers, 8, 256), F32),
            dma((10,)), dma((2,)), dma((2,)), dma((10,)),
            dma((2 * steps + 5,)), dma((2 * steps + 5,)), dma((peers,)), dma((peers,)),
            pltpu.SemaphoreType.REGULAR,
        ],
        after,
        out_spaces,
    )


def shards(
    tokens,
    row_ids,
    select,
    priority,
    first_gain,
    first_shift,
    router,
    w_attend,
    w_output,
    second_gain,
    second_shift,
    w_expand,
    w_reduce,
    cotangent,
):
    dp_count = lax.axis_size("dp")
    mp_count = lax.axis_size("mp")
    core = lax.axis_index("mp")
    bits = dp_count.bit_length() - 1
    order_a = list(range(bits))
    order_b = [1, 0] + list(range(bits - 1, 1, -1))
    capacity = 5 * ROW_LEN // (8 * dp_count)
    count, width = tokens.shape
    own = count // mp_count
    own_pad = -(-own // 128) * 128
    heads_cols = w_attend.shape[2]
    whole, left, parts = block_plan(capacity, width)
    maps = rest_map(dp_count, left, parts)

    w_attend = w_attend.transpose(1, 0, 2)

    total = max(-(-count // 128) * 128, mp_count * own_pad)
    (gathered, gate, routes, route_cols, vectors, buffer, proj, probs, x, ct,
     w_other, wo_other, we_other, wr_other) = attend(
        row_ids, select, priority, (first_gain, first_shift, router, second_gain, second_shift),
        maps, tokens, cotangent, w_attend, w_output, w_expand, w_reduce, capacity, own, own_pad, total,
    )
    orders = (order_a, order_b) if width // dp_count % 16 == 0 else None
    expand_sum, reduce_sum, attend_sum, output_sum, layer_out, tokens_grad, vectors = back(
        (maps, gate, vectors, routes, route_cols),
        (gathered, w_output, wo_other, x, ct, w_expand, we_other, w_reduce, wr_other, w_attend, w_other,
         proj, probs, buffer),
        probs, capacity, orders, count,
    )
    if orders is None:
        expand_sum = scatter_sum(expand_sum, order_a)
        reduce_sum = scatter_sum(reduce_sum, order_b)
        attend_sum = scatter_sum(attend_sum, order_a)
        output_sum = scatter_sum(output_sum, order_b)
    rows_here = width // dp_count
    vectors = lax.dynamic_slice_in_dim(vectors, lax.axis_index("dp") * rows_here % 128, rows_here, 1)

    return (
        layer_out[:count],
        tokens_grad[:count].astype(F32),
        vectors[0],
        vectors[1],
        vectors[2],
        attend_sum.reshape(-1, 3, heads_cols),
        output_sum.T,
        vectors[3],
        vectors[4],
        expand_sum,
        reduce_sum.T,
    )


def solution(mesh):
    in_specs = (
        P("dp", None),
        P("dp"),
        P("dp"),
        P("dp"),
        P(),
        P(),
        P(),
        P(None, None, "mp"),
        P("mp", None),
        P(),
        P(),
        P(None, "mp"),
        P("mp", None),
        P("dp", None),
    )
    out_specs = (
        P("dp", None),
        P("dp", None),
        P("dp"),
        P("dp"),
        P("dp"),
        P("dp", None, "mp"),
        P("mp", "dp"),
        P("dp"),
        P("dp"),
        P("dp", "mp"),
        P("mp", "dp"),
    )
    return jax.shard_map(shards, mesh=mesh, in_specs=in_specs, out_specs=out_specs, check_vma=False)
```
